256 devices in a mesh: load: 8 (over x, y_lo), gz: 32 (over z, y_hi, core).
Axes of the slice: x: 4, y: 4 (y_hi: 2, y_lo: 2; y = y_hi * 2 + y_lo), z: 8, core: 2. Of those that a mesh axis runs over, the one named last changes fastest.
Arguments:
- density: float32 [64, 64, 128], P('gz', 'load'), may hold values from 0.1 to 1
- labels: int32 [64, 64, 128], P('gz'), may hold values from 0 to 11
- forces: float32 [16, 3, 64, 64, 128], P('load', None, 'gz'), may hold values from -6 to 6
- case_weights: int32 [16], replicated, may hold values from 1 to 4
Outputs:
- new_density: float32 [64, 64, 128], P('gz', 'load')
- displacement: float32 [16, 3, 64, 64, 128], P('load', None, 'gz')
The draws below stay inside these ranges and needn't reach their ends.
All inputs are finite; a program needn't handle non-finite values.
Results may differ from the reference program's by a relative error of at most 0.00016.
Values sent between devices are 32-bit elements; how exact they have to be, the bound alone decides.
A program may use at most 64 MiB of HBM per device.

```python
import jax
import jax.numpy as jnp
import numpy as np
from jax import lax

NX = 128
SWEEPS = 3
NY = 64
NZ = 64
LOADS = 16


def touch_ends(drawn, stream_key, smallest, high):
    shape = drawn.shape
    place = [jax.random.randint(jax.random.fold_in(stream_key, axis), (), 0, shape[axis]) for axis in range(len(shape))]
    drawn = drawn.at[tuple(place)].set(smallest)
    longest = shape.index(max(shape))
    place[longest] = (place[longest] + 1) % shape[longest]
    return drawn.at[tuple(place)].set(high)


def block_scale(rng, extent, cuts, low, largest):
    gain = 1.0
    for position, shards_of in cuts:
        steps = jax.random.uniform(jax.random.fold_in(jax.random.fold_in(rng, 6), position), (shards_of,), jnp.float32, low / len(cuts), largest / len(cuts))
        gain = gain * jnp.repeat(jnp.exp(steps), extent[position] // shards_of).reshape((-1,) + (1,) * (len(extent) - 1 - position))
    return gain


def normal_values(key, dims, scale, reach, cuts=(), kind=jnp.bfloat16):
    values = jax.random.normal(key, dims, jnp.float32) * scale
    if len(cuts) > 0:
        values = block_scale(key, dims, cuts, -0.22, 0.18) * values
    return jnp.clip(values, min=-reach, max=reach).astype(kind)


def setup_inputs(seed: int = 0) -> dict:
    seeds = jax.random.split(jax.random.key(seed), 5)
    return {
        "density": jnp.clip(0.1 + 0.9 * jax.random.uniform(seeds[0], (NZ, NY, NX), jnp.float32) ** block_scale(seeds[0], (NZ, NY, NX), ((0, 32), (1, 8)), -0.2, 0.2), 0.1, 1.0),
        "labels": touch_ends(jax.random.randint(seeds[1], (NZ, NY, NX), 0, 12), jax.random.fold_in(seeds[1], 1), 0, 11).astype(jnp.int32),
        "forces": normal_values(seeds[2], (LOADS, 3, NZ, NY, NX), 1.0, 6.0, ((0, 8), (2, 32)), jnp.float32),
        "case_weights": touch_ends(jax.random.randint(seeds[3], (LOADS,), 1, 5), jax.random.fold_in(seeds[3], 1), 1, 4).astype(jnp.int32),
    }


EMIN = 0.001
LOWER_EIG = 0.1
UPPER_EIG = 2.5
MOVE_LIMIT = 0.2
FLOOR_DENSITY = 0.001
CORNER_OFFSETS = [(corner // 4, corner // 2 % 2, corner % 2) for corner in range(8)]

def element_matrix():
    poisson = 0.3
    lame_first = poisson / ((1 + poisson) * (1 - 2 * poisson))
    shear_modulus = 1.0 / (2 * (1 + poisson))
    elastic = np.zeros((6, 6))
    elastic[:3, :3] = lame_first
    for which in range(3):
        elastic[which, which] += 2 * shear_modulus
        elastic[which + 3, which + 3] = shear_modulus
    points = [0.5 - 0.5 / np.sqrt(3.0), 0.5 + 0.5 / np.sqrt(3.0)]
    result = np.zeros((24, 24))
    for point_z in points:
        for point_y in points:
            for point_x in points:
                strain = np.zeros((6, 24))
                for corner in range(8):
                    corner_z, corner_y, corner_x = CORNER_OFFSETS[corner]
                    along_x = point_x if corner_x else 1.0 - point_x
                    along_y = point_y if corner_y else 1.0 - point_y
                    along_z = point_z if corner_z else 1.0 - point_z
                    sign_x = 1.0 if corner_x else -1.0
                    sign_y = 1.0 if corner_y else -1.0
                    sign_z = 1.0 if corner_z else -1.0
                    grad_x = sign_x * along_y * along_z
                    grad_y = sign_y * along_x * along_z
                    grad_z = sign_z * along_x * along_y
                    column = 3 * corner
                    strain[0, column] = grad_x
                    strain[1, column + 1] = grad_y
                    strain[2, column + 2] = grad_z
                    strain[3, column] = grad_y
                    strain[3, column + 1] = grad_x
                    strain[4, column + 1] = grad_z
                    strain[4, column + 2] = grad_y
                    strain[5, column] = grad_z
                    strain[5, column + 2] = grad_x
                result += strain.T @ elastic @ strain / 8.0
    return result

def corner_views(padded, layers, rows, columns):
    views = []
    for shift_z, shift_y, shift_x in CORNER_OFFSETS:
        views.append(padded[:, :, shift_z:shift_z + layers, shift_y:shift_y + rows, shift_x:shift_x + columns])
    return views

def element_forces(views, stiffness, scale):
    stacked = jnp.concatenate(views, axis=1)
    product = jnp.einsum('ij,bjzyx->bizyx', stiffness, stacked, precision=lax.Precision.HIGHEST) * scale
    return [product[:, 3 * target:3 * target + 3] for target in range(8)]

def assemble(weighted, first, layers):
    total = None
    for target in range(8):
        shift_z, shift_y, shift_x = CORNER_OFFSETS[target]
        piece = weighted[target]
        rows = piece.shape[3]
        columns = piece.shape[4]
        padded = jnp.pad(piece, ((0, 0), (0, 0), (1, 1), (1, 0), (1, 0)))
        part_sum = padded[:, :, first - shift_z:first - shift_z + layers, 1 - shift_y:1 - shift_y + rows, 1 - shift_x:1 - shift_x + columns]
        total = part_sum if total is None else total + part_sum
    return total

def smooth(padded, layers, rows, columns):
    total = None
    for off_z in (-1, 0, 1):
        for off_y in (-1, 0, 1):
            for off_x in (-1, 0, 1):
                weight = 1.5 - float(np.sqrt(off_z * off_z + off_y * off_y + off_x * off_x))
                if weight > 0:
                    term = weight * padded[1 + off_z:1 + off_z + layers, 1 + off_y:1 + off_y + rows, 1 + off_x:1 + off_x + columns]
                    total = term if total is None else total + term
    return total

def reference(density, labels, forces, case_weights):
    stiffness = jnp.asarray(element_matrix(), jnp.float32)
    layers, rows, columns = density.shape
    solid = jnp.where(labels == 2, jnp.float32(1.0), density)
    moduli = EMIN + (1.0 - EMIN) * solid * solid * solid
    scale = moduli[None, None]
    free = (labels != 1).astype(jnp.float32)[None, None]
    diag_terms = []
    for target in range(8):
        entries = jnp.stack([stiffness[3 * target + comp, 3 * target + comp] for comp in range(3)])
        diag_terms.append(entries[None, :, None, None, None] * scale)
    diagonal = assemble(diag_terms, 1, layers)
    inverse_diag = free / diagonal
    theta = 0.5 * (UPPER_EIG + LOWER_EIG)
    delta = 0.5 * (UPPER_EIG - LOWER_EIG)
    sigma = theta / delta

    def pad_high(field):
        return jnp.pad(field, ((0, 0), (0, 0), (0, 1), (0, 1), (0, 1)))

    def operate(field):
        views = corner_views(pad_high(field), layers, rows, columns)
        return assemble(element_forces(views, stiffness, scale), 1, layers)

    def one_case(case_force):
        load = case_force[None] * free
        residual = load
        step_dir = inverse_diag * residual / theta
        solution = step_dir
        factor = 1.0 / sigma
        for sweep in range(SWEEPS):
            residual = residual - free * operate(step_dir)
            next_factor = 1.0 / (2.0 * sigma - factor)
            step_dir = next_factor * factor * step_dir + 2.0 * next_factor / delta * inverse_diag * residual
            solution = solution + step_dir
            factor = next_factor
        views = corner_views(pad_high(solution), layers, rows, columns)
        pushed = element_forces(views, stiffness, jnp.float32(1.0))
        energy = None
        for target in range(8):
            term = lax.optimization_barrier(jnp.sum(views[target] * pushed[target], axis=1))
            energy = term if energy is None else energy + term
        return (solution[0], energy[0])
    solutions, energies = lax.map(one_case, forces)
    weights = case_weights.astype(jnp.float32)
    weighted = lax.optimization_barrier(jnp.sum(weights[:, None, None, None] * energies, axis=0)) / jnp.sum(weights)
    sensitivity = 3.0 * (1.0 - EMIN) * solid * solid * weighted
    numer = smooth(jnp.pad(density * sensitivity, 1), layers, rows, columns)
    denom = smooth(jnp.pad(density, 1), layers, rows, columns)
    filtered = numer / denom
    mean_value = jnp.sum(filtered) / (layers * rows * columns)
    candidate = density * jnp.sqrt(filtered / mean_value)
    lower = jnp.maximum(density - MOVE_LIMIT, FLOOR_DENSITY)
    upper = jnp.minimum(density + MOVE_LIMIT, 1.0)
    new_density = jnp.clip(candidate, lower, upper)
    new_density = jnp.where(labels == 2, jnp.float32(1.0), new_density)
    return (new_density, solutions)
```

```python
import functools

import jax
import jax.numpy as jnp
import numpy as np
from jax import lax
from jax.experimental import pallas as pl
from jax.experimental.pallas import tpu as pltpu
from jax.sharding import PartitionSpec as P

MESH = pl.DeviceIdType.MESH
SWEEPS = 3
EMIN = 0.001
LOWER_EIG = 0.1
UPPER_EIG = 2.5
MOVE_LIMIT = 0.2
FLOOR_DENSITY = 0.001
THETA = 0.5 * (UPPER_EIG + LOWER_EIG)
DELTA = 0.5 * (UPPER_EIG - LOWER_EIG)
POISSON = 0.3
SHEAR = 1.0 / (2 * (1 + POISSON))
RATIO = 2 * POISSON / (1 - 2 * POISSON)
UNIT = SHEAR / 16.0
DIAG = UNIT * ((RATIO + 4.0) + (2.0 * (RATIO + 3.0) + 2.0) / 3.0 + (RATIO + 4.0) / 9.0)
EDGE = 1.5 - float(np.sqrt(2.0))


def chebyshev():
    sigma = THETA / DELTA
    factor = 1.0 / sigma
    pairs = []
    for _ in range(SWEEPS):
        following = 1.0 / (2.0 * sigma - factor)
        pairs.append((following * factor, 2.0 * following / DELTA))
        factor = following
    return pairs


def kernel(
    NL, Z, density, labels, forces, weights, newd, disp,
    F, LAB, D, DOWN, LNAT, EM, TX, INVD, R, STEP, SOL, XA, XD, UP, GU, OUT,
    PA, PB, V, G, QN, MS, RX, DS, SV, RX2,
    s_load, r_load, s_f, r_f, s_l, r_l, s_d, r_d, s_gh, r_gh, s_x, r_x, s_o, r_o, s_m, r_m, s_h, r_h, s_s, r_s, loc,
):
    rows = 8 * NL
    f32 = jnp.float32
    l = lax.axis_index("load")
    g = lax.axis_index("gz")
    core = g % 2
    yh = (g // 2) % 2
    z = g // 4

    def dev(ll, zz, yy, cc):
        return (lax.rem(ll + NL, NL), (lax.rem(zz + Z, Z) * 2 + yy) * 2 + cc)

    def remote(src, dst, ssem, rsem, target):
        return pltpu.make_async_remote_copy(
            src_ref=src, dst_ref=dst, send_sem=ssem, recv_sem=rsem, device_id=target, device_id_type=MESH
        )

    def arrived(ref, sem):
        pltpu.make_async_copy(ref, ref, sem).wait()

    lane = lax.broadcasted_iota(jnp.int32, (8, 128), 1)

    def xnext(v):
        return jnp.where(lane == 127, 0.0, pltpu.roll(v, 127, 1))

    def xprev(v):
        return jnp.where(lane == 0, 0.0, pltpu.roll(v, 1, 1))

    barrier = pltpu.get_barrier_semaphore()

    def greet(target):
        pl.semaphore_signal(barrier, inc=1, device_id=target, device_id_type=MESH)

    for a, b in ((0, 1), (1, 0), (1, 1)):
        greet(dev(l, z, (yh + a) % 2, (core + b) % 2))
    for k in range(1, NL):
        greet(dev(l + k, z, yh, core))
    for cc in range(2):
        greet(dev(l, z + 2 * core - 1, 1 - core, cc))
    for k in range(1, Z):
        greet(dev(l, z + k, yh, core))

    own_labels = pltpu.make_async_copy(labels, LNAT, loc.at[0])
    own_labels.start()
    zero8 = jnp.zeros((8, 128), f32)
    for r in range(12):
        D[r, 0:8, :] = zero8
        D[r, rows + 8 : rows + 16, :] = zero8
    for r in range(8):
        V[r, 0:8, :] = zero8
        V[r, rows + 8 : rows + 16, :] = zero8
    for m in range(9):
        TX[m, 0:8, :] = zero8
    for f in range(6):
        GU[f, 0:8, :] = zero8
    for k in range(2):
        QN[k, 0:8, :] = zero8
        QN[k, rows + 8 : rows + 16, :] = zero8
        for c in range(3):
            for m in range(10):
                XA[k, c, m, rows : rows + 8, :] = zero8
                XD[k, c, m, rows : rows + 8, :] = zero8
    for k in range(4):
        for t in range(3):
            DS[k, 8 * t : 8 * t + 8, :] = zero8
    for c in range(NL):
        for k in range(4):
            MS[c, k, 8:16, :] = zero8
    pl.semaphore_wait(barrier, 3 + (NL - 1) + 2 + (Z - 1))

    mine = pl.ds(pl.multiple_of(8 * l, 8), 8)
    load_copies = []
    for k in range(1, NL):
        cp = remote(density, DOWN.at[:, mine, :], s_load.at[k - 1], r_load, dev(l + k, z, yh, core))
        cp.start()
        load_copies.append(cp)
    load_self = pltpu.make_async_copy(density, DOWN.at[:, mine, :], r_load)
    load_self.start()

    first = (1 - yh) * 4 + 2 * core
    slot = first // 2
    zn = z + 2 * yh - 1
    targets = [(z, 0, yh), (z, 1, yh), (zn, 0, 1 - yh), (zn, 1, 1 - yh)]
    is_self = [jnp.logical_and(yh == 0, core == 0), jnp.logical_and(yh == 1, core == 1)]
    own_core = [yh, yh, 1 - yh, 1 - yh]

    def spread(make, local):
        for t, (zz, yy, cc) in enumerate(targets):
            if t < 2:
                @pl.when(is_self[t])
                def _():
                    local(t).start()

                @pl.when(jnp.logical_not(is_self[t]))
                def _():
                    make(t, dev(l, zz, yy, cc)).start()
            else:
                make(t, dev(l, zz, yy, cc)).start()

    def spread_sent(make):
        for t, (zz, yy, cc) in enumerate(targets):
            if t < 2:
                @pl.when(jnp.logical_not(is_self[t]))
                def _():
                    make(t, dev(l, zz, yy, cc)).wait_send()
            else:
                make(t, dev(l, zz, yy, cc)).wait_send()

    def f_dst():
        return F.at[:, pl.ds(first, 2), :, :]

    def f_make(t, target):
        return remote(forces.at[t % 2], f_dst(), s_f.at[t], r_f.at[slot], target)

    def f_local(t):
        return pltpu.make_async_copy(forces.at[t % 2], f_dst(), r_f.at[slot])

    def l_make(t, target):
        return remote(labels, LAB.at[pl.ds(first + 4 * own_core[t], 2)], s_l.at[t], r_l.at[slot + 2 * own_core[t]], target)

    def l_local(t):
        return pltpu.make_async_copy(labels, LAB.at[pl.ds(first + 4 * own_core[t], 2)], r_l.at[slot + 2 * own_core[t]])

    def d_dst(t):
        return D.at[pl.ds(first + 4 * own_core[t], 2), 8 : rows + 8, :]

    def d_make(t, target):
        return remote(DOWN, d_dst(t), s_d.at[t], r_d.at[slot + 2 * own_core[t]], target)

    def d_local(t):
        return pltpu.make_async_copy(DOWN, d_dst(t), r_d.at[slot + 2 * own_core[t]])

    is_a1 = jnp.logical_and(yh == 0, core == 1)

    def le_make():
        return remote(labels, LAB.at[2:4], s_l.at[4], r_l.at[1], dev(l, z, 1, 1))

    def de_make():
        return remote(DOWN, D.at[2:4, 8 : rows + 8, :], s_d.at[4], r_d.at[1], dev(l, z, 1, 1))

    spread(f_make, f_local)
    spread(l_make, l_local)

    @pl.when(is_a1)
    def _():
        le_make().start()
        pltpu.make_async_copy(labels, LAB.at[2:4], r_l.at[1]).start()

    arrived(DOWN, r_load)
    spread(d_make, d_local)

    @pl.when(is_a1)
    def _():
        de_make().start()
        pltpu.make_async_copy(DOWN, D.at[2:4, 8 : rows + 8, :], r_d.at[1]).start()

    own_labels.wait()
    for k in range(2):
        for c in range(NL):
            d = DOWN[k, 8 * c : 8 * c + 8, :]
            solid = jnp.where(LNAT[k, 8 * c : 8 * c + 8, :] == 2, 1.0, d)
            QN[k, 8 * c + 8 : 8 * c + 16, :] = d * solid * solid

    for k in range(4):
        at = 2 * k + 4 * core
        arrived(LAB.at[pl.ds(at, 2)], r_l.at[k + 2 * core])
        arrived(D.at[pl.ds(at, 2), 8 : rows + 8, :], r_d.at[k + 2 * core])

    @pl.when(core == 1)
    def _():
        arrived(LAB.at[2:4], r_l.at[1])
        arrived(D.at[2:4, 8 : rows + 8, :], r_d.at[1])

    sibling = dev(l, z, yh, 1 - core)

    def up_make():
        return remote(D.at[4:6, 8 : rows + 8, :], D.at[0:2, 8 : rows + 8, :], s_gh, r_gh, sibling)

    def down_make():
        return remote(D.at[4:8, 8 : rows + 8, :], D.at[8:12, 8 : rows + 8, :], s_gh, r_gh, sibling)

    @pl.when(core == 0)
    def _():
        up_make().start()

    @pl.when(core == 1)
    def _():
        down_make().start()

    sgn = 2 * core - 1

    def inside(p):
        at = 8 * z + p
        return jnp.logical_and(at >= 0, at < 8 * Z)

    def moduli_layer(m, _):
        p = 3 + sgn * m
        r = p + 4 * (1 - core)
        scale = jnp.where(inside(p), f32(UNIT), f32(0.0))
        for c in range(NL):
            d = D[r, 8 * c + 8 : 8 * c + 16, :]
            solid = jnp.where(LAB[r, 8 * c : 8 * c + 8, :] == 2, 1.0, d)
            e = (EMIN + (1.0 - EMIN) * solid * solid * solid) * scale
            EM[m, 8 * c : 8 * c + 8, :] = e
            TX[m, 8 * c + 8 : 8 * c + 16, :] = e + xprev(e)
        return 0

    lax.fori_loop(0, 8 + core, moduli_layer, 0)
    nodes = 7 + core

    def inverse_layer(m, _):
        p = jnp.where(core == 1, 3 + m, 4 - m)
        r = p + 4 * (1 - core)
        keep = inside(p).astype(jnp.int32)
        for c in range(NL):
            near = TX[m, 8 * c + 8 : 8 * c + 16, :] + TX[m, 8 * c + 7 : 8 * c + 15, :]
            far = TX[m - 1, 8 * c + 8 : 8 * c + 16, :] + TX[m - 1, 8 * c + 7 : 8 * c + 15, :]
            lab = LAB[r, 8 * c : 8 * c + 8, :] * keep + (1 - keep)
            INVD[m, 8 * c : 8 * c + 8, :] = jnp.where(lab != 1, (UNIT / DIAG) / (near + far), 0.0)
        return 0

    lax.fori_loop(1, nodes + 1, inverse_layer, 0)

    @pl.when(core == 0)
    def _():
        arrived(D.at[8:12, 8 : rows + 8, :], r_gh)

    @pl.when(core == 1)
    def _():
        arrived(D.at[0:2, 8 : rows + 8, :], r_gh)

    def plane_sums(center, above, below):
        ysum = above + below
        xsum = xnext(center) + xprev(center)
        cross = ysum + xsum
        corner = xnext(ysum) + xprev(ysum)
        return 1.5 * center + 0.5 * cross + EDGE * corner, 0.5 * center + EDGE * cross

    def d_plane(r, _):
        p = r - 4 * (1 - core)
        scale = jnp.where(inside(p), f32(1.0), f32(0.0))
        for c in range(NL):
            a, b = plane_sums(
                D[r, 8 * c + 8 : 8 * c + 16, :], D[r, 8 * c + 7 : 8 * c + 15, :], D[r, 8 * c + 9 : 8 * c + 17, :]
            )
            PA[r, 8 * c : 8 * c + 8, :] = a * scale
            PB[r, 8 * c : 8 * c + 8, :] = b * scale
        return 0

    lax.fori_loop(1, 11, d_plane, 0)

    def v_plane(r, _):
        p = r - 4 * (1 - core)
        ok = jnp.where(inside(p), f32(1.0), f32(0.0))
        for c in range(NL):
            at = slice(8 * c, 8 * c + 8)
            total = PA[r, at, :] + PB[r - 1, at, :] + PB[r + 1, at, :]
            V[r - 2, 8 * c + 8 : 8 * c + 16, :] = ok / (total + (1.0 - ok))
        return 0

    lax.fori_loop(2, 10, v_plane, 0)

    def w_plane(r, _):
        for c in range(NL):
            a, b = plane_sums(
                V[r - 2, 8 * c + 8 : 8 * c + 16, :], V[r - 2, 8 * c + 7 : 8 * c + 15, :], V[r - 2, 8 * c + 9 : 8 * c + 17, :]
            )
            PA[r, 8 * c : 8 * c + 8, :] = a
            PB[r, 8 * c : 8 * c + 8, :] = b
        return 0

    lax.fori_loop(3, 9, w_plane, 0)

    def g_plane(k, _):
        r = k + 4
        for c in range(NL):
            at = slice(8 * c, 8 * c + 8)
            d = D[r, 8 * c + 8 : 8 * c + 16, :]
            solid = jnp.where(LAB[r, at, :] == 2, 1.0, d)
            G[k, at, :] = (PA[r, at, :] + PB[r - 1, at, :] + PB[r + 1, at, :]) * (d * solid * solid)
        return 0

    lax.fori_loop(0, 4, g_plane, 0)

    for k in range(4):
        arrived(F.at[:, 2 * k : 2 * k + 2, :, :], r_f.at[k])
    flip = jnp.where(core == 1, f32(1.0), f32(-1.0))

    def x_make(par):
        return [
            remote(X.at[par, :, 1, 0:rows, :], X.at[par, :, 0, 0:rows, :], s_x.at[par, n], r_x.at[par, n], sibling)
            for n, X in enumerate((XA, XD))
        ]

    def first_step(m, _):
        i = jnp.where(core == 1, m - 1, 8 - m)
        for c in range(NL):
            at = slice(8 * c, 8 * c + 8)
            inv = INVD[m, at, :]
            for comp in range(3):
                f = F[comp, i, at, :]
                if comp == 2:
                    f = f * flip
                R[comp, m, at, :] = f
                s = inv * f * (1.0 / THETA)
                STEP[comp, m, at, :] = s
                SOL[comp, m, at, :] = s
                n = xnext(s)
                XA[0, comp, m, at, :] = s + n
                XD[0, comp, m, at, :] = n - s

        @pl.when(m == 1)
        def _():
            for cp in x_make(0):
                cp.start()

        return 0

    lax.fori_loop(1, nodes + 1, first_step, 0)

    def fields(par, comp, m, c):
        a0 = XA[par, comp, m, 8 * c : 8 * c + 8, :]
        a1 = XA[par, comp, m, 8 * c + 1 : 8 * c + 9, :]
        d0 = XD[par, comp, m, 8 * c : 8 * c + 8, :]
        d1 = XD[par, comp, m, 8 * c + 1 : 8 * c + 9, :]
        return a0 + a1, a1 - a0, d0 + d1, d1 - d0

    def modes(par, m, c):
        out = []
        for comp in range(3):
            lo = fields(par, comp, m, c)
            hi = fields(par, comp, m + 1, c)
            out.append(
                dict(
                    z=hi[0] - lo[0], y=hi[1] + lo[1], yz=hi[1] - lo[1], x=hi[2] + lo[2], zx=hi[2] - lo[2],
                    xy=hi[3] + lo[3], xyz=hi[3] - lo[3],
                )
            )
        return out

    def ghost(par):
        for n, X in enumerate((XA, XD)):
            arrived(X.at[par, :, 0, 0:rows, :], r_x.at[par, n])
            for c in range(NL):
                X[par, 2, 0, 8 * c : 8 * c + 8, :] = -X[par, 2, 0, 8 * c : 8 * c + 8, :]

    coefs = chebyshev()

    def sweep(s, _):
        par = s % 2
        nxt = 1 - par
        c1, c2 = f32(coefs[0][0]), f32(coefs[0][1])
        for n in range(1, SWEEPS):
            c1 = jnp.where(s == n, f32(coefs[n][0]), c1)
            c2 = jnp.where(s == n, f32(coefs[n][1]), c2)
        last = jnp.where(s == SWEEPS - 1, f32(1.0), f32(0.0))
        count = nodes - 1 - s
        ghost(par)

        def layer(m, _):
            put = jnp.where(m == 0, 9, m)
            for c in range(NL):
                at = slice(8 * c, 8 * c + 8)
                u, v, w = modes(par, m, c)
                e = EM[m, at, :]
                e2, e3, eq = e + e, e * (1.0 / 3.0), e * ((RATIO + 4.0) / 9.0)
                tr = (0.5 * RATIO) * (u["x"] + v["y"] + w["z"])
                fx = e2 * (tr + u["x"])
                fy = e2 * (tr + v["y"])
                fz = e2 * (tr + w["z"])
                sxy = e * (u["y"] + v["x"])
                syz = e * (v["z"] + w["y"])
                szx = e * (u["z"] + w["x"])
                h = 0.5 * (v["xy"] + w["zx"])
                vxy, wzx = e * (v["xy"] + h), e * (w["zx"] + h)
                h = 0.5 * (u["xy"] + w["yz"])
                uxy, wyz = e * (u["xy"] + h), e * (w["yz"] + h)
                h = 0.5 * (u["zx"] + v["yz"])
                uzx, vyz = e * (u["zx"] + h), e * (v["yz"] + h)
                h = u["yz"] + v["zx"] + w["xy"]
                uyz, vzx, wxy = e3 * (u["yz"] + h), e3 * (v["zx"] + h), e3 * (w["xy"] + h)
                uq, vq, wq = eq * u["xyz"], eq * v["xyz"], eq * w["xyz"]
                forces_of = (
                    (szx, sxy, uyz, fx, uzx, uxy, uq),
                    (syz, fy, vyz, sxy, vzx, vxy, vq),
                    (fz, syz, wyz, szx, wzx, wxy, wq),
                )
                inv = INVD[m, at, :]
                for comp in range(3):
                    gz_, gy, gyz, gx, gzx, gxy, gxyz = forces_of[comp]
                    taa = UP[4 * comp, at, :] - gz_
                    tay = UP[4 * comp + 1, at, :] + (gy - gyz)
                    tda = UP[4 * comp + 2, at, :] + (gx - gzx)
                    tdy = UP[4 * comp + 3, at, :] + (gxy - gxyz)
                    UP[4 * comp, at, :] = gz_
                    UP[4 * comp + 1, at, :] = gy + gyz
                    UP[4 * comp + 2, at, :] = gx + gzx
                    UP[4 * comp + 3, at, :] = gxy + gxyz
                    GU[2 * comp, 8 * c + 8 : 8 * c + 16, :] = taa + tay
                    GU[2 * comp + 1, 8 * c + 8 : 8 * c + 16, :] = tda + tdy
                    a = (taa - tay) + GU[2 * comp, 8 * c + 7 : 8 * c + 15, :]
                    b = (tda - tdy) + GU[2 * comp + 1, 8 * c + 7 : 8 * c + 15, :]
                    pushed = (a - b) + xprev(a + b)
                    res = R[comp, m, at, :] - pushed
                    R[comp, put, at, :] = res
                    step = c1 * STEP[comp, m, at, :] + c2 * (inv * res)
                    STEP[comp, put, at, :] = step
                    before = SOL[comp, m, at, :]
                    SOL[comp, put, at, :] = before + step
                    sent = step + last * before
                    n = xnext(sent)
                    XA[nxt, comp, put, at, :] = sent + n
                    XD[nxt, comp, put, at, :] = n - sent

            @pl.when(m == 1)
            def _():
                for cp in x_make(par):
                    cp.wait_send()
                for cp in x_make(nxt):
                    cp.start()

            return 0

        lax.fori_loop(0, count + 1, layer, 0)
        return 0

    for f in range(12):
        for c in range(NL):
            UP[f, 8 * c : 8 * c + 8, :] = zero8
    for c in range(NL):
        at = slice(8 * c, 8 * c + 8)
        INVD[0, at, :] = zero8
        for comp in range(3):
            R[comp, 0, at, :] = zero8
            STEP[comp, 0, at, :] = zero8
            SOL[comp, 0, at, :] = zero8
    lax.fori_loop(0, SWEEPS, sweep, 0)

    def lay_out(k, _):
        m = jnp.where(core == 1, k + 1, 4 - k)
        for c in range(NL):
            at = slice(8 * c, 8 * c + 8)
            for comp in range(3):
                v = SOL[comp, m, at, :]
                OUT[comp, k, at, :] = v * flip if comp == 2 else v
        return 0

    lax.fori_loop(0, 4, lay_out, 0)

    fin = SWEEPS % 2
    ghost(fin)
    weight = weights[2 * l + yh].astype(f32)
    weight_sum = weights[0]
    for n in range(1, 2 * NL):
        weight_sum = weight_sum + weights[n]
    weight_sum = weight_sum.astype(f32)

    def energy_layer(k, share):
        m = jnp.where(core == 1, k + 1, 3 - k)
        for c in range(NL):
            u, v, w = modes(fin, m, c)
            tr = u["x"] + v["y"] + w["z"]
            sq = lambda t: t * t
            normal = sq(u["x"]) + sq(v["y"]) + sq(w["z"])
            shear = sq(u["y"] + v["x"]) + sq(v["z"] + w["y"]) + sq(u["z"] + w["x"])
            pairs = (
                sq(v["xy"]) + sq(w["zx"]) + sq(u["xy"]) + sq(w["yz"]) + sq(u["zx"]) + sq(v["yz"])
            )
            joint = sq(v["xy"] + w["zx"]) + sq(u["xy"] + w["yz"]) + sq(u["zx"] + v["yz"])
            s = u["yz"] + v["zx"] + w["xy"]
            triple = sq(u["yz"]) + sq(v["zx"]) + sq(w["xy"]) + sq(s)
            quad = sq(u["xyz"]) + sq(v["xyz"]) + sq(w["xyz"])
            total = (
                (RATIO * sq(tr) + 2.0 * normal + shear) + (pairs + 0.5 * joint)
                + (1.0 / 3.0) * triple + ((RATIO + 4.0) / 9.0) * quad
            )
            t = (weight * UNIT) * total
            MS[c, k, 0:8, :] = t
            if c > 0:
                MS[c - 1, k, 9:10, :] = t[0:1, :]
            if c < NL - 1:
                MS[c + 1, k, 8:9, :] = t[7:8, :]
            share = share + t * G[k, 8 * c : 8 * c + 8, :]
        return share

    share = lax.fori_loop(0, 4, energy_layer, zero8)
    share = jnp.sum(share, axis=0, keepdims=True)
    for c in range(NL):
        for k in (0, 2):
            MS[c, k, 10:11, :] = share

    me = 2 * l + yh
    m_copies = []
    both = yh == core

    def m_make(k, cc):
        ll = lax.rem(l + k, NL)
        return remote(MS.at[ll, 2 * cc : 2 * cc + 2], RX.at[me], s_m.at[k, cc], r_m, dev(ll, z, core, cc))

    for k in range(NL):
        for cc in range(2):
            if k > 0:
                m_make(k, cc).start()
            else:
                alone = jnp.logical_and(both, core == cc)

                @pl.when(alone)
                def _():
                    pltpu.make_async_copy(MS.at[l, 2 * cc : 2 * cc + 2], RX.at[me], r_m).start()

                @pl.when(jnp.logical_not(alone))
                def _():
                    m_make(k, cc).start()

    def o_make(cc):
        return remote(OUT.at[:, 2 * cc : 2 * cc + 2], disp.at[yh], s_o.at[cc], r_o.at[yh], dev(l, z, core, cc))

    for cc in range(2):
        alone = jnp.logical_and(both, core == cc)

        @pl.when(alone)
        def _():
            pltpu.make_async_copy(OUT.at[:, 2 * cc : 2 * cc + 2], disp.at[yh], r_o.at[yh]).start()

        @pl.when(jnp.logical_not(alone))
        def _():
            o_make(cc).start()

    arrived(RX, r_m)
    scale = (3.0 * (1.0 - EMIN)) / weight_sum
    mean_part = None
    sums = []
    for k in range(2):
        main, rim = RX[0, k, 0:8, :], RX[0, k, 8:16, :]
        for n in range(1, 2 * NL):
            main = main + RX[n, k, 0:8, :]
            rim = rim + RX[n, k, 8:16, :]
        sums.append((main, rim))
    SV[...] = sums[0][1][2:3, :]

    def s_make(kz, ky):
        return remote(SV, RX2.at[2 * z + yh], s_s.at[kz, ky], r_s, dev(l, z + kz, (yh + ky) % 2, core))

    for kz in range(Z):
        for ky in range(2):
            if (kz, ky) != (0, 0):
                s_make(kz, ky).start()
    pltpu.make_async_copy(SV, RX2.at[2 * z + yh], r_s).start()

    base = pl.multiple_of(8 * l, 8)
    for k in range(2):
        main, rim = sums[k]
        before = QN[k, pl.ds(base, 8), :]
        here = QN[k, pl.ds(base + 8, 8), :]
        after = QN[k, pl.ds(base + 16, 8), :]
        DS[k + 1, 8:16, :] = main * here * scale
        DS[k + 1, 7:8, :] = rim[0:1, :] * before[7:8, :] * scale
        DS[k + 1, 16:17, :] = rim[1:2, :] * after[0:1, :] * scale

    def h_make(up):
        to = lax.rem(g + (1 if up else 4 * Z - 1), 4 * Z)
        return remote(DS.at[2 if up else 1], DS.at[0 if up else 3], s_h.at[int(up)], r_h.at[int(up)], (l, to))

    for up in (False, True):
        h_make(up).start()
    arrived(DS.at[3], r_h.at[0])
    arrived(DS.at[0], r_h.at[1])

    planes = []
    for k in range(4):
        planes.append(plane_sums(DS[k, 8:16, :], DS[k, 7:15, :], DS[k, 9:17, :]))
    low = jnp.where(g > 0, f32(1.0), f32(0.0)) * planes[0][1]
    high = jnp.where(g < 4 * Z - 1, f32(1.0), f32(0.0)) * planes[3][1]
    numer = [planes[1][0] + low + planes[2][1], planes[2][0] + planes[1][1] + high]
    v_at = 4 * yh + 2 * (1 - core)
    arrived(RX2, r_s)
    total = RX2[0]
    for n in range(1, 2 * Z):
        total = total + RX2[n]
    mean = jnp.sum(total, axis=1, keepdims=True) * scale / (8 * Z * rows * 128)
    for k in range(2):
        filtered = numer[k] * V[v_at + k, pl.ds(base + 8, 8), :]
        d = DOWN[k, mine, :]
        candidate = d * jnp.sqrt(filtered / mean)
        lower = jnp.maximum(d - MOVE_LIMIT, FLOOR_DENSITY)
        upper = jnp.minimum(d + MOVE_LIMIT, 1.0)
        new = jnp.minimum(jnp.maximum(candidate, lower), upper)
        newd[k] = jnp.where(LNAT[k, mine, :] == 2, 1.0, new)

    for cp in load_copies:
        cp.wait_send()
    spread_sent(f_make)
    spread_sent(l_make)
    spread_sent(d_make)

    @pl.when(is_a1)
    def _():
        le_make().wait_send()
        de_make().wait_send()

    @pl.when(core == 0)
    def _():
        up_make().wait_send()

    @pl.when(core == 1)
    def _():
        down_make().wait_send()

    for cp in x_make(fin):
        cp.wait_send()
    for k in range(NL):
        for cc in range(2):
            if k > 0:
                m_make(k, cc).wait_send()
            else:
                @pl.when(jnp.logical_not(jnp.logical_and(both, core == cc)))
                def _():
                    m_make(k, cc).wait_send()
    for cc in range(2):
        @pl.when(jnp.logical_not(jnp.logical_and(both, core == cc)))
        def _():
            o_make(cc).wait_send()
    for kz in range(Z):
        for ky in range(2):
            if (kz, ky) != (0, 0):
                s_make(kz, ky).wait_send()
    for up in (False, True):
        h_make(up).wait_send()
    for k in range(2):
        arrived(disp.at[k], r_o.at[k])


def solution(mesh):
    NL, Z = mesh.shape["load"], mesh.shape["gz"] // 4
    rows = 8 * NL

    def on_device(density, labels, forces, case_weights):
        vm = lambda *shape: pltpu.VMEM(shape, jnp.float32)
        dma = lambda *shape: pltpu.SemaphoreType.DMA(shape)
        scratch = [
            vm(3, 8, rows, 128),
            pltpu.VMEM((12, rows, 128), jnp.int32),
            vm(12, rows + 16, 128),
            vm(2, rows, 128),
            pltpu.VMEM((2, rows, 128), jnp.int32),
            vm(9, rows, 128),
            vm(9, rows + 8, 128),
            vm(9, rows, 128),
            vm(3, 10, rows, 128),
            vm(3, 10, rows, 128),
            vm(3, 10, rows, 128),
            vm(2, 3, 10, rows + 8, 128),
            vm(2, 3, 10, rows + 8, 128),
            vm(12, rows, 128),
            vm(6, rows + 8, 128),
            vm(3, 4, rows, 128),
            vm(12, rows, 128),
            vm(12, rows, 128),
            vm(8, rows + 16, 128),
            vm(4, rows, 128),
            vm(2, rows + 16, 128),
            vm(NL, 4, 16, 128),
            vm(2 * NL, 2, 16, 128),
            vm(4, 24, 128),
            vm(1, 128),
            vm(2 * Z, 1, 128),
            dma(NL), pltpu.SemaphoreType.DMA,
            dma(4), dma(4),
            dma(5), dma(6),
            dma(5), dma(6),
            pltpu.SemaphoreType.DMA, pltpu.SemaphoreType.DMA,
            dma(2, 2), dma(2, 2),
            dma(2), dma(2),
            dma(NL, 2), pltpu.SemaphoreType.DMA,
            dma(2), dma(2),
            dma(Z, 2), pltpu.SemaphoreType.DMA,
            dma(1),
        ]
        return pl.pallas_call(
            functools.partial(kernel, NL, Z),
            out_shape=(
                jax.ShapeDtypeStruct(density.shape, jnp.float32),
                jax.ShapeDtypeStruct(forces.shape, jnp.float32),
            ),
            in_specs=[pl.BlockSpec(memory_space=pl.ANY)] * 3 + [pl.BlockSpec(memory_space=pltpu.SMEM)],
            out_specs=(pl.BlockSpec(memory_space=pltpu.VMEM), pl.BlockSpec(memory_space=pl.ANY)),
            scratch_shapes=scratch,
            compiler_params=pltpu.CompilerParams(
                collective_id=1, has_side_effects=True, vmem_limit_bytes=32 << 20
            ),
            name="step",
        )(density, labels, forces, case_weights)

    return jax.shard_map(
        on_device,
        mesh=mesh,
        in_specs=(
            P("gz", "load", None),
            P("gz", None, None),
            P("load", None, "gz", None, None),
            P(),
        ),
        out_specs=(P("gz", "load", None), P("load", None, "gz", None, None)),
        check_vma=False,
    )
```

```python
import functools

import jax
import jax.numpy as jnp
import numpy as np
from jax import lax
from jax.experimental import pallas as pl
from jax.experimental.pallas import tpu as pltpu
from jax.sharding import PartitionSpec as P

MESH = pl.DeviceIdType.MESH
SWEEPS = 3
EMIN = 0.001
LOWER_EIG = 0.1
UPPER_EIG = 2.5
MOVE_LIMIT = 0.2
FLOOR_DENSITY = 0.001
THETA = 0.5 * (UPPER_EIG + LOWER_EIG)
DELTA = 0.5 * (UPPER_EIG - LOWER_EIG)
POISSON = 0.3
SHEAR = 1.0 / (2 * (1 + POISSON))
RATIO = 2 * POISSON / (1 - 2 * POISSON)
UNIT = SHEAR / 16.0
DIAG = UNIT * ((RATIO + 4.0) + (2.0 * (RATIO + 3.0) + 2.0) / 3.0 + (RATIO + 4.0) / 9.0)
EDGE = 1.5 - float(np.sqrt(2.0))


def chebyshev():
    sigma = THETA / DELTA
    factor = 1.0 / sigma
    pairs = []
    for _ in range(SWEEPS):
        following = 1.0 / (2.0 * sigma - factor)
        pairs.append((following * factor, 2.0 * following / DELTA))
        factor = following
    return pairs


def kernel(
    NL, Z, density, labels, forces, weights, newd, disp,
    F, LAB, D, DOWN, LNAT, EM, TX, INVD, R, STEP, SOL, XA0, XA1, XD0, XD1, UP, GU, OUT,
    PA, PB, V, G, QN, MS, RX, DS, SV, RX2,
    s_load, r_load, s_f, r_f, s_l, r_l, s_d, r_d, s_gh, r_gh, s_x, r_x, s_o, r_o, s_m, r_m, s_h, r_h, s_s, r_s, loc,
):
    rows = 8 * NL
    f32 = jnp.float32
    XA, XD = (XA0, XA1), (XD0, XD1)
    l = lax.axis_index("load")
    g = lax.axis_index("gz")
    core = g % 2
    yh = (g // 2) % 2
    z = g // 4

    def dev(ll, zz, yy, cc):
        return (lax.rem(ll + NL, NL), (lax.rem(zz + Z, Z) * 2 + yy) * 2 + cc)

    def remote(src, dst, ssem, rsem, target):
        return pltpu.make_async_remote_copy(
            src_ref=src, dst_ref=dst, send_sem=ssem, recv_sem=rsem, device_id=target, device_id_type=MESH
        )

    def arrived(ref, sem):
        pltpu.make_async_copy(ref, ref, sem).wait()

    lane = lax.broadcasted_iota(jnp.int32, (8, 128), 1)

    def xnext(v):
        return jnp.where(lane == 127, 0.0, pltpu.roll(v, 127, 1))

    def xprev(v):
        return jnp.where(lane == 0, 0.0, pltpu.roll(v, 1, 1))

    barrier = pltpu.get_barrier_semaphore()

    def greet(target):
        pl.semaphore_signal(barrier, inc=1, device_id=target, device_id_type=MESH)

    for a, b in ((0, 1), (1, 0), (1, 1)):
        greet(dev(l, z, (yh + a) % 2, (core + b) % 2))
    for k in range(1, NL):
        greet(dev(l + k, z, yh, core))
    for cc in range(2):
        greet(dev(l, z + 2 * core - 1, 1 - core, cc))
    for k in range(1, Z):
        greet(dev(l, z + k, yh, core))

    own_labels = pltpu.make_async_copy(labels, LNAT, loc.at[0])
    own_labels.start()
    zero8 = jnp.zeros((8, 128), f32)
    for r in range(12):
        D[r, 0:8, :] = zero8
        D[r, rows + 8 : rows + 16, :] = zero8
    for r in range(8):
        V[r, 0:8, :] = zero8
        V[r, rows + 8 : rows + 16, :] = zero8
    for m in range(9):
        TX[m, 0:8, :] = zero8
    for f in range(6):
        GU[f, 0:8, :] = zero8
    for k in range(2):
        QN[k, 0:8, :] = zero8
        QN[k, rows + 8 : rows + 16, :] = zero8
        for c in range(3):
            for m in range(10):
                XA[k][c, m, rows : rows + 8, :] = zero8
                XD[k][c, m, rows : rows + 8, :] = zero8
    for k in range(4):
        for t in range(3):
            DS[k, 8 * t : 8 * t + 8, :] = zero8
    for c in range(NL):
        for k in range(4):
            MS[c, k, 8:16, :] = zero8
    pl.semaphore_wait(barrier, 3 + (NL - 1) + 2 + (Z - 1))

    mine = pl.ds(pl.multiple_of(8 * l, 8), 8)
    load_copies = []
    for k in range(1, NL):
        cp = remote(density, DOWN.at[:, mine, :], s_load.at[k - 1], r_load, dev(l + k, z, yh, core))
        cp.start()
        load_copies.append(cp)
    load_self = pltpu.make_async_copy(density, DOWN.at[:, mine, :], r_load)
    load_self.start()

    first = (1 - yh) * 4 + 2 * core
    slot = first // 2
    zn = z + 2 * yh - 1
    targets = [(z, 0, yh), (z, 1, yh), (zn, 0, 1 - yh), (zn, 1, 1 - yh)]
    is_self = [jnp.logical_and(yh == 0, core == 0), jnp.logical_and(yh == 1, core == 1)]
    own_core = [yh, yh, 1 - yh, 1 - yh]

    def spread(make, local):
        for t, (zz, yy, cc) in enumerate(targets):
            if t < 2:
                @pl.when(is_self[t])
                def _():
                    local(t).start()

                @pl.when(jnp.logical_not(is_self[t]))
                def _():
                    make(t, dev(l, zz, yy, cc)).start()
            else:
                make(t, dev(l, zz, yy, cc)).start()

    def spread_sent(make):
        for t, (zz, yy, cc) in enumerate(targets):
            if t < 2:
                @pl.when(jnp.logical_not(is_self[t]))
                def _():
                    make(t, dev(l, zz, yy, cc)).wait_send()
            else:
                make(t, dev(l, zz, yy, cc)).wait_send()

    def f_dst():
        return F.at[:, pl.ds(first, 2), :, :]

    def f_make(t, target):
        return remote(forces.at[t % 2], f_dst(), s_f.at[t], r_f.at[slot], target)

    def f_local(t):
        return pltpu.make_async_copy(forces.at[t % 2], f_dst(), r_f.at[slot])

    def l_make(t, target):
        return remote(labels, LAB.at[pl.ds(first + 4 * own_core[t], 2)], s_l.at[t], r_l.at[slot + 2 * own_core[t]], target)

    def l_local(t):
        return pltpu.make_async_copy(labels, LAB.at[pl.ds(first + 4 * own_core[t], 2)], r_l.at[slot + 2 * own_core[t]])

    def d_dst(t):
        return D.at[pl.ds(first + 4 * own_core[t], 2), 8 : rows + 8, :]

    def d_make(t, target):
        return remote(DOWN, d_dst(t), s_d.at[t], r_d.at[slot + 2 * own_core[t]], target)

    def d_local(t):
        return pltpu.make_async_copy(DOWN, d_dst(t), r_d.at[slot + 2 * own_core[t]])

    is_a1 = jnp.logical_and(yh == 0, core == 1)

    def le_make():
        return remote(labels, LAB.at[2:4], s_l.at[4], r_l.at[1], dev(l, z, 1, 1))

    def de_make():
        return remote(DOWN, D.at[2:4, 8 : rows + 8, :], s_d.at[4], r_d.at[1], dev(l, z, 1, 1))

    spread(f_make, f_local)
    spread(l_make, l_local)

    @pl.when(is_a1)
    def _():
        le_make().start()
        pltpu.make_async_copy(labels, LAB.at[2:4], r_l.at[1]).start()

    arrived(DOWN, r_load)
    spread(d_make, d_local)

    @pl.when(is_a1)
    def _():
        de_make().start()
        pltpu.make_async_copy(DOWN, D.at[2:4, 8 : rows + 8, :], r_d.at[1]).start()

    own_labels.wait()
    for k in range(2):
        for c in range(NL):
            d = DOWN[k, 8 * c : 8 * c + 8, :]
            solid = jnp.where(LNAT[k, 8 * c : 8 * c + 8, :] == 2, 1.0, d)
            QN[k, 8 * c + 8 : 8 * c + 16, :] = d * solid * solid

    for k in range(4):
        at = 2 * k + 4 * core
        arrived(LAB.at[pl.ds(at, 2)], r_l.at[k + 2 * core])
        arrived(D.at[pl.ds(at, 2), 8 : rows + 8, :], r_d.at[k + 2 * core])

    @pl.when(core == 1)
    def _():
        arrived(LAB.at[2:4], r_l.at[1])
        arrived(D.at[2:4, 8 : rows + 8, :], r_d.at[1])

    sibling = dev(l, z, yh, 1 - core)

    def up_make():
        return remote(D.at[4:6, 8 : rows + 8, :], D.at[0:2, 8 : rows + 8, :], s_gh, r_gh, sibling)

    def down_make():
        return remote(D.at[4:8, 8 : rows + 8, :], D.at[8:12, 8 : rows + 8, :], s_gh, r_gh, sibling)

    @pl.when(core == 0)
    def _():
        up_make().start()

    @pl.when(core == 1)
    def _():
        down_make().start()

    sgn = 2 * core - 1

    def inside(p):
        at = 8 * z + p
        return jnp.logical_and(at >= 0, at < 8 * Z)

    def moduli_layer(m, _):
        p = 3 + sgn * m
        r = p + 4 * (1 - core)
        scale = jnp.where(inside(p), f32(UNIT), f32(0.0))
        for c in range(NL):
            d = D[r, 8 * c + 8 : 8 * c + 16, :]
            solid = jnp.where(LAB[r, 8 * c : 8 * c + 8, :] == 2, 1.0, d)
            e = (EMIN + (1.0 - EMIN) * solid * solid * solid) * scale
            EM[m, 8 * c : 8 * c + 8, :] = e
            TX[m, 8 * c + 8 : 8 * c + 16, :] = e + xprev(e)
        return 0

    lax.fori_loop(0, 8 + core, moduli_layer, 0)
    nodes = 7 + core

    def inverse_layer(m, _):
        p = jnp.where(core == 1, 3 + m, 4 - m)
        r = p + 4 * (1 - core)
        keep = inside(p).astype(jnp.int32)
        for c in range(NL):
            near = TX[m, 8 * c + 8 : 8 * c + 16, :] + TX[m, 8 * c + 7 : 8 * c + 15, :]
            far = TX[m - 1, 8 * c + 8 : 8 * c + 16, :] + TX[m - 1, 8 * c + 7 : 8 * c + 15, :]
            lab = LAB[r, 8 * c : 8 * c + 8, :] * keep + (1 - keep)
            INVD[m, 8 * c : 8 * c + 8, :] = jnp.where(lab != 1, (UNIT / DIAG) / (near + far), 0.0)
        return 0

    lax.fori_loop(1, nodes + 1, inverse_layer, 0)

    @pl.when(core == 0)
    def _():
        arrived(D.at[8:12, 8 : rows + 8, :], r_gh)

    @pl.when(core == 1)
    def _():
        arrived(D.at[0:2, 8 : rows + 8, :], r_gh)

    def plane_sums(center, above, below):
        ysum = above + below
        xsum = xnext(center) + xprev(center)
        cross = ysum + xsum
        corner = xnext(ysum) + xprev(ysum)
        return 1.5 * center + 0.5 * cross + EDGE * corner, 0.5 * center + EDGE * cross

    def d_plane(r, _):
        p = r - 4 * (1 - core)
        scale = jnp.where(inside(p), f32(1.0), f32(0.0))
        for c in range(NL):
            a, b = plane_sums(
                D[r, 8 * c + 8 : 8 * c + 16, :], D[r, 8 * c + 7 : 8 * c + 15, :], D[r, 8 * c + 9 : 8 * c + 17, :]
            )
            PA[r, 8 * c : 8 * c + 8, :] = a * scale
            PB[r, 8 * c : 8 * c + 8, :] = b * scale
        return 0

    lax.fori_loop(1, 11, d_plane, 0)

    def v_plane(r, _):
        p = r - 4 * (1 - core)
        ok = jnp.where(inside(p), f32(1.0), f32(0.0))
        for c in range(NL):
            at = slice(8 * c, 8 * c + 8)
            total = PA[r, at, :] + PB[r - 1, at, :] + PB[r + 1, at, :]
            V[r - 2, 8 * c + 8 : 8 * c + 16, :] = ok / (total + (1.0 - ok))
        return 0

    lax.fori_loop(2, 10, v_plane, 0)

    def w_plane(r, _):
        for c in range(NL):
            a, b = plane_sums(
                V[r - 2, 8 * c + 8 : 8 * c + 16, :], V[r - 2, 8 * c + 7 : 8 * c + 15, :], V[r - 2, 8 * c + 9 : 8 * c + 17, :]
            )
            PA[r, 8 * c : 8 * c + 8, :] = a
            PB[r, 8 * c : 8 * c + 8, :] = b
        return 0

    lax.fori_loop(3, 9, w_plane, 0)

    def g_plane(k, _):
        r = k + 4
        for c in range(NL):
            at = slice(8 * c, 8 * c + 8)
            d = D[r, 8 * c + 8 : 8 * c + 16, :]
            solid = jnp.where(LAB[r, at, :] == 2, 1.0, d)
            G[k, at, :] = (PA[r, at, :] + PB[r - 1, at, :] + PB[r + 1, at, :]) * (d * solid * solid)
        return 0

    lax.fori_loop(0, 4, g_plane, 0)

    for k in range(4):
        arrived(F.at[:, 2 * k : 2 * k + 2, :, :], r_f.at[k])
    flip = jnp.where(core == 1, f32(1.0), f32(-1.0))

    def x_make(par):
        return [
            remote(X[par].at[:, 1, 0:rows, :], X[par].at[:, 0, 0:rows, :], s_x.at[par, n], r_x.at[par, n], sibling)
            for n, X in enumerate((XA, XD))
        ]

    def first_step(m, _):
        i = jnp.where(core == 1, m - 1, 8 - m)
        for c in range(NL):
            at = slice(8 * c, 8 * c + 8)
            inv = INVD[m, at, :]
            for comp in range(3):
                f = F[comp, i, at, :]
                if comp == 2:
                    f = f * flip
                R[comp, m, at, :] = f
                s = inv * f * (1.0 / THETA)
                STEP[comp, m, at, :] = s
                SOL[comp, m, at, :] = s
                n = xnext(s)
                XA[0][comp, m, at, :] = s + n
                XD[0][comp, m, at, :] = n - s

        @pl.when(m == 1)
        def _():
            for cp in x_make(0):
                cp.start()

        return 0

    lax.fori_loop(1, nodes + 1, first_step, 0)

    def fields(par, comp, m, c):
        a0 = XA[par][comp, m, 8 * c : 8 * c + 8, :]
        a1 = XA[par][comp, m, 8 * c + 1 : 8 * c + 9, :]
        d0 = XD[par][comp, m, 8 * c : 8 * c + 8, :]
        d1 = XD[par][comp, m, 8 * c + 1 : 8 * c + 9, :]
        return a0 + a1, a1 - a0, d0 + d1, d1 - d0

    def modes(par, m, c):
        out = []
        for comp in range(3):
            lo = fields(par, comp, m, c)
            hi = fields(par, comp, m + 1, c)
            out.append(
                dict(
                    z=hi[0] - lo[0], y=hi[1] + lo[1], yz=hi[1] - lo[1], x=hi[2] + lo[2], zx=hi[2] - lo[2],
                    xy=hi[3] + lo[3], xyz=hi[3] - lo[3],
                )
            )
        return out

    def ghost(par):
        for n, X in enumerate((XA, XD)):
            arrived(X[par].at[:, 0, 0:rows, :], r_x.at[par, n])
            for c in range(NL):
                X[par][2, 0, 8 * c : 8 * c + 8, :] = -X[par][2, 0, 8 * c : 8 * c + 8, :]

    coefs = chebyshev()

    def element_forces(par, m, c):
        u, v, w = modes(par, m, c)
        e = EM[m, 8 * c : 8 * c + 8, :]
        e2, e3, eq = e + e, e * (1.0 / 3.0), e * ((RATIO + 4.0) / 9.0)
        tr = (0.5 * RATIO) * (u["x"] + v["y"] + w["z"])
        fx = e2 * (tr + u["x"])
        fy = e2 * (tr + v["y"])
        fz = e2 * (tr + w["z"])
        sxy = e * (u["y"] + v["x"])
        syz = e * (v["z"] + w["y"])
        szx = e * (u["z"] + w["x"])
        h = 0.5 * (v["xy"] + w["zx"])
        vxy, wzx = e * (v["xy"] + h), e * (w["zx"] + h)
        h = 0.5 * (u["xy"] + w["yz"])
        uxy, wyz = e * (u["xy"] + h), e * (w["yz"] + h)
        h = 0.5 * (u["zx"] + v["yz"])
        uzx, vyz = e * (u["zx"] + h), e * (v["yz"] + h)
        h = u["yz"] + v["zx"] + w["xy"]
        uyz, vzx, wxy = e3 * (u["yz"] + h), e3 * (v["zx"] + h), e3 * (w["xy"] + h)
        uq, vq, wq = eq * u["xyz"], eq * v["xyz"], eq * w["xyz"]
        return (
            (szx, sxy, uyz, fx, uzx, uxy, uq),
            (syz, fy, vyz, sxy, vzx, vxy, vq),
            (fz, syz, wyz, szx, wzx, wxy, wq),
        )

    def push_up(comp, at, force):
        gz_, gy, gyz, gx, gzx, gxy, gxyz = force
        UP[4 * comp, at, :] = gz_
        UP[4 * comp + 1, at, :] = gy + gyz
        UP[4 * comp + 2, at, :] = gx + gzx
        UP[4 * comp + 3, at, :] = gxy + gxyz

    def sweep(s):
        par = s % 2
        nxt = 1 - par
        c1, c2 = coefs[s]
        ghost(par)
        for c in range(NL):
            at = slice(8 * c, 8 * c + 8)
            for comp, force in enumerate(element_forces(par, 0, c)):
                push_up(comp, at, force)

        def layer(m, _):
            for c in range(NL):
                at = slice(8 * c, 8 * c + 8)
                inv = INVD[m, at, :]
                for comp, force in enumerate(element_forces(par, m, c)):
                    gz_, gy, gyz, gx, gzx, gxy, gxyz = force
                    taa = UP[4 * comp, at, :] - gz_
                    tay = UP[4 * comp + 1, at, :] + (gy - gyz)
                    tda = UP[4 * comp + 2, at, :] + (gx - gzx)
                    tdy = UP[4 * comp + 3, at, :] + (gxy - gxyz)
                    push_up(comp, at, force)
                    GU[2 * comp, 8 * c + 8 : 8 * c + 16, :] = taa + tay
                    GU[2 * comp + 1, 8 * c + 8 : 8 * c + 16, :] = tda + tdy
                    a = (taa - tay) + GU[2 * comp, 8 * c + 7 : 8 * c + 15, :]
                    b = (tda - tdy) + GU[2 * comp + 1, 8 * c + 7 : 8 * c + 15, :]
                    pushed = (a - b) + xprev(a + b)
                    res = R[comp, m, at, :] - pushed
                    R[comp, m, at, :] = res
                    step = c1 * STEP[comp, m, at, :] + c2 * (inv * res)
                    STEP[comp, m, at, :] = step
                    sent = SOL[comp, m, at, :] + step
                    SOL[comp, m, at, :] = sent
                    if s < SWEEPS - 1:
                        sent = step
                    n = xnext(sent)
                    XA[nxt][comp, m, at, :] = sent + n
                    XD[nxt][comp, m, at, :] = n - sent

            @pl.when(m == 1)
            def _():
                for cp in x_make(par):
                    cp.wait_send()
                for cp in x_make(nxt):
                    cp.start()

            return 0

        lax.fori_loop(1, nodes - s, layer, 0)

    for s in range(SWEEPS):
        sweep(s)

    def lay_out(k, _):
        m = jnp.where(core == 1, k + 1, 4 - k)
        for c in range(NL):
            at = slice(8 * c, 8 * c + 8)
            for comp in range(3):
                v = SOL[comp, m, at, :]
                OUT[comp, k, at, :] = v * flip if comp == 2 else v
        return 0

    lax.fori_loop(0, 4, lay_out, 0)

    fin = SWEEPS % 2
    ghost(fin)
    weight = weights[2 * l + yh].astype(f32)
    weight_sum = weights[0]
    for n in range(1, 2 * NL):
        weight_sum = weight_sum + weights[n]
    weight_sum = weight_sum.astype(f32)

    def energy_layer(k, share):
        m = jnp.where(core == 1, k + 1, 3 - k)
        for c in range(NL):
            u, v, w = modes(fin, m, c)
            tr = u["x"] + v["y"] + w["z"]
            sq = lambda t: t * t
            normal = sq(u["x"]) + sq(v["y"]) + sq(w["z"])
            shear = sq(u["y"] + v["x"]) + sq(v["z"] + w["y"]) + sq(u["z"] + w["x"])
            pairs = (
                sq(v["xy"]) + sq(w["zx"]) + sq(u["xy"]) + sq(w["yz"]) + sq(u["zx"]) + sq(v["yz"])
            )
            joint = sq(v["xy"] + w["zx"]) + sq(u["xy"] + w["yz"]) + sq(u["zx"] + v["yz"])
            s = u["yz"] + v["zx"] + w["xy"]
            triple = sq(u["yz"]) + sq(v["zx"]) + sq(w["xy"]) + sq(s)
            quad = sq(u["xyz"]) + sq(v["xyz"]) + sq(w["xyz"])
            total = (
                (RATIO * sq(tr) + 2.0 * normal + shear) + (pairs + 0.5 * joint)
                + (1.0 / 3.0) * triple + ((RATIO + 4.0) / 9.0) * quad
            )
            t = (weight * UNIT) * total
            MS[c, k, 0:8, :] = t
            if c > 0:
                MS[c - 1, k, 9:10, :] = t[0:1, :]
            if c < NL - 1:
                MS[c + 1, k, 8:9, :] = t[7:8, :]
            share = share + t * G[k, 8 * c : 8 * c + 8, :]
        return share

    share = lax.fori_loop(0, 4, energy_layer, zero8)
    share = jnp.sum(share, axis=0, keepdims=True)
    for c in range(NL):
        for k in (0, 2):
            MS[c, k, 10:11, :] = share

    me = 2 * l + yh
    m_copies = []
    both = yh == core

    def m_make(k, cc):
        ll = lax.rem(l + k, NL)
        return remote(MS.at[ll, 2 * cc : 2 * cc + 2], RX.at[me], s_m.at[k, cc], r_m, dev(ll, z, core, cc))

    for k in range(NL):
        for cc in range(2):
            if k > 0:
                m_make(k, cc).start()
            else:
                alone = jnp.logical_and(both, core == cc)

                @pl.when(alone)
                def _():
                    pltpu.make_async_copy(MS.at[l, 2 * cc : 2 * cc + 2], RX.at[me], r_m).start()

                @pl.when(jnp.logical_not(alone))
                def _():
                    m_make(k, cc).start()

    def o_make(cc):
        return remote(OUT.at[:, 2 * cc : 2 * cc + 2], disp.at[yh], s_o.at[cc], r_o.at[yh], dev(l, z, core, cc))

    for cc in range(2):
        alone = jnp.logical_and(both, core == cc)

        @pl.when(alone)
        def _():
            pltpu.make_async_copy(OUT.at[:, 2 * cc : 2 * cc + 2], disp.at[yh], r_o.at[yh]).start()

        @pl.when(jnp.logical_not(alone))
        def _():
            o_make(cc).start()

    arrived(RX, r_m)
    scale = (3.0 * (1.0 - EMIN)) / weight_sum
    mean_part = None
    sums = []
    for k in range(2):
        main, rim = RX[0, k, 0:8, :], RX[0, k, 8:16, :]
        for n in range(1, 2 * NL):
            main = main + RX[n, k, 0:8, :]
            rim = rim + RX[n, k, 8:16, :]
        sums.append((main, rim))
    SV[...] = sums[0][1][2:3, :]

    def s_make(kz, ky):
        return remote(SV, RX2.at[2 * z + yh], s_s.at[kz, ky], r_s, dev(l, z + kz, (yh + ky) % 2, core))

    for kz in range(Z):
        for ky in range(2):
            if (kz, ky) != (0, 0):
                s_make(kz, ky).start()
    pltpu.make_async_copy(SV, RX2.at[2 * z + yh], r_s).start()

    base = pl.multiple_of(8 * l, 8)
    for k in range(2):
        main, rim = sums[k]
        before = QN[k, pl.ds(base, 8), :]
        here = QN[k, pl.ds(base + 8, 8), :]
        after = QN[k, pl.ds(base + 16, 8), :]
        DS[k + 1, 8:16, :] = main * here * scale
        DS[k + 1, 7:8, :] = rim[0:1, :] * before[7:8, :] * scale
        DS[k + 1, 16:17, :] = rim[1:2, :] * after[0:1, :] * scale

    def h_make(up):
        to = lax.rem(g + (1 if up else 4 * Z - 1), 4 * Z)
        return remote(DS.at[2 if up else 1], DS.at[0 if up else 3], s_h.at[int(up)], r_h.at[int(up)], (l, to))

    for up in (False, True):
        h_make(up).start()
    arrived(DS.at[3], r_h.at[0])
    arrived(DS.at[0], r_h.at[1])

    planes = []
    for k in range(4):
        planes.append(plane_sums(DS[k, 8:16, :], DS[k, 7:15, :], DS[k, 9:17, :]))
    low = jnp.where(g > 0, f32(1.0), f32(0.0)) * planes[0][1]
    high = jnp.where(g < 4 * Z - 1, f32(1.0), f32(0.0)) * planes[3][1]
    numer = [planes[1][0] + low + planes[2][1], planes[2][0] + planes[1][1] + high]
    v_at = 4 * yh + 2 * (1 - core)
    arrived(RX2, r_s)
    total = RX2[0]
    for n in range(1, 2 * Z):
        total = total + RX2[n]
    mean = jnp.sum(total, axis=1, keepdims=True) * scale / (8 * Z * rows * 128)
    for k in range(2):
        filtered = numer[k] * V[v_at + k, pl.ds(base + 8, 8), :]
        d = DOWN[k, mine, :]
        candidate = d * jnp.sqrt(filtered / mean)
        lower = jnp.maximum(d - MOVE_LIMIT, FLOOR_DENSITY)
        upper = jnp.minimum(d + MOVE_LIMIT, 1.0)
        new = jnp.minimum(jnp.maximum(candidate, lower), upper)
        newd[k] = jnp.where(LNAT[k, mine, :] == 2, 1.0, new)

    for cp in load_copies:
        cp.wait_send()
    spread_sent(f_make)
    spread_sent(l_make)
    spread_sent(d_make)

    @pl.when(is_a1)
    def _():
        le_make().wait_send()
        de_make().wait_send()

    @pl.when(core == 0)
    def _():
        up_make().wait_send()

    @pl.when(core == 1)
    def _():
        down_make().wait_send()

    for cp in x_make(fin):
        cp.wait_send()
    for k in range(NL):
        for cc in range(2):
            if k > 0:
                m_make(k, cc).wait_send()
            else:
                @pl.when(jnp.logical_not(jnp.logical_and(both, core == cc)))
                def _():
                    m_make(k, cc).wait_send()
    for cc in range(2):
        @pl.when(jnp.logical_not(jnp.logical_and(both, core == cc)))
        def _():
            o_make(cc).wait_send()
    for kz in range(Z):
        for ky in range(2):
            if (kz, ky) != (0, 0):
                s_make(kz, ky).wait_send()
    for up in (False, True):
        h_make(up).wait_send()
    for k in range(2):
        arrived(disp.at[k], r_o.at[k])


def solution(mesh):
    NL, Z = mesh.shape["load"], mesh.shape["gz"] // 4
    rows = 8 * NL

    def on_device(density, labels, forces, case_weights):
        vm = lambda *shape: pltpu.VMEM(shape, jnp.float32)
        dma = lambda *shape: pltpu.SemaphoreType.DMA(shape)
        scratch = [
            vm(3, 8, rows, 128),
            pltpu.VMEM((12, rows, 128), jnp.int32),
            vm(12, rows + 16, 128),
            vm(2, rows, 128),
            pltpu.VMEM((2, rows, 128), jnp.int32),
            vm(9, rows, 128),
            vm(9, rows + 8, 128),
            vm(9, rows, 128),
            vm(3, 10, rows, 128),
            vm(3, 10, rows, 128),
            vm(3, 10, rows, 128),
            vm(3, 10, rows + 8, 128),
            vm(3, 10, rows + 8, 128),
            vm(3, 10, rows + 8, 128),
            vm(3, 10, rows + 8, 128),
            vm(12, rows, 128),
            vm(6, rows + 8, 128),
            vm(3, 4, rows, 128),
            vm(12, rows, 128),
            vm(12, rows, 128),
            vm(8, rows + 16, 128),
            vm(4, rows, 128),
            vm(2, rows + 16, 128),
            vm(NL, 4, 16, 128),
            vm(2 * NL, 2, 16, 128),
            vm(4, 24, 128),
            vm(1, 128),
            vm(2 * Z, 1, 128),
            dma(NL), pltpu.SemaphoreType.DMA,
            dma(4), dma(4),
            dma(5), dma(6),
            dma(5), dma(6),
            pltpu.SemaphoreType.DMA, pltpu.SemaphoreType.DMA,
            dma(2, 2), dma(2, 2),
            dma(2), dma(2),
            dma(NL, 2), pltpu.SemaphoreType.DMA,
            dma(2), dma(2),
            dma(Z, 2), pltpu.SemaphoreType.DMA,
            dma(1),
        ]
        return pl.pallas_call(
            functools.partial(kernel, NL, Z),
            out_shape=(
                jax.ShapeDtypeStruct(density.shape, jnp.float32),
                jax.ShapeDtypeStruct(forces.shape, jnp.float32),
            ),
            in_specs=[pl.BlockSpec(memory_space=pl.ANY)] * 3 + [pl.BlockSpec(memory_space=pltpu.SMEM)],
            out_specs=(pl.BlockSpec(memory_space=pltpu.VMEM), pl.BlockSpec(memory_space=pl.ANY)),
            scratch_shapes=scratch,
            compiler_params=pltpu.CompilerParams(
                collective_id=1, has_side_effects=True, vmem_limit_bytes=32 << 20
            ),
            name="step",
        )(density, labels, forces, case_weights)

    return jax.shard_map(
        on_device,
        mesh=mesh,
        in_specs=(
            P("gz", "load", None),
            P("gz", None, None),
            P("load", None, "gz", None, None),
            P(),
        ),
        out_specs=(P("gz", "load", None), P("load", None, "gz", None, None)),
        check_vma=False,
    )
```

```python
import functools

import jax
import jax.numpy as jnp
import numpy as np
from jax import lax
from jax.experimental import pallas as pl
from jax.experimental.pallas import tpu as pltpu
from jax.sharding import PartitionSpec as P

MESH = pl.DeviceIdType.MESH
SWEEPS = 3
EMIN = 0.001
LOWER_EIG = 0.1
UPPER_EIG = 2.5
MOVE_LIMIT = 0.2
FLOOR_DENSITY = 0.001
THETA = 0.5 * (UPPER_EIG + LOWER_EIG)
DELTA = 0.5 * (UPPER_EIG - LOWER_EIG)
POISSON = 0.3
SHEAR = 1.0 / (2 * (1 + POISSON))
RATIO = 2 * POISSON / (1 - 2 * POISSON)
UNIT = SHEAR / 16.0
DIAG = UNIT * ((RATIO + 4.0) + (2.0 * (RATIO + 3.0) + 2.0) / 3.0 + (RATIO + 4.0) / 9.0)
EDGE = 1.5 - float(np.sqrt(2.0))


def chebyshev():
    sigma = THETA / DELTA
    factor = 1.0 / sigma
    pairs = []
    for _ in range(SWEEPS):
        following = 1.0 / (2.0 * sigma - factor)
        pairs.append((following * factor, 2.0 * following / DELTA))
        factor = following
    return pairs


def kernel(
    NL, Z, density, labels, forces, weights_in, newd, disp,
    F, LAB, D, EM, TX, INVD, R, STEP, SOL, XA0, XA1, XD0, XD1, UP, GU, OUT, ZS, ZG,
    PA, PB, V, VO, G, MS, RX, DS, SV, RX2, weights, spare,
    s_d, r_d, s_e, r_e, s_f, r_f, s_l, r_l, s_v, r_v, s_x, r_x, s_z, r_z,
    s_o, r_o, s_m, r_m, s_h, r_h, s_s, r_s, loc,
):
    rows = 8 * NL
    f32 = jnp.float32
    XA, XD = (XA0, XA1), (XD0, XD1)
    l = lax.axis_index("load")
    g = lax.axis_index("gz")
    core = g % 2
    yh = (g // 2) % 2
    z = g // 4

    def dev(ll, zz, yy, cc):
        return (lax.rem(ll + NL, NL), (lax.rem(zz + Z, Z) * 2 + yy) * 2 + cc)

    def remote(src, dst, ssem, rsem, target):
        return pltpu.make_async_remote_copy(
            src_ref=src, dst_ref=dst, send_sem=ssem, recv_sem=rsem, device_id=target, device_id_type=MESH
        )

    def arrived(ref, sem):
        pltpu.make_async_copy(ref, ref, sem).wait()

    pending = []
    lane = lax.broadcasted_iota(jnp.int32, (8, 128), 1)

    def xnext(v):
        return jnp.where(lane == 127, 0.0, pltpu.roll(v, 127, 1))

    def xprev(v):
        return jnp.where(lane == 0, 0.0, pltpu.roll(v, 1, 1))

    barrier = pltpu.get_barrier_semaphore()

    def greet(target):
        pl.semaphore_signal(barrier, inc=1, device_id=target, device_id_type=MESH)

    both = yh == core
    flipped = l + 1 - 2 * (l % 2)
    far = z + 2 * core - 1
    for a, b in ((0, 1), (1, 0), (1, 1)):
        greet(dev(l, z, (yh + a) % 2, (core + b) % 2))
    combos = [(t, a, b) for t in range(2) for a in range(2) for b in range(2)][1:]
    for t, a, b in combos:
        yy = (yh + a) % 2
        greet(dev(flipped if t else l, z + b * (core - yy), yy, (core + b) % 2))
    greet(dev(l, far, 1 - core, 1 - core))
    greet(dev(l, far, yh, 1 - core))
    for k in range(1, NL // 2):
        greet(dev(l + 2 * k, z, yh, core))
    for k in range(1, Z):
        greet(dev(l, z + k, yh, core))
    pl.semaphore_wait(barrier, 11 + (NL // 2 - 1) + (Z - 1) + jnp.where(both, 2, 0))

    mine = pl.ds(pl.multiple_of(8 * l, 8), 8)
    here8 = pl.ds(pl.multiple_of(8 * l + 8, 8), 8)
    quarter = 2 * yh + core
    block_of = [(quarter + 1) % 4, (quarter + 3) % 4]
    block = [jnp.where(core == 0, block_of[0], block_of[1]), jnp.where(core == 0, block_of[1], block_of[0])]

    def holder(t, a, b):
        return dev(flipped if t else l, z + b * (core + yh - 1), (yh + a) % 2, (core + b) % 2)

    for n, (t, a, b) in enumerate(combos):
        cp = remote(density, D.at[pl.ds(2 * block[b], 2), here8, :], s_d.at[n], r_d, holder(t, a, b))
        cp.start()
        pending.append(cp.wait_send)
    pltpu.make_async_copy(density, D.at[pl.ds(2 * block[0], 2), here8, :], r_d).start()

    def l_make(n, two):
        a, b = ((1, 0), (0, 1), (1, 1))[n]
        if two:
            src, dst = labels, LAB.at[pl.ds(2 * block[b], 2)]
        else:
            src, dst = labels.at[core], LAB.at[2 * block[b] + core]
        return remote(src, dst, s_l.at[n], r_l.at[block[b]], holder(a, a, b))

    def l_each(act):
        @pl.when(both)
        def _():
            act(l_make(0, True))

        @pl.when(quarter == 1)
        def _():
            act(l_make(0, False))

        for n in (1, 2):
            @pl.when(quarter == 0)
            def _():
                act(l_make(n, False))

            @pl.when(quarter != 0)
            def _():
                act(l_make(n, True))

    l_each(lambda cp: cp.start())
    pending.append(lambda: l_each(lambda cp: cp.wait_send()))
    pltpu.make_async_copy(labels, LAB.at[pl.ds(2 * block[0], 2)], r_l.at[block[0]]).start()

    is_self = [jnp.logical_and(both, yh == 0), jnp.logical_and(both, yh == 1)]

    def f_make(k):
        return remote(
            forces.at[k], F.at[:, pl.ds(2 * core, 2)], s_f.at[0, k], r_f.at[core], dev(l, z, k, yh)
        )

    def f_far(k):
        return remote(
            forces.at[k, :, yh], F.at[:, 4], s_f.at[1, k], r_f.at[2], dev(l, z + 2 * yh - 1, k, 1 - yh)
        )

    def f_sent():
        for k in range(2):
            @pl.when(jnp.logical_not(is_self[k]))
            def _():
                f_make(k).wait_send()

        @pl.when(both)
        def _():
            for k in range(2):
                f_far(k).wait_send()

    pending.append(f_sent)
    get_weights = pltpu.make_async_copy(weights_in, weights, loc.at[0])
    get_weights.start()

    zero8 = jnp.zeros((8, 128), f32)
    for r in range(8):
        D[r, 0:8, :] = zero8
        D[r, rows + 8 : rows + 16, :] = zero8
    for r in range(6):
        V[r, 0:8, :] = zero8
        V[r, rows + 8 : rows + 16, :] = zero8
        TX[r, 0:8, :] = zero8
        GU[r, 0:8, :] = zero8
        for k in range(2):
            for c in range(3):
                XA[k][c, r, rows : rows + 8, :] = zero8
                XD[k][c, r, rows : rows + 8, :] = zero8
    for k in range(4):
        for t in range(3):
            DS[k, 8 * t : 8 * t + 8, :] = zero8
    for c in range(NL):
        for k in range(2):
            MS[c, k, 2] = zero8

    own16 = l // 2

    def strip(x):
        return D.at[:, pl.ds(pl.multiple_of(16 * x + 8, 8), 16), :]

    arrived(strip(own16), r_d)
    for k in range(1, NL // 2):
        cp = remote(strip(own16), strip(own16), s_e.at[k - 1], r_e.at[k - 1], dev(l + 2 * k, z, yh, core))
        cp.start()
        pending.append(cp.wait_send)
    for k in range(2):
        @pl.when(is_self[k])
        def _():
            pltpu.make_async_copy(forces.at[k], F.at[:, pl.ds(2 * core, 2)], r_f.at[core]).start()

        @pl.when(jnp.logical_not(is_self[k]))
        def _():
            f_make(k).start()

    @pl.when(both)
    def _():
        for k in range(2):
            f_far(k).start()

    for k in range(1, NL // 2):
        arrived(strip(lax.rem(own16 + NL // 2 - k, NL // 2)), r_e.at[k - 1])

    @pl.when(jnp.logical_or(core == 0, yh == 0))
    def _():
        arrived(LAB.at[0:2], r_l.at[0])

    @pl.when(quarter == 3)
    def _():
        arrived(LAB.at[1], r_l.at[0])

    for b in (1, 2):
        arrived(LAB.at[2 * b : 2 * b + 2], r_l.at[b])

    @pl.when(core == 1)
    def _():
        arrived(LAB.at[6], r_l.at[3])

    @pl.when(quarter == 2)
    def _():
        arrived(LAB.at[6:8], r_l.at[3])

    sibling = dev(l, z, yh, 1 - core)

    sgn = 2 * core - 1

    def inside(p):
        at = 8 * z + p
        return jnp.logical_and(at >= 0, at < 8 * Z)

    def moduli_layer(m, _):
        p = 3 + sgn * m
        r = p + 2 - 4 * core
        scale = jnp.where(inside(p), f32(UNIT), f32(0.0))
        for c in range(NL):
            d = D[r, 8 * c + 8 : 8 * c + 16, :]
            solid = jnp.where(LAB[r, 8 * c : 8 * c + 8, :] == 2, 1.0, d)
            e = (EMIN + (1.0 - EMIN) * solid * solid * solid) * scale
            EM[m, 8 * c : 8 * c + 8, :] = e
            TX[m, 8 * c + 8 : 8 * c + 16, :] = e + xprev(e)
        return 0

    lax.fori_loop(0, 6, moduli_layer, 0)

    def inverse_layer(m, _):
        p = jnp.where(core == 1, 3 + m, 4 - m)
        r = p + 2 - 4 * core
        keep = jnp.where(inside(p), 1, 0)
        for c in range(NL):
            near = TX[m, 8 * c + 8 : 8 * c + 16, :] + TX[m, 8 * c + 7 : 8 * c + 15, :]
            back = TX[m - 1, 8 * c + 8 : 8 * c + 16, :] + TX[m - 1, 8 * c + 7 : 8 * c + 15, :]
            lab = LAB[r, 8 * c : 8 * c + 8, :] * keep + (1 - keep)
            INVD[m, 8 * c : 8 * c + 8, :] = jnp.where(lab != 1, (UNIT / DIAG) / (near + back), 0.0)
        return 0

    lax.fori_loop(1, 6, inverse_layer, 0)

    def plane_sums(center, above, below):
        ysum = above + below
        xsum = xnext(center) + xprev(center)
        cross = ysum + xsum
        corner = xnext(ysum) + xprev(ysum)
        return 1.5 * center + 0.5 * cross + EDGE * corner, 0.5 * center + EDGE * cross

    def d_plane(r, _):
        scale = jnp.where(inside(r - 2 + 4 * core), f32(1.0), f32(0.0))
        for c in range(NL):
            a, b = plane_sums(
                D[r, 8 * c + 8 : 8 * c + 16, :], D[r, 8 * c + 7 : 8 * c + 15, :], D[r, 8 * c + 9 : 8 * c + 17, :]
            )
            PA[r, 8 * c : 8 * c + 8, :] = a * scale
            PB[r, 8 * c : 8 * c + 8, :] = b * scale
        return 0

    def v_plane(r, _):
        ok = jnp.where(inside(r - 2 + 4 * core), f32(1.0), f32(0.0))
        for c in range(NL):
            at = slice(8 * c, 8 * c + 8)
            total = PA[r, at, :] + PB[r - 1, at, :] + PB[r + 1, at, :]
            V[r - 1, 8 * c + 8 : 8 * c + 16, :] = ok / (total + (1.0 - ok))
        return 0

    def v_make():
        return remote(V.at[pl.ds(3 - 2 * core, 2), here8, :], VO, s_v, r_v, sibling)

    def v_sent():
        @pl.when(both)
        def _():
            v_make().wait_send()

    def w_plane(n, _):
        for c in range(NL):
            a, b = plane_sums(
                V[n, 8 * c + 8 : 8 * c + 16, :], V[n, 8 * c + 7 : 8 * c + 15, :], V[n, 8 * c + 9 : 8 * c + 17, :]
            )
            PA[n, 8 * c : 8 * c + 8, :] = a
            PB[n, 8 * c : 8 * c + 8, :] = b
        return 0

    def g_plane(k, _):
        r = k + 2
        for c in range(NL):
            at = slice(8 * c, 8 * c + 8)
            d = D[r, 8 * c + 8 : 8 * c + 16, :]
            solid = jnp.where(LAB[r, at, :] == 2, 1.0, d)
            G[k, at, :] = (PA[k + 1, at, :] + PB[k, at, :] + PB[k + 2, at, :]) * (d * solid * solid)
        return 0

    def filter_part(s):
        if s == 1:
            lax.fori_loop(0, 8, d_plane, 0)
            lax.fori_loop(1, 7, v_plane, 0)

            @pl.when(both)
            def _():
                v_make().start()
        elif s == 2:
            lax.fori_loop(0, 6, w_plane, 0)
            lax.fori_loop(0, 4, g_plane, 0)

    for k in range(2):
        arrived(F.at[:, 2 * k : 2 * k + 2], r_f.at[k])
    arrived(F.at[:, 4], r_f.at[2])
    flip = jnp.where(core == 1, f32(1.0), f32(-1.0))

    def x_make(par):
        return [
            remote(X[par].at[:, 1, 0:rows, :], X[par].at[:, 0, 0:rows, :], s_x.at[par, n], r_x.at[par, n], sibling)
            for n, X in enumerate((XA, XD))
        ]

    def first_step(m, _):
        i = jnp.where(jnp.logical_or(core == 1, m == 5), m - 1, 4 - m)
        for c in range(NL):
            at = slice(8 * c, 8 * c + 8)
            inv = INVD[m, at, :]
            for comp in range(3):
                f = F[comp, i, at, :]
                if comp == 2:
                    f = f * flip
                R[comp, m, at, :] = f
                s = inv * f * (1.0 / THETA)
                STEP[comp, m, at, :] = s
                SOL[comp, m, at, :] = s
                n = xnext(s)
                XA[0][comp, m, at, :] = s + n
                XD[0][comp, m, at, :] = n - s

        @pl.when(m == 1)
        def _():
            for cp in x_make(0):
                cp.start()

        return 0

    lax.fori_loop(1, 6, first_step, 0)

    def fields(par, comp, m, c):
        a0 = XA[par][comp, m, 8 * c : 8 * c + 8, :]
        a1 = XA[par][comp, m, 8 * c + 1 : 8 * c + 9, :]
        d0 = XD[par][comp, m, 8 * c : 8 * c + 8, :]
        d1 = XD[par][comp, m, 8 * c + 1 : 8 * c + 9, :]
        return a0 + a1, a1 - a0, d0 + d1, d1 - d0

    def modes(par, m, c):
        out = []
        for comp in range(3):
            lo = fields(par, comp, m, c)
            hi = fields(par, comp, m + 1, c)
            out.append(
                dict(
                    z=hi[0] - lo[0], y=hi[1] + lo[1], yz=hi[1] - lo[1], x=hi[2] + lo[2], zx=hi[2] - lo[2],
                    xy=hi[3] + lo[3], xyz=hi[3] - lo[3],
                )
            )
        return out

    def ghost(par):
        for n, X in enumerate((XA, XD)):
            arrived(X[par].at[:, 0, 0:rows, :], r_x.at[par, n])
            for c in range(NL):
                X[par][2, 0, 8 * c : 8 * c + 8, :] = -X[par][2, 0, 8 * c : 8 * c + 8, :]

    there = jnp.where(inside(jnp.where(core == 1, 8, -1)), f32(1.0), f32(0.0))

    def z_make(par):
        return remote(ZS.at[par], ZG.at[par], s_z.at[par], r_z.at[par], dev(l, far, yh, 1 - core))

    def far_ghost(par):
        arrived(ZG.at[par], r_z.at[par])
        for comp in range(3):
            scale = -there if comp == 2 else there
            for c in range(NL):
                at = slice(8 * c, 8 * c + 8)
                v = ZG[par, comp, at, :] * scale
                n = xnext(v)
                XA[par][comp, 5, at, :] = v + n
                XD[par][comp, 5, at, :] = n - v

    def lay_out(half):
        for n in range(2):
            k = 2 * half + n
            m = jnp.where(core == 1, k + 1, 4 - k)
            for c in range(NL):
                at = slice(8 * c, 8 * c + 8)
                for comp in range(3):
                    v = SOL[comp, m, at, :]
                    OUT[comp, k, at, :] = v * flip if comp == 2 else v

    def o_make(half):
        return remote(
            OUT.at[:, pl.ds(2 * half, 2)], disp.at[yh], s_o.at[half], r_o.at[yh], dev(l, z, core, half)
        )

    coefs = chebyshev()

    def element_forces(par, m, c):
        u, v, w = modes(par, m, c)
        e = EM[m, 8 * c : 8 * c + 8, :]
        e2, e3, eq = e + e, e * (1.0 / 3.0), e * ((RATIO + 4.0) / 9.0)
        tr = (0.5 * RATIO) * (u["x"] + v["y"] + w["z"])
        fx = e2 * (tr + u["x"])
        fy = e2 * (tr + v["y"])
        fz = e2 * (tr + w["z"])
        sxy = e * (u["y"] + v["x"])
        syz = e * (v["z"] + w["y"])
        szx = e * (u["z"] + w["x"])
        h = 0.5 * (v["xy"] + w["zx"])
        vxy, wzx = e * (v["xy"] + h), e * (w["zx"] + h)
        h = 0.5 * (u["xy"] + w["yz"])
        uxy, wyz = e * (u["xy"] + h), e * (w["yz"] + h)
        h = 0.5 * (u["zx"] + v["yz"])
        uzx, vyz = e * (u["zx"] + h), e * (v["yz"] + h)
        h = u["yz"] + v["zx"] + w["xy"]
        uyz, vzx, wxy = e3 * (u["yz"] + h), e3 * (v["zx"] + h), e3 * (w["xy"] + h)
        uq, vq, wq = eq * u["xyz"], eq * v["xyz"], eq * w["xyz"]
        return (
            (szx, sxy, uyz, fx, uzx, uxy, uq),
            (syz, fy, vyz, sxy, vzx, vxy, vq),
            (fz, syz, wyz, szx, wzx, wxy, wq),
        )

    def push_up(comp, at, force):
        gz_, gy, gyz, gx, gzx, gxy, gxyz = force
        UP[4 * comp, at, :] = gz_
        UP[4 * comp + 1, at, :] = gy + gyz
        UP[4 * comp + 2, at, :] = gx + gzx
        UP[4 * comp + 3, at, :] = gxy + gxyz

    def sweep(s):
        par = s % 2
        nxt = 1 - par
        c1, c2 = coefs[s]
        ghost(par)
        for c in range(NL):
            at = slice(8 * c, 8 * c + 8)
            for comp, force in enumerate(element_forces(par, 0, c)):
                push_up(comp, at, force)

        def layer(m, _):
            if s > 0:
                @pl.when(m == 4)
                def _():
                    if s == SWEEPS - 1:
                        lay_out(1 - core)
                        o_make(1 - core).start()
                    filter_part(s)
                    far_ghost(par)

            for c in range(NL):
                at = slice(8 * c, 8 * c + 8)
                inv = INVD[m, at, :]
                for comp, force in enumerate(element_forces(par, m, c)):
                    gz_, gy, gyz, gx, gzx, gxy, gxyz = force
                    taa = UP[4 * comp, at, :] - gz_
                    tay = UP[4 * comp + 1, at, :] + (gy - gyz)
                    tda = UP[4 * comp + 2, at, :] + (gx - gzx)
                    tdy = UP[4 * comp + 3, at, :] + (gxy - gxyz)
                    push_up(comp, at, force)
                    GU[2 * comp, 8 * c + 8 : 8 * c + 16, :] = taa + tay
                    GU[2 * comp + 1, 8 * c + 8 : 8 * c + 16, :] = tda + tdy
                    a = (taa - tay) + GU[2 * comp, 8 * c + 7 : 8 * c + 15, :]
                    b = (tda - tdy) + GU[2 * comp + 1, 8 * c + 7 : 8 * c + 15, :]
                    pushed = (a - b) + xprev(a + b)
                    res = R[comp, m, at, :] - pushed
                    R[comp, m, at, :] = res
                    step = c1 * STEP[comp, m, at, :] + c2 * (inv * res)
                    STEP[comp, m, at, :] = step
                    sent = SOL[comp, m, at, :] + step
                    SOL[comp, m, at, :] = sent
                    if s < SWEEPS - 1:
                        sent = step
                    n = xnext(sent)
                    XA[nxt][comp, m, at, :] = sent + n
                    XD[nxt][comp, m, at, :] = n - sent

            @pl.when(m == 1)
            def _():
                for cp in x_make(par):
                    cp.wait_send()
                for cp in x_make(nxt):
                    cp.start()

            @pl.when(m == 4)
            def _():
                if s > 0:
                    z_make(par).wait_send()
                for comp in range(3):
                    for c in range(NL):
                        at = slice(8 * c, 8 * c + 8)
                        ZS[nxt, comp, at, :] = (STEP if s < SWEEPS - 1 else SOL)[comp, 4, at, :]
                if s < SWEEPS - 1:
                    z_make(nxt).start()
                else:
                    @pl.when(core == 0)
                    def _():
                        z_make(nxt).start()

            return 0

        lax.fori_loop(1, 5, layer, 0)

    for s in range(SWEEPS):
        sweep(s)

    @pl.when(both)
    def _():
        lay_out(core)
        pltpu.make_async_copy(OUT.at[:, pl.ds(2 * core, 2)], disp.at[yh], r_o.at[yh]).start()

    @pl.when(jnp.logical_not(both))
    def _():
        lay_out(core)
        o_make(core).start()

    def o_ended():
        o_make(1 - core).wait_send()

        @pl.when(jnp.logical_not(both))
        def _():
            o_make(core).wait_send()

        for k in range(2):
            arrived(disp.at[k], r_o.at[k])

    pending.append(o_ended)

    fin = SWEEPS % 2
    get_weights.wait()
    pending.extend(cp.wait_send for cp in x_make(fin))
    pending.append(v_sent)

    def z_sent():
        @pl.when(core == 0)
        def _():
            z_make(fin).wait_send()

    pending.append(z_sent)
    weight = weights[2 * l + yh].astype(f32)
    weight_sum = weights[0]
    for n in range(1, 2 * NL):
        weight_sum = weight_sum + weights[n]
    weight_sum = weight_sum.astype(f32)

    def energy_layer(k, share):
        m = jnp.where(core == 1, k + 1, 3 - k)
        for c in range(NL):
            u, v, w = modes(fin, m, c)
            tr = u["x"] + v["y"] + w["z"]
            sq = lambda t: t * t
            normal = sq(u["x"]) + sq(v["y"]) + sq(w["z"])
            shear = sq(u["y"] + v["x"]) + sq(v["z"] + w["y"]) + sq(u["z"] + w["x"])
            pairs = (
                sq(v["xy"]) + sq(w["zx"]) + sq(u["xy"]) + sq(w["yz"]) + sq(u["zx"]) + sq(v["yz"])
            )
            joint = sq(v["xy"] + w["zx"]) + sq(u["xy"] + w["yz"]) + sq(u["zx"] + v["yz"])
            s = u["yz"] + v["zx"] + w["xy"]
            triple = sq(u["yz"]) + sq(v["zx"]) + sq(w["xy"]) + sq(s)
            quad = sq(u["xyz"]) + sq(v["xyz"]) + sq(w["xyz"])
            total = (
                (RATIO * sq(tr) + 2.0 * normal + shear) + (pairs + 0.5 * joint)
                + (1.0 / 3.0) * triple + ((RATIO + 4.0) / 9.0) * quad
            )
            t = (weight * UNIT) * total
            half, j = k // 2, k % 2
            MS[c, half, j] = t
            if c > 0:
                MS[c - 1, half, 2, pl.ds(2 * j + 1, 1), :] = t[0:1, :]
            if c < NL - 1:
                MS[c + 1, half, 2, pl.ds(2 * j, 1), :] = t[7:8, :]
            share = share + t * G[k, 8 * c : 8 * c + 8, :]
        return share

    def last_layer(k, got):
        @pl.when(k == 3)
        def _():
            ghost(fin)

            @pl.when(core == 1)
            def _():
                far_ghost(fin)

        return energy_layer(k, got)

    share = lax.fori_loop(0, 4, last_layer, zero8)
    share = jnp.sum(share, axis=0, keepdims=True)
    for c in range(NL):
        for k in range(2):
            MS[c, k, 2, 4:5, :] = share

    me = 2 * l + yh
    m_copies = []
    def m_make(k, cc):
        ll = lax.rem(l + k, NL)
        return remote(MS.at[ll, cc], RX.at[me], s_m.at[k, cc], r_m, dev(ll, z, core, cc))

    for k in range(NL):
        for cc in range(2):
            if k > 0:
                m_make(k, cc).start()
            else:
                alone = jnp.logical_and(both, core == cc)

                @pl.when(alone)
                def _():
                    pltpu.make_async_copy(MS.at[l, cc], RX.at[me], r_m).start()

                @pl.when(jnp.logical_not(alone))
                def _():
                    m_make(k, cc).start()

    def m_sent():
        for k in range(NL):
            for cc in range(2):
                if k > 0:
                    m_make(k, cc).wait_send()
                else:
                    @pl.when(jnp.logical_not(jnp.logical_and(both, core == cc)))
                    def _():
                        m_make(k, cc).wait_send()

    pending.append(m_sent)

    arrived(RX, r_m)
    scale = (3.0 * (1.0 - EMIN)) / weight_sum
    sums = []
    for k in range(3):
        part = RX[0, k]
        for n in range(1, 2 * NL):
            part = part + RX[n, k]
        sums.append(part)
    rim = sums[2]
    SV[...] = rim[4:5, :]

    def s_make(kz, ky):
        return remote(SV, RX2.at[2 * z + yh], s_s.at[kz, ky], r_s, dev(l, z + kz, (yh + ky) % 2, core))

    for kz in range(Z):
        for ky in range(2):
            if (kz, ky) != (0, 0):
                s_make(kz, ky).start()
    pltpu.make_async_copy(SV, RX2.at[2 * z + yh], r_s).start()

    def s_sent():
        for kz in range(Z):
            for ky in range(2):
                if (kz, ky) != (0, 0):
                    s_make(kz, ky).wait_send()

    pending.append(s_sent)
    native = 4 * yh + 2 * (1 - core)
    for k in range(2):
        main = sums[k]
        rated = []
        for n in range(3):
            near = pl.ds(pl.multiple_of(8 * l + 8 * n, 8), 8)
            d = D[native + k, near, :]
            row = jnp.clip(8 * l + 8 * (n - 1), 0, rows - 8)
            lab = LAB[native + k, pl.ds(pl.multiple_of(row, 8), 8), :]
            solid = jnp.where(lab == 2, 1.0, d)
            rated.append(d * solid * solid * scale)
        above = jnp.where(l > 0, f32(1.0), f32(0.0)) * rated[0][7:8, :]
        below = jnp.where(l < NL - 1, f32(1.0), f32(0.0)) * rated[2][0:1, :]
        DS[k + 1, 8:16, :] = main * rated[1]
        DS[k + 1, 7:8, :] = rim[2 * k : 2 * k + 1, :] * above
        DS[k + 1, 16:17, :] = rim[2 * k + 1 : 2 * k + 2, :] * below

    def h_make(up):
        to = lax.rem(g + (1 if up else 4 * Z - 1), 4 * Z)
        return remote(DS.at[2 if up else 1], DS.at[0 if up else 3], s_h.at[int(up)], r_h.at[int(up)], (l, to))

    for up in (False, True):
        h_make(up).start()
        pending.append(h_make(up).wait_send)
    arrived(DS.at[3], r_h.at[0])
    arrived(DS.at[0], r_h.at[1])

    planes = []
    for k in range(4):
        planes.append(plane_sums(DS[k, 8:16, :], DS[k, 7:15, :], DS[k, 9:17, :]))
    low = jnp.where(g > 0, f32(1.0), f32(0.0)) * planes[0][1]
    high = jnp.where(g < 4 * Z - 1, f32(1.0), f32(0.0)) * planes[3][1]
    numer = [planes[1][0] + low + planes[2][1], planes[2][0] + planes[1][1] + high]
    @pl.when(both)
    def _():
        for k in range(2):
            VO[k] = V[1 + 2 * core + k, here8, :]

    @pl.when(jnp.logical_not(both))
    def _():
        arrived(VO, r_v)

    arrived(RX2, r_s)
    total = RX2[0]
    for n in range(1, 2 * Z):
        total = total + RX2[n]
    mean = jnp.sum(total, axis=1, keepdims=True) * scale / (8 * Z * rows * 128)
    for k in range(2):
        filtered = numer[k] * VO[k]
        d = D[native + k, here8, :]
        candidate = d * jnp.sqrt(filtered / mean)
        lower = jnp.maximum(d - MOVE_LIMIT, FLOOR_DENSITY)
        upper = jnp.minimum(d + MOVE_LIMIT, 1.0)
        new = jnp.minimum(jnp.maximum(candidate, lower), upper)
        newd[k] = jnp.where(LAB[native + k, mine, :] == 2, 1.0, new)

    for end in pending:
        end()


def solution(mesh):
    NL, Z = mesh.shape["load"], mesh.shape["gz"] // 4
    rows = 8 * NL

    def on_device(density, labels, forces, case_weights):
        vm = lambda *shape: pltpu.VMEM(shape, jnp.float32)
        dma = lambda *shape: pltpu.SemaphoreType.DMA(shape)
        scratch = [
            vm(3, 5, rows, 128),
            pltpu.VMEM((8, rows, 128), jnp.int32),
            vm(8, rows + 16, 128),
            vm(6, rows, 128),
            vm(6, rows + 8, 128),
            vm(6, rows, 128),
            vm(3, 6, rows, 128),
            vm(3, 6, rows, 128),
            vm(3, 6, rows, 128),
            vm(3, 6, rows + 8, 128),
            vm(3, 6, rows + 8, 128),
            vm(3, 6, rows + 8, 128),
            vm(3, 6, rows + 8, 128),
            vm(12, rows, 128),
            vm(6, rows + 8, 128),
            vm(3, 4, rows, 128),
            vm(2, 3, rows, 128),
            vm(2, 3, rows, 128),
            vm(8, rows, 128),
            vm(8, rows, 128),
            vm(6, rows + 16, 128),
            vm(2, 8, 128),
            vm(4, rows, 128),
            vm(NL, 2, 3, 8, 128),
            vm(2 * NL, 3, 8, 128),
            vm(4, 24, 128),
            vm(1, 128),
            vm(2 * Z, 1, 128),
            pltpu.SMEM((2 * NL,), jnp.int32),
            vm(46 << 11, 128),
            dma(7), pltpu.SemaphoreType.DMA,
            dma(NL // 2), dma(NL // 2),
            dma(2, 2), dma(3),
            dma(3), dma(4),
            pltpu.SemaphoreType.DMA, pltpu.SemaphoreType.DMA,
            dma(2, 2), dma(2, 2),
            dma(2), dma(2),
            dma(2), dma(2),
            dma(NL, 2), pltpu.SemaphoreType.DMA,
            dma(2), dma(2),
            dma(Z, 2), pltpu.SemaphoreType.DMA,
            dma(1),
        ]
        return pl.pallas_call(
            functools.partial(kernel, NL, Z),
            out_shape=(
                pltpu.VMEM(density.shape, jnp.float32),
                pltpu.VMEM(forces.shape, jnp.float32),
            ),
            in_specs=[pl.BlockSpec(memory_space=pltpu.HBM)] * 4,
            out_specs=(pl.BlockSpec(memory_space=pltpu.VMEM), pl.BlockSpec(memory_space=pltpu.VMEM)),
            scratch_shapes=scratch,
            compiler_params=pltpu.CompilerParams(
                collective_id=1, has_side_effects=True, vmem_limit_bytes=60 << 20
            ),
            name="step",
        )(density, labels, forces, case_weights)

    return jax.shard_map(
        on_device,
        mesh=mesh,
        in_specs=(
            P("gz", "load", None),
            P("gz", None, None),
            P("load", None, "gz", None, None),
            P(),
        ),
        out_specs=(P("gz", "load", None), P("load", None, "gz", None, None)),
        check_vma=False,
    )
```

```python
import functools

import jax
import jax.numpy as jnp
import numpy as np
from jax import lax
from jax.experimental import pallas as pl
from jax.experimental.pallas import tpu as pltpu
from jax.sharding import PartitionSpec as P

MESH = pl.DeviceIdType.MESH
SWEEPS = 3
EMIN = 0.001
LOWER_EIG = 0.1
UPPER_EIG = 2.5
MOVE_LIMIT = 0.2
FLOOR_DENSITY = 0.001
THETA = 0.5 * (UPPER_EIG + LOWER_EIG)
DELTA = 0.5 * (UPPER_EIG - LOWER_EIG)
POISSON = 0.3
SHEAR = 1.0 / (2 * (1 + POISSON))
RATIO = 2 * POISSON / (1 - 2 * POISSON)
UNIT = SHEAR / 16.0
DIAG = UNIT * ((RATIO + 4.0) + (2.0 * (RATIO + 3.0) + 2.0) / 3.0 + (RATIO + 4.0) / 9.0)
EDGE = 1.5 - float(np.sqrt(2.0))


def chebyshev():
    sigma = THETA / DELTA
    factor = 1.0 / sigma
    pairs = []
    for _ in range(SWEEPS):
        following = 1.0 / (2.0 * sigma - factor)
        pairs.append((following * factor, 2.0 * following / DELTA))
        factor = following
    return pairs


def kernel(
    NL, Z, density_in, labels_in, forces_in, weights_in, newd, disp,
    density, labels, forces, F, LAB, D, EM, TX, INVD, R, STEP, SOL, XA0, XA1, XD0, XD1, UP, GU, GV, KU, OUT, ZS, ZG,
    PA, PB, V, VO, G, MS, RX, DS, SV, RX2, weights, spare,
    s_d, r_d, s_e, r_e, s_f, r_f, s_l, r_l, s_y, r_y, s_w, r_w, s_i, r_i, s_v, r_v, s_x, r_x, s_z, r_z,
    s_o, r_o, s_m, r_m, s_h, r_h, s_s, r_s, loc,
):
    rows = 8 * NL
    f32 = jnp.float32
    XA, XD = (XA0, XA1), (XD0, XD1)
    l = lax.axis_index("load")
    g = lax.axis_index("gz")
    core = g % 2
    yh = (g // 2) % 2
    z = g // 4

    def dev(ll, zz, yy, cc):
        return (lax.rem(ll + NL, NL), (lax.rem(zz + Z, Z) * 2 + yy) * 2 + cc)

    def remote(src, dst, ssem, rsem, target):
        return pltpu.make_async_remote_copy(
            src_ref=src, dst_ref=dst, send_sem=ssem, recv_sem=rsem, device_id=target, device_id_type=MESH
        )

    def arrived(ref, sem):
        pltpu.make_async_copy(ref, ref, sem).wait()

    pending = []

    def far_first(count):
        return sorted(range(count), key=lambda k: -min(k, count - k))

    lane = lax.broadcasted_iota(jnp.int32, (8, 128), 1)

    def xnext(v):
        return jnp.where(lane == 127, 0.0, pltpu.roll(v, 127, 1))

    def xprev(v):
        return jnp.where(lane == 0, 0.0, pltpu.roll(v, 1, 1))

    staged = [
        pltpu.make_async_copy(given, here, loc.at[n])
        for n, (given, here) in enumerate(
            ((density_in, density), (labels_in, labels), (forces_in, forces), (weights_in, weights))
        )
    ]
    for cp in staged:
        cp.start()
    barrier = pltpu.get_barrier_semaphore()

    def greet(target):
        pl.semaphore_signal(barrier, inc=1, device_id=target, device_id_type=MESH)

    both = yh == core
    far = z + 2 * core - 1
    sibling = dev(l, z, yh, 1 - core)
    is_self = [jnp.logical_and(both, yh == 0), jnp.logical_and(both, yh == 1)]

    for k in range(NL):
        for cc in range(2):
            if k > 0:
                greet(dev(l + k, z, core, cc))
            else:
                @pl.when(jnp.logical_not(jnp.logical_and(both, core == cc)))
                def _():
                    greet(dev(l, z, core, cc))
    greet(sibling)
    greet(dev(l, far, yh, 1 - core))
    for k in range(1, Z):
        greet(dev(l, z + k, yh, core))
    pl.semaphore_wait(barrier, 2 * NL + 2 + (Z - 1) - jnp.where(both, 1, 0))

    for cp in staged:
        cp.wait()

    mine = pl.ds(pl.multiple_of(8 * l, 8), 8)
    here8 = pl.ds(pl.multiple_of(8 * l + 8, 8), 8)
    two = pl.ds(2 * core + 2, 2)

    def d_make(n, k):
        return remote(density, D.at[two, here8, :], s_d.at[n, k], r_d, dev(l + n, z, k, yh))

    def l_make(k):
        return remote(labels, LAB.at[two], s_l.at[k], r_l.at[core], dev(l, z, k, yh))

    def f_make(k):
        return remote(forces.at[k], F.at[:, pl.ds(2 * core, 2)], s_f.at[k], r_f.at[core], dev(l, z, k, yh))

    for n in far_first(NL)[:-1]:
        for k in range(2):
            cp = d_make(n, k)
            cp.start()
            pending.append(cp.wait_send)
    for k in range(2):
        @pl.when(is_self[k])
        def _():
            pltpu.make_async_copy(density, D.at[two, here8, :], r_d).start()
            pltpu.make_async_copy(labels, LAB.at[two], r_l.at[core]).start()
            pltpu.make_async_copy(forces.at[k], F.at[:, pl.ds(2 * core, 2)], r_f.at[core]).start()

        @pl.when(jnp.logical_not(is_self[k]))
        def _():
            d_make(0, k).start()
            l_make(k).start()
            f_make(k).start()

    def native_sent():
        for k in range(2):
            @pl.when(jnp.logical_not(is_self[k]))
            def _():
                d_make(0, k).wait_send()
                l_make(k).wait_send()
                f_make(k).wait_send()

    pending.append(native_sent)
    zero8 = jnp.zeros((8, 128), f32)
    for r in range(8):
        D[r, 0:8, :] = zero8
        D[r, rows + 8 : rows + 16, :] = zero8
    for r in range(6):
        V[r, 0:8, :] = zero8
        V[r, rows + 8 : rows + 16, :] = zero8
        TX[r, 0:8, :] = zero8
        GU[r, 0:8, :] = zero8
        GV[r, 0:8, :] = zero8
        for k in range(2):
            for c in range(3):
                XA[k][c, r, rows : rows + 8, :] = zero8
                XD[k][c, r, rows : rows + 8, :] = zero8
    for k in range(4):
        for t in range(3):
            DS[k, 8 * t : 8 * t + 8, :] = zero8
    for c in range(NL):
        for k in range(2):
            MS[c, k, 2] = zero8

    arrived(D.at[2:6, 8 : rows + 8, :], r_d)
    for k in range(2):
        arrived(LAB.at[2 + 2 * k : 4 + 2 * k], r_l.at[k])

    src2, dst2 = pl.ds(4 - 2 * core, 2), pl.ds(6 * core, 2)
    got2 = pl.ds(6 * (1 - core), 2)
    relays = [
        remote(LAB.at[src2], LAB.at[pl.ds(6 * core, 2)], s_y.at[0], r_y.at[0], sibling),
        remote(D.at[src2, 8 : rows + 8, :], D.at[dst2, 8 : rows + 8, :], s_y.at[1], r_y.at[1], sibling),
    ]
    for cp in relays:
        cp.start()
        pending.append(cp.wait_send)

    sgn = 2 * core - 1

    def inside(p):
        at = 8 * z + p
        return jnp.logical_and(at >= 0, at < 8 * Z)

    def moduli_layer(m, _):
        p = 3 + sgn * m
        r = p + 2 - 4 * core
        scale = jnp.where(inside(p), f32(UNIT), f32(0.0))
        for c in range(NL):
            d = D[r, 8 * c + 8 : 8 * c + 16, :]
            solid = jnp.where(LAB[r, 8 * c : 8 * c + 8, :] == 2, 1.0, d)
            e = (EMIN + (1.0 - EMIN) * solid * solid * solid) * scale
            EM[m, 8 * c : 8 * c + 8, :] = e
            TX[m, 8 * c + 8 : 8 * c + 16, :] = e + xprev(e)
        return 0

    lax.fori_loop(core, core + 4, moduli_layer, 0)

    def e_make():
        return remote(EM.at[4], EM.at[4], s_e, r_e, dev(l, far, yh, 1 - core))

    @pl.when(core == 1)
    def _():
        e_make().start()

    def e_sent():
        @pl.when(core == 1)
        def _():
            e_make().wait_send()

    pending.append(e_sent)

    def w_make():
        return remote(
            D.at[pl.ds(2 + 2 * core, 2), 8 : rows + 8, :],
            D.at[pl.ds(6 * (1 - core), 2), 8 : rows + 8, :],
            s_w, r_w, dev(l, far, yh, 1 - core),
        )

    w_make().start()
    pending.append(w_make().wait_send)
    arrived(LAB.at[pl.ds(6 * (1 - core), 2)], r_y.at[0])
    arrived(D.at[got2, 8 : rows + 8, :], r_y.at[1])

    @pl.when(core == 1)
    def _():
        moduli_layer(0, 0)

    def inverse_layer(m, _):
        p = jnp.where(core == 1, 3 + m, 4 - m)
        r = p + 2 - 4 * core
        keep = jnp.where(inside(p), 1, 0)
        for c in range(NL):
            near = TX[m, 8 * c + 8 : 8 * c + 16, :] + TX[m, 8 * c + 7 : 8 * c + 15, :]
            back = TX[m - 1, 8 * c + 8 : 8 * c + 16, :] + TX[m - 1, 8 * c + 7 : 8 * c + 15, :]
            lab = LAB[r, 8 * c : 8 * c + 8, :] * keep + (1 - keep)
            INVD[m, 8 * c : 8 * c + 8, :] = jnp.where(lab != 1, (UNIT / DIAG) / (near + back), 0.0)
        return 0

    lax.fori_loop(1, 4, inverse_layer, 0)

    @pl.when(core == 0)
    def _():
        arrived(EM.at[4], r_e)
        known = jnp.where(inside(-1), f32(1.0), f32(0.0))
        for c in range(NL):
            e = EM[4, 8 * c : 8 * c + 8, :] * known
            EM[4, 8 * c : 8 * c + 8, :] = e
            TX[4, 8 * c + 8 : 8 * c + 16, :] = e + xprev(e)

    inverse_layer(4, 0)

    give_inverse = remote(INVD.at[4], INVD.at[5], s_i, r_i, dev(l, far, yh, 1 - core))
    give_inverse.start()
    pending.append(give_inverse.wait_send)

    def plane_sums(center, above, below):
        ysum = above + below
        xsum = xnext(center) + xprev(center)
        cross = ysum + xsum
        corner = xnext(ysum) + xprev(ysum)
        return 1.5 * center + 0.5 * cross + EDGE * corner, 0.5 * center + EDGE * cross

    def d_plane(r, _):
        scale = jnp.where(inside(r - 2 + 4 * core), f32(1.0), f32(0.0))
        for c in range(NL):
            a, b = plane_sums(
                D[r, 8 * c + 8 : 8 * c + 16, :], D[r, 8 * c + 7 : 8 * c + 15, :], D[r, 8 * c + 9 : 8 * c + 17, :]
            )
            PA[r, 8 * c : 8 * c + 8, :] = a * scale
            PB[r, 8 * c : 8 * c + 8, :] = b * scale
        return 0

    def v_plane(r, _):
        ok = jnp.where(inside(r - 2 + 4 * core), f32(1.0), f32(0.0))
        for c in range(NL):
            at = slice(8 * c, 8 * c + 8)
            total = PA[r, at, :] + PB[r - 1, at, :] + PB[r + 1, at, :]
            V[r - 1, 8 * c + 8 : 8 * c + 16, :] = ok / (total + (1.0 - ok))
        return 0

    def v_make():
        return remote(V.at[pl.ds(3 - 2 * core, 2), here8, :], VO, s_v, r_v, sibling)

    def v_sent():
        @pl.when(both)
        def _():
            v_make().wait_send()

    def w_plane(n, _):
        for c in range(NL):
            a, b = plane_sums(
                V[n, 8 * c + 8 : 8 * c + 16, :], V[n, 8 * c + 7 : 8 * c + 15, :], V[n, 8 * c + 9 : 8 * c + 17, :]
            )
            PA[n, 8 * c : 8 * c + 8, :] = a
            PB[n, 8 * c : 8 * c + 8, :] = b
        return 0

    def g_plane(k, _):
        r = k + 2
        for c in range(NL):
            at = slice(8 * c, 8 * c + 8)
            d = D[r, 8 * c + 8 : 8 * c + 16, :]
            solid = jnp.where(LAB[r, at, :] == 2, 1.0, d)
            G[k, at, :] = (PA[k + 1, at, :] + PB[k, at, :] + PB[k + 2, at, :]) * (d * solid * solid)
        return 0

    def filter_part(s):
        if s == 0:
            arrived(D.at[pl.ds(6 * core, 2), 8 : rows + 8, :], r_w)
            lax.fori_loop(0, 8, d_plane, 0)
            lax.fori_loop(1, 7, v_plane, 0)

            @pl.when(both)
            def _():
                v_make().start()
        elif s == 2:
            lax.fori_loop(0, 6, w_plane, 0)
            lax.fori_loop(0, 4, g_plane, 0)

    for k in range(2):
        arrived(F.at[:, 2 * k : 2 * k + 2], r_f.at[k])
    flip = jnp.where(core == 1, f32(1.0), f32(-1.0))

    def x_make(par):
        return [
            remote(X[par].at[:, 1, 0:rows, :], X[par].at[:, 0, 0:rows, :], s_x.at[par, n], r_x.at[par, n], sibling)
            for n, X in enumerate((XA, XD))
        ]

    def z_make(n):
        return remote(ZS.at[n], ZG.at[n], s_z.at[n], r_z.at[n], dev(l, far, yh, 1 - core))

    def first_step(m, _):
        i = jnp.where(core == 1, m - 1, 4 - m)
        for c in range(NL):
            at = slice(8 * c, 8 * c + 8)
            inv = INVD[m, at, :]
            for comp in range(3):
                f = F[comp, i, at, :]
                if comp == 2:
                    f = f * flip
                R[comp, m, at, :] = f
                s = inv * f * (1.0 / THETA)
                STEP[comp, m, at, :] = s
                SOL[comp, m, at, :] = s
                n = xnext(s)
                XA[0][comp, m, at, :] = s + n
                XD[0][comp, m, at, :] = n - s

        @pl.when(m == 1)
        def _():
            for cp in x_make(0):
                cp.start()

        @pl.when(m == 4)
        def _():
            for comp in range(3):
                for c in range(NL):
                    ZS[0, comp, 8 * c : 8 * c + 8, :] = STEP[comp, 4, 8 * c : 8 * c + 8, :]
            z_make(0).start()

        return 0

    lax.fori_loop(1, 5, first_step, 0)
    pending.append(z_make(0).wait_send)

    def fields(par, comp, m, c):
        a0 = XA[par][comp, m, 8 * c : 8 * c + 8, :]
        a1 = XA[par][comp, m, 8 * c + 1 : 8 * c + 9, :]
        d0 = XD[par][comp, m, 8 * c : 8 * c + 8, :]
        d1 = XD[par][comp, m, 8 * c + 1 : 8 * c + 9, :]
        return a0 + a1, a1 - a0, d0 + d1, d1 - d0

    def modes(par, m, c):
        out = []
        for comp in range(3):
            lo = fields(par, comp, m, c)
            hi = fields(par, comp, m + 1, c)
            out.append(
                dict(
                    z=hi[0] - lo[0], y=hi[1] + lo[1], yz=hi[1] - lo[1], x=hi[2] + lo[2], zx=hi[2] - lo[2],
                    xy=hi[3] + lo[3], xyz=hi[3] - lo[3],
                )
            )
        return out

    def ghost(par):
        for n, X in enumerate((XA, XD)):
            arrived(X[par].at[:, 0, 0:rows, :], r_x.at[par, n])
            for c in range(NL):
                X[par][2, 0, 8 * c : 8 * c + 8, :] = -X[par][2, 0, 8 * c : 8 * c + 8, :]

    there = jnp.where(inside(jnp.where(core == 1, 8, -1)), f32(1.0), f32(0.0))

    def far_ghost(s):
        arrived(ZG.at[s], r_z.at[s])
        par = s % 2
        if s == 1:
            arrived(INVD.at[5], r_i)
            for c in range(NL):
                INVD[5, 8 * c : 8 * c + 8, :] = INVD[5, 8 * c : 8 * c + 8, :] * there
        for comp in range(3):
            scale = -there if comp == 2 else there
            for c in range(NL):
                at = slice(8 * c, 8 * c + 8)
                v = ZG[s, comp, at, :] * scale
                if s > 0:
                    v = v - coefs[s - 1][1] * (INVD[5, at, :] * KU[comp, at, :])
                n = xnext(v)
                XA[par][comp, 5, at, :] = v + n
                XD[par][comp, 5, at, :] = n - v

    coefs = chebyshev()

    def lay_out(half):
        for n in range(2):
            k = 2 * half + n
            m = jnp.where(core == 1, k + 1, 4 - k)
            for c in range(NL):
                at = slice(8 * c, 8 * c + 8)
                for comp in range(3):
                    v = SOL[comp, m, at, :]
                    OUT[comp, k, at, :] = v * flip if comp == 2 else v

    def o_make(half):
        return remote(
            OUT.at[:, pl.ds(2 * half, 2)], disp.at[yh], s_o.at[half], r_o.at[yh], dev(l, z, core, half)
        )

    def element_forces(par, m, c):
        u, v, w = modes(par, m, c)
        e = EM[m, 8 * c : 8 * c + 8, :]
        e2, e3, eq = e + e, e * (1.0 / 3.0), e * ((RATIO + 4.0) / 9.0)
        tr = (0.5 * RATIO) * (u["x"] + v["y"] + w["z"])
        fx = e2 * (tr + u["x"])
        fy = e2 * (tr + v["y"])
        fz = e2 * (tr + w["z"])
        sxy = e * (u["y"] + v["x"])
        syz = e * (v["z"] + w["y"])
        szx = e * (u["z"] + w["x"])
        h = 0.5 * (v["xy"] + w["zx"])
        vxy, wzx = e * (v["xy"] + h), e * (w["zx"] + h)
        h = 0.5 * (u["xy"] + w["yz"])
        uxy, wyz = e * (u["xy"] + h), e * (w["yz"] + h)
        h = 0.5 * (u["zx"] + v["yz"])
        uzx, vyz = e * (u["zx"] + h), e * (v["yz"] + h)
        h = u["yz"] + v["zx"] + w["xy"]
        uyz, vzx, wxy = e3 * (u["yz"] + h), e3 * (v["zx"] + h), e3 * (w["xy"] + h)
        uq, vq, wq = eq * u["xyz"], eq * v["xyz"], eq * w["xyz"]
        return (
            (szx, sxy, uyz, fx, uzx, uxy, uq),
            (syz, fy, vyz, sxy, vzx, vxy, vq),
            (fz, syz, wyz, szx, wzx, wxy, wq),
        )

    def push_up(comp, at, force):
        gz_, gy, gyz, gx, gzx, gxy, gxyz = force
        UP[4 * comp, at, :] = gz_
        UP[4 * comp + 1, at, :] = gy + gyz
        UP[4 * comp + 2, at, :] = gx + gzx
        UP[4 * comp + 3, at, :] = gxy + gxyz

    def pull(buf, comp, c, taa, tay, tda, tdy):
        buf[2 * comp, 8 * c + 8 : 8 * c + 16, :] = taa + tay
        buf[2 * comp + 1, 8 * c + 8 : 8 * c + 16, :] = tda + tdy
        a = (taa - tay) + buf[2 * comp, 8 * c + 7 : 8 * c + 15, :]
        b = (tda - tdy) + buf[2 * comp + 1, 8 * c + 7 : 8 * c + 15, :]
        return (a - b) + xprev(a + b)

    def sweep(s):
        par = s % 2
        nxt = 1 - par
        c1, c2 = coefs[s]
        ghost(par)
        for c in range(NL):
            at = slice(8 * c, 8 * c + 8)
            for comp, force in enumerate(element_forces(par, 0, c)):
                push_up(comp, at, force)

        def send_on(comp, m, at, step):
            sent = SOL[comp, m, at, :] + step
            SOL[comp, m, at, :] = sent
            if s < SWEEPS - 1:
                sent = step
            n = xnext(sent)
            XA[nxt][comp, m, at, :] = sent + n
            XD[nxt][comp, m, at, :] = n - sent

        def layer(m, _):
            for c in range(NL):
                at = slice(8 * c, 8 * c + 8)
                inv = INVD[m, at, :]
                for comp, force in enumerate(element_forces(par, m, c)):
                    gz_, gy, gyz, gx, gzx, gxy, gxyz = force
                    taa = UP[4 * comp, at, :] - gz_
                    tay = UP[4 * comp + 1, at, :] + (gy - gyz)
                    tda = UP[4 * comp + 2, at, :] + (gx - gzx)
                    tdy = UP[4 * comp + 3, at, :] + (gxy - gxyz)
                    push_up(comp, at, force)
                    res = R[comp, m, at, :] - pull(GU, comp, c, taa, tay, tda, tdy)
                    R[comp, m, at, :] = res
                    step = c1 * STEP[comp, m, at, :] + c2 * (inv * res)
                    STEP[comp, m, at, :] = step
                    send_on(comp, m, at, step)

            @pl.when(m == 1)
            def _():
                for cp in x_make(par):
                    cp.wait_send()
                for cp in x_make(nxt):
                    cp.start()

            return 0

        lax.fori_loop(1, 4, layer, 0)

        for c in range(NL):
            at = slice(8 * c, 8 * c + 8)
            inv = INVD[4, at, :]
            for comp in range(3):
                held = [UP[4 * comp + f, at, :] for f in range(4)]
                res = R[comp, 4, at, :] - pull(GU, comp, c, *held)
                R[comp, 4, at, :] = res
                step = c1 * STEP[comp, 4, at, :] + c2 * (inv * res)
                STEP[comp, 4, at, :] = step
                ZS[s + 1, comp, at, :] = SOL[comp, 4, at, :] + step if s == SWEEPS - 1 else step
        if s < SWEEPS - 1:
            z_make(s + 1).start()
            pending.append(z_make(s + 1).wait_send)
        else:
            @pl.when(core == 0)
            def _():
                z_make(SWEEPS).start()

            lay_out(1 - core)
            o_make(1 - core).start()
        filter_part(s)
        far_ghost(s)
        for c in range(NL):
            at = slice(8 * c, 8 * c + 8)
            inv = INVD[4, at, :]
            for comp, force in enumerate(element_forces(par, 4, c)):
                gz_, gy, gyz, gx, gzx, gxy, gxyz = force
                near = pull(GU, comp, c, -gz_, gy - gyz, gx - gzx, gxy - gxyz)
                KU[comp, at, :] = pull(GV, comp, c, gz_, gy + gyz, gx + gzx, gxy + gxyz)
                R[comp, 4, at, :] = R[comp, 4, at, :] - near
                step = STEP[comp, 4, at, :] - c2 * (inv * near)
                STEP[comp, 4, at, :] = step
                send_on(comp, 4, at, step)

    for s in range(SWEEPS):
        sweep(s)

    @pl.when(both)
    def _():
        lay_out(core)
        pltpu.make_async_copy(OUT.at[:, pl.ds(2 * core, 2)], disp.at[yh], r_o.at[yh]).start()

    @pl.when(jnp.logical_not(both))
    def _():
        lay_out(core)
        o_make(core).start()

    def o_ended():
        o_make(1 - core).wait_send()

        @pl.when(jnp.logical_not(both))
        def _():
            o_make(core).wait_send()

        for k in range(2):
            arrived(disp.at[k], r_o.at[k])

    pending.append(o_ended)

    fin = SWEEPS % 2
    pending.extend(cp.wait_send for cp in x_make(fin))
    pending.append(v_sent)

    def z_sent():
        @pl.when(core == 0)
        def _():
            z_make(SWEEPS).wait_send()

    pending.append(z_sent)
    weight = weights[2 * l + yh].astype(f32)
    weight_sum = weights[0]
    for n in range(1, 2 * NL):
        weight_sum = weight_sum + weights[n]
    weight_sum = weight_sum.astype(f32)

    def energy_layer(k, share):
        m = jnp.where(core == 1, k + 1, 3 - k)
        for c in range(NL):
            u, v, w = modes(fin, m, c)
            tr = u["x"] + v["y"] + w["z"]
            sq = lambda t: t * t
            normal = sq(u["x"]) + sq(v["y"]) + sq(w["z"])
            shear = sq(u["y"] + v["x"]) + sq(v["z"] + w["y"]) + sq(u["z"] + w["x"])
            pairs = (
                sq(v["xy"]) + sq(w["zx"]) + sq(u["xy"]) + sq(w["yz"]) + sq(u["zx"]) + sq(v["yz"])
            )
            joint = sq(v["xy"] + w["zx"]) + sq(u["xy"] + w["yz"]) + sq(u["zx"] + v["yz"])
            s = u["yz"] + v["zx"] + w["xy"]
            triple = sq(u["yz"]) + sq(v["zx"]) + sq(w["xy"]) + sq(s)
            quad = sq(u["xyz"]) + sq(v["xyz"]) + sq(w["xyz"])
            total = (
                (RATIO * sq(tr) + 2.0 * normal + shear) + (pairs + 0.5 * joint)
                + (1.0 / 3.0) * triple + ((RATIO + 4.0) / 9.0) * quad
            )
            t = (weight * UNIT) * total
            half, j = k // 2, k % 2
            MS[c, half, j] = t
            if c > 0:
                MS[c - 1, half, 2, pl.ds(2 * j + 1, 1), :] = t[0:1, :]
            if c < NL - 1:
                MS[c + 1, half, 2, pl.ds(2 * j, 1), :] = t[7:8, :]
            share = share + t * G[k, 8 * c : 8 * c + 8, :]
        return share

    def last_layer(k, got):
        @pl.when(k == 3)
        def _():
            ghost(fin)

            @pl.when(core == 1)
            def _():
                far_ghost(SWEEPS)

        return energy_layer(k, got)

    share = lax.fori_loop(0, 4, last_layer, zero8)
    share = jnp.sum(share, axis=0, keepdims=True)
    for c in range(NL):
        for k in range(2):
            MS[c, k, 2, 4:5, :] = share

    me = 2 * l + yh
    m_copies = []
    def m_make(k, cc):
        ll = lax.rem(l + k, NL)
        return remote(MS.at[ll, cc], RX.at[me], s_m.at[k, cc], r_m, dev(ll, z, core, cc))

    for k in far_first(NL):
        for cc in range(2):
            if k > 0:
                m_make(k, cc).start()
            else:
                alone = jnp.logical_and(both, core == cc)

                @pl.when(alone)
                def _():
                    pltpu.make_async_copy(MS.at[l, cc], RX.at[me], r_m).start()

                @pl.when(jnp.logical_not(alone))
                def _():
                    m_make(k, cc).start()

    def m_sent():
        for k in range(NL):
            for cc in range(2):
                if k > 0:
                    m_make(k, cc).wait_send()
                else:
                    @pl.when(jnp.logical_not(jnp.logical_and(both, core == cc)))
                    def _():
                        m_make(k, cc).wait_send()

    pending.append(m_sent)

    arrived(RX, r_m)
    scale = (3.0 * (1.0 - EMIN)) / weight_sum
    def summed(k):
        parts = [RX[n, k] for n in range(2 * NL)]
        while len(parts) > 1:
            parts = [a + b for a, b in zip(parts[::2], parts[1::2])]
        return parts[0]

    rim = summed(2)
    SV[...] = rim[4:5, :]

    def s_make(kz, ky):
        return remote(SV, RX2.at[2 * z + yh], s_s.at[kz, ky], r_s, dev(l, z + kz, (yh + ky) % 2, core))

    for kz in far_first(Z):
        for ky in (1, 0):
            if (kz, ky) != (0, 0):
                s_make(kz, ky).start()
    pltpu.make_async_copy(SV, RX2.at[2 * z + yh], r_s).start()

    def s_sent():
        for kz in range(Z):
            for ky in range(2):
                if (kz, ky) != (0, 0):
                    s_make(kz, ky).wait_send()

    pending.append(s_sent)
    native = 4 * yh + 2 * (1 - core)
    for k in range(2):
        main = summed(k)
        rated = []
        for n in range(3):
            near = pl.ds(pl.multiple_of(8 * l + 8 * n, 8), 8)
            d = D[native + k, near, :]
            row = jnp.clip(8 * l + 8 * (n - 1), 0, rows - 8)
            lab = LAB[native + k, pl.ds(pl.multiple_of(row, 8), 8), :]
            solid = jnp.where(lab == 2, 1.0, d)
            rated.append(d * solid * solid * scale)
        above = jnp.where(l > 0, f32(1.0), f32(0.0)) * rated[0][7:8, :]
        below = jnp.where(l < NL - 1, f32(1.0), f32(0.0)) * rated[2][0:1, :]
        DS[k + 1, 8:16, :] = main * rated[1]
        DS[k + 1, 7:8, :] = rim[2 * k : 2 * k + 1, :] * above
        DS[k + 1, 16:17, :] = rim[2 * k + 1 : 2 * k + 2, :] * below

    def h_make(up):
        to = lax.rem(g + (1 if up else 4 * Z - 1), 4 * Z)
        return remote(DS.at[2 if up else 1], DS.at[0 if up else 3], s_h.at[int(up)], r_h.at[int(up)], (l, to))

    for up in (False, True):
        h_make(up).start()
        pending.append(h_make(up).wait_send)
    arrived(DS.at[3], r_h.at[0])
    arrived(DS.at[0], r_h.at[1])

    planes = []
    for k in range(4):
        planes.append(plane_sums(DS[k, 8:16, :], DS[k, 7:15, :], DS[k, 9:17, :]))
    low = jnp.where(g > 0, f32(1.0), f32(0.0)) * planes[0][1]
    high = jnp.where(g < 4 * Z - 1, f32(1.0), f32(0.0)) * planes[3][1]
    numer = [planes[1][0] + low + planes[2][1], planes[2][0] + planes[1][1] + high]
    @pl.when(both)
    def _():
        for k in range(2):
            VO[k] = V[1 + 2 * core + k, here8, :]

    @pl.when(jnp.logical_not(both))
    def _():
        arrived(VO, r_v)

    arrived(RX2, r_s)
    total = RX2[0]
    for n in range(1, 2 * Z):
        total = total + RX2[n]
    mean = jnp.sum(total, axis=1, keepdims=True) * scale / (8 * Z * rows * 128)
    for k in range(2):
        filtered = numer[k] * VO[k]
        d = D[native + k, here8, :]
        candidate = d * jnp.sqrt(filtered / mean)
        lower = jnp.maximum(d - MOVE_LIMIT, FLOOR_DENSITY)
        upper = jnp.minimum(d + MOVE_LIMIT, 1.0)
        new = jnp.minimum(jnp.maximum(candidate, lower), upper)
        newd[k] = jnp.where(LAB[native + k, mine, :] == 2, 1.0, new)

    for end in pending:
        end()


def solution(mesh):
    NL, Z = mesh.shape["load"], mesh.shape["gz"] // 4
    rows = 8 * NL

    def on_device(density, labels, forces, case_weights):
        vm = lambda *shape: pltpu.VMEM(shape, jnp.float32)
        dma = lambda *shape: pltpu.SemaphoreType.DMA(shape)
        scratch = [
            vm(*density.shape),
            pltpu.VMEM(labels.shape, jnp.int32),
            vm(*forces.shape),
            vm(3, 4, rows, 128),
            pltpu.VMEM((8, rows, 128), jnp.int32),
            vm(8, rows + 16, 128),
            vm(6, rows, 128),
            vm(6, rows + 8, 128),
            vm(6, rows, 128),
            vm(3, 6, rows, 128),
            vm(3, 6, rows, 128),
            vm(3, 6, rows, 128),
            vm(3, 6, rows + 8, 128),
            vm(3, 6, rows + 8, 128),
            vm(3, 6, rows + 8, 128),
            vm(3, 6, rows + 8, 128),
            vm(12, rows, 128),
            vm(6, rows + 8, 128),
            vm(6, rows + 8, 128),
            vm(3, rows, 128),
            vm(3, 4, rows, 128),
            vm(4, 3, rows, 128),
            vm(4, 3, rows, 128),
            vm(8, rows, 128),
            vm(8, rows, 128),
            vm(6, rows + 16, 128),
            vm(2, 8, 128),
            vm(4, rows, 128),
            vm(NL, 2, 3, 8, 128),
            vm(2 * NL, 3, 8, 128),
            vm(4, 24, 128),
            vm(1, 128),
            vm(2 * Z, 1, 128),
            pltpu.SMEM((2 * NL,), jnp.int32),
            vm(46 << 11, 128),
            dma(NL, 2), pltpu.SemaphoreType.DMA,
            pltpu.SemaphoreType.DMA, pltpu.SemaphoreType.DMA,
            dma(2), dma(2),
            dma(2), dma(2),
            dma(2), dma(2),
            pltpu.SemaphoreType.DMA, pltpu.SemaphoreType.DMA,
            pltpu.SemaphoreType.DMA, pltpu.SemaphoreType.DMA,
            pltpu.SemaphoreType.DMA, pltpu.SemaphoreType.DMA,
            dma(2, 2), dma(2, 2),
            dma(4), dma(4),
            dma(2), dma(2),
            dma(NL, 2), pltpu.SemaphoreType.DMA,
            dma(2), dma(2),
            dma(Z, 2), pltpu.SemaphoreType.DMA,
            dma(4),
        ]
        return pl.pallas_call(
            functools.partial(kernel, NL, Z),
            out_shape=(
                pltpu.VMEM(density.shape, jnp.float32),
                pltpu.VMEM(forces.shape, jnp.float32),
            ),
            in_specs=[pl.BlockSpec(memory_space=pltpu.HBM)] * 4,
            out_specs=(pl.BlockSpec(memory_space=pltpu.VMEM), pl.BlockSpec(memory_space=pltpu.VMEM)),
            scratch_shapes=scratch,
            compiler_params=pltpu.CompilerParams(
                collective_id=1, has_side_effects=True, vmem_limit_bytes=60 << 20
            ),
            name="step",
        )(density, labels, forces, case_weights)

    return jax.shard_map(
        on_device,
        mesh=mesh,
        in_specs=(
            P("gz", "load", None),
            P("gz", None, None),
            P("load", None, "gz", None, None),
            P(),
        ),
        out_specs=(P("gz", "load", None), P("load", None, "gz", None, None)),
        check_vma=False,
    )
```

```python
import functools

import jax
import jax.numpy as jnp
import numpy as np
from jax import lax
from jax.experimental import pallas as pl
from jax.experimental.pallas import tpu as pltpu
from jax.sharding import PartitionSpec as P

MESH = pl.DeviceIdType.MESH
SWEEPS = 3
EMIN = 0.001
LOWER_EIG = 0.1
UPPER_EIG = 2.5
MOVE_LIMIT = 0.2
FLOOR_DENSITY = 0.001
THETA = 0.5 * (UPPER_EIG + LOWER_EIG)
DELTA = 0.5 * (UPPER_EIG - LOWER_EIG)
POISSON = 0.3
SHEAR = 1.0 / (2 * (1 + POISSON))
RATIO = 2 * POISSON / (1 - 2 * POISSON)
UNIT = SHEAR / 16.0
DIAG = UNIT * ((RATIO + 4.0) + (2.0 * (RATIO + 3.0) + 2.0) / 3.0 + (RATIO + 4.0) / 9.0)
EDGE = 1.5 - float(np.sqrt(2.0))


def chebyshev():
    sigma = THETA / DELTA
    factor = 1.0 / sigma
    pairs = []
    for _ in range(SWEEPS):
        following = 1.0 / (2.0 * sigma - factor)
        pairs.append((following * factor, 2.0 * following / DELTA))
        factor = following
    return pairs


def kernel(
    NL, Z, density_in, labels_in, forces_in, weights_in, newd, disp,
    density, labels, forces, F, LAB, D, EM, TX, INVD, R, STEP, SOL, XA0, XA1, XD0, XD1, UP, GU, GV, KU, OUT, ZS, ZG,
    PA, PB, V, VO, G, MS, RX, DS, SV, RX2, weights, spare,
    s_d, r_d, s_e, r_e, s_f, r_f, s_l, r_l, s_y, r_y, s_w, r_w, s_i, r_i, s_v, r_v, s_x, r_x, s_z, r_z,
    s_o, r_o, s_m, r_m, s_h, r_h, s_s, r_s, loc,
):
    rows = 8 * NL
    f32 = jnp.float32
    XA, XD = (XA0, XA1), (XD0, XD1)
    l = lax.axis_index("load")
    g = lax.axis_index("gz")
    core = g % 2
    yh = (g // 2) % 2
    z = g // 4

    def dev(ll, zz, yy, cc):
        return (lax.rem(ll + NL, NL), (lax.rem(zz + Z, Z) * 2 + yy) * 2 + cc)

    def remote(src, dst, ssem, rsem, target):
        return pltpu.make_async_remote_copy(
            src_ref=src, dst_ref=dst, send_sem=ssem, recv_sem=rsem, device_id=target, device_id_type=MESH
        )

    def arrived(ref, sem):
        pltpu.make_async_copy(ref, ref, sem).wait()

    pending = []

    def far_first(count):
        return sorted(range(count), key=lambda k: -min(k, count - k))

    lane = lax.broadcasted_iota(jnp.int32, (8, 128), 1)

    def xnext(v):
        return jnp.where(lane == 127, 0.0, pltpu.roll(v, 127, 1))

    def xprev(v):
        return jnp.where(lane == 0, 0.0, pltpu.roll(v, 1, 1))

    staged = [
        pltpu.make_async_copy(given, here, loc.at[n])
        for n, (given, here) in enumerate(
            ((density_in, density), (labels_in, labels), (forces_in, forces), (weights_in, weights))
        )
    ]
    for cp in staged:
        cp.start()
    barrier = pltpu.get_barrier_semaphore()

    def greet(target):
        pl.semaphore_signal(barrier, inc=1, device_id=target, device_id_type=MESH)

    both = yh == core
    far = z + 2 * core - 1
    sibling = dev(l, z, yh, 1 - core)
    is_self = [jnp.logical_and(both, yh == 0), jnp.logical_and(both, yh == 1)]

    for k in range(NL):
        for cc in range(2):
            if k > 0:
                greet(dev(l + k, z, core, cc))
            else:
                @pl.when(jnp.logical_not(jnp.logical_and(both, core == cc)))
                def _():
                    greet(dev(l, z, core, cc))
    greet(sibling)
    greet(dev(l, far, yh, 1 - core))
    for k in range(1, Z):
        greet(dev(l, z + k, yh, core))
    pl.semaphore_wait(barrier, 2 * NL + 2 + (Z - 1) - jnp.where(both, 1, 0))

    for cp in staged:
        cp.wait()

    mine = pl.ds(pl.multiple_of(8 * l, 8), 8)
    here8 = pl.ds(pl.multiple_of(8 * l + 8, 8), 8)
    two = pl.ds(2 * core + 2, 2)

    def d_make(n, k):
        return remote(density, D.at[two, here8, :], s_d.at[n, k], r_d, dev(l + n, z, k, yh))

    def l_make(k):
        return remote(labels, LAB.at[two], s_l.at[k], r_l.at[core], dev(l, z, k, yh))

    def f_make(k):
        return remote(forces.at[k], F.at[:, pl.ds(2 * core, 2)], s_f.at[k], r_f.at[core], dev(l, z, k, yh))

    for n in far_first(NL)[:-1]:
        for k in range(2):
            cp = d_make(n, k)
            cp.start()
            pending.append(cp.wait_send)
    for k in range(2):
        @pl.when(is_self[k])
        def _():
            pltpu.make_async_copy(density, D.at[two, here8, :], r_d).start()
            pltpu.make_async_copy(labels, LAB.at[two], r_l.at[core]).start()
            pltpu.make_async_copy(forces.at[k], F.at[:, pl.ds(2 * core, 2)], r_f.at[core]).start()

        @pl.when(jnp.logical_not(is_self[k]))
        def _():
            d_make(0, k).start()
            l_make(k).start()
            f_make(k).start()

    def native_sent():
        for k in range(2):
            @pl.when(jnp.logical_not(is_self[k]))
            def _():
                d_make(0, k).wait_send()
                l_make(k).wait_send()
                f_make(k).wait_send()

    pending.append(native_sent)
    zero8 = jnp.zeros((8, 128), f32)
    for r in range(8):
        D[r, 0:8, :] = zero8
        D[r, rows + 8 : rows + 16, :] = zero8
    for r in range(6):
        V[r, 0:8, :] = zero8
        V[r, rows + 8 : rows + 16, :] = zero8
        TX[r, 0:8, :] = zero8
        GU[r, 0:8, :] = zero8
        GV[r, 0:8, :] = zero8
        for k in range(2):
            for c in range(3):
                XA[k][c, r, rows : rows + 8, :] = zero8
                XD[k][c, r, rows : rows + 8, :] = zero8
    for k in range(4):
        for t in range(3):
            DS[k, 8 * t : 8 * t + 8, :] = zero8
    for c in range(NL):
        for k in range(2):
            MS[c, k, 2] = zero8

    arrived(D.at[2:6, 8 : rows + 8, :], r_d)
    for k in range(2):
        arrived(LAB.at[2 + 2 * k : 4 + 2 * k], r_l.at[k])

    src2, dst2 = pl.ds(4 - 2 * core, 2), pl.ds(6 * core, 2)
    got2 = pl.ds(6 * (1 - core), 2)
    relays = [
        remote(LAB.at[src2], LAB.at[pl.ds(6 * core, 2)], s_y.at[0], r_y.at[0], sibling),
        remote(D.at[src2, 8 : rows + 8, :], D.at[dst2, 8 : rows + 8, :], s_y.at[1], r_y.at[1], sibling),
    ]
    for cp in relays:
        cp.start()
        pending.append(cp.wait_send)

    sgn = 2 * core - 1

    def inside(p):
        at = 8 * z + p
        return jnp.logical_and(at >= 0, at < 8 * Z)

    def moduli_layer(m, _):
        p = 3 + sgn * m
        r = p + 2 - 4 * core
        scale = jnp.where(inside(p), f32(UNIT), f32(0.0))
        for c in range(NL):
            d = D[r, 8 * c + 8 : 8 * c + 16, :]
            solid = jnp.where(LAB[r, 8 * c : 8 * c + 8, :] == 2, 1.0, d)
            e = (EMIN + (1.0 - EMIN) * solid * solid * solid) * scale
            EM[m, 8 * c : 8 * c + 8, :] = e
            TX[m, 8 * c + 8 : 8 * c + 16, :] = e + xprev(e)
        return 0

    lax.fori_loop(core, core + 4, moduli_layer, 0)

    def e_make():
        return remote(EM.at[4], EM.at[4], s_e, r_e, dev(l, far, yh, 1 - core))

    @pl.when(core == 1)
    def _():
        e_make().start()

    def e_sent():
        @pl.when(core == 1)
        def _():
            e_make().wait_send()

    pending.append(e_sent)

    def w_make():
        return remote(
            D.at[pl.ds(2 + 2 * core, 2), 8 : rows + 8, :],
            D.at[pl.ds(6 * (1 - core), 2), 8 : rows + 8, :],
            s_w, r_w, dev(l, far, yh, 1 - core),
        )

    w_make().start()
    pending.append(w_make().wait_send)
    arrived(LAB.at[pl.ds(6 * (1 - core), 2)], r_y.at[0])
    arrived(D.at[got2, 8 : rows + 8, :], r_y.at[1])

    @pl.when(core == 1)
    def _():
        moduli_layer(0, 0)

    def inverse_layer(m, _):
        p = jnp.where(core == 1, 3 + m, 4 - m)
        r = p + 2 - 4 * core
        keep = jnp.where(inside(p), 1, 0)
        for c in range(NL):
            near = TX[m, 8 * c + 8 : 8 * c + 16, :] + TX[m, 8 * c + 7 : 8 * c + 15, :]
            back = TX[m - 1, 8 * c + 8 : 8 * c + 16, :] + TX[m - 1, 8 * c + 7 : 8 * c + 15, :]
            lab = LAB[r, 8 * c : 8 * c + 8, :] * keep + (1 - keep)
            INVD[m, 8 * c : 8 * c + 8, :] = jnp.where(lab != 1, (UNIT / DIAG) / (near + back), 0.0)
        return 0

    lax.fori_loop(1, 4, inverse_layer, 0)

    @pl.when(core == 0)
    def _():
        arrived(EM.at[4], r_e)
        known = jnp.where(inside(-1), f32(1.0), f32(0.0))
        for c in range(NL):
            e = EM[4, 8 * c : 8 * c + 8, :] * known
            EM[4, 8 * c : 8 * c + 8, :] = e
            TX[4, 8 * c + 8 : 8 * c + 16, :] = e + xprev(e)

    inverse_layer(4, 0)

    give_inverse = remote(INVD.at[4], INVD.at[5], s_i, r_i, dev(l, far, yh, 1 - core))
    give_inverse.start()
    pending.append(give_inverse.wait_send)

    def plane_sums(center, above, below):
        ysum = above + below
        xsum = xnext(center) + xprev(center)
        cross = ysum + xsum
        corner = xnext(ysum) + xprev(ysum)
        return 1.5 * center + 0.5 * cross + EDGE * corner, 0.5 * center + EDGE * cross

    def d_plane(r, _):
        scale = jnp.where(inside(r - 2 + 4 * core), f32(1.0), f32(0.0))
        for c in range(NL):
            a, b = plane_sums(
                D[r, 8 * c + 8 : 8 * c + 16, :], D[r, 8 * c + 7 : 8 * c + 15, :], D[r, 8 * c + 9 : 8 * c + 17, :]
            )
            PA[r, 8 * c : 8 * c + 8, :] = a * scale
            PB[r, 8 * c : 8 * c + 8, :] = b * scale
        return 0

    def v_plane(r, _):
        ok = jnp.where(inside(r - 2 + 4 * core), f32(1.0), f32(0.0))
        for c in range(NL):
            at = slice(8 * c, 8 * c + 8)
            total = PA[r, at, :] + PB[r - 1, at, :] + PB[r + 1, at, :]
            V[r - 1, 8 * c + 8 : 8 * c + 16, :] = ok / (total + (1.0 - ok))
        return 0

    def v_make():
        return remote(V.at[pl.ds(3 - 2 * core, 2), here8, :], VO, s_v, r_v, sibling)

    def v_sent():
        @pl.when(both)
        def _():
            v_make().wait_send()

    def w_plane(n, _):
        for c in range(NL):
            a, b = plane_sums(
                V[n, 8 * c + 8 : 8 * c + 16, :], V[n, 8 * c + 7 : 8 * c + 15, :], V[n, 8 * c + 9 : 8 * c + 17, :]
            )
            PA[n, 8 * c : 8 * c + 8, :] = a
            PB[n, 8 * c : 8 * c + 8, :] = b
        return 0

    def g_plane(k, _):
        r = k + 2
        for c in range(NL):
            at = slice(8 * c, 8 * c + 8)
            d = D[r, 8 * c + 8 : 8 * c + 16, :]
            solid = jnp.where(LAB[r, at, :] == 2, 1.0, d)
            G[k, at, :] = (PA[k + 1, at, :] + PB[k, at, :] + PB[k + 2, at, :]) * (d * solid * solid)
        return 0

    def filter_part(s):
        if s == 0:
            arrived(D.at[pl.ds(6 * core, 2), 8 : rows + 8, :], r_w)
            lax.fori_loop(0, 8, d_plane, 0)
            lax.fori_loop(1, 7, v_plane, 0)

            @pl.when(both)
            def _():
                v_make().start()
        elif s == 2:
            lax.fori_loop(0, 6, w_plane, 0)
            lax.fori_loop(0, 4, g_plane, 0)

    for k in range(2):
        arrived(F.at[:, 2 * k : 2 * k + 2], r_f.at[k])
    flip = jnp.where(core == 1, f32(1.0), f32(-1.0))

    def x_make(par):
        return [
            remote(X[par].at[:, 1, 0:rows, :], X[par].at[:, 0, 0:rows, :], s_x.at[par, n], r_x.at[par, n], sibling)
            for n, X in enumerate((XA, XD))
        ]

    def z_make(n):
        return remote(ZS.at[n], ZG.at[n], s_z.at[n], r_z.at[n], dev(l, far, yh, 1 - core))

    def first_step(n, _):
        m = jnp.where(n == 0, 4, n)
        i = jnp.where(core == 1, m - 1, 4 - m)
        for c in range(NL):
            at = slice(8 * c, 8 * c + 8)
            inv = INVD[m, at, :]
            for comp in range(3):
                f = F[comp, i, at, :]
                if comp == 2:
                    f = f * flip
                R[comp, m, at, :] = f
                s = inv * f * (1.0 / THETA)
                STEP[comp, m, at, :] = s
                SOL[comp, m, at, :] = s
                n = xnext(s)
                XA[0][comp, m, at, :] = s + n
                XD[0][comp, m, at, :] = n - s

        @pl.when(m == 1)
        def _():
            for cp in x_make(0):
                cp.start()

        @pl.when(m == 4)
        def _():
            for comp in range(3):
                for c in range(NL):
                    ZS[0, comp, 8 * c : 8 * c + 8, :] = STEP[comp, 4, 8 * c : 8 * c + 8, :]
            z_make(0).start()

        return 0

    lax.fori_loop(0, 4, first_step, 0)
    pending.append(z_make(0).wait_send)

    def fields(par, comp, m, c):
        a0 = XA[par][comp, m, 8 * c : 8 * c + 8, :]
        a1 = XA[par][comp, m, 8 * c + 1 : 8 * c + 9, :]
        d0 = XD[par][comp, m, 8 * c : 8 * c + 8, :]
        d1 = XD[par][comp, m, 8 * c + 1 : 8 * c + 9, :]
        return a0 + a1, a1 - a0, d0 + d1, d1 - d0

    def modes(par, m, c):
        out = []
        for comp in range(3):
            lo = fields(par, comp, m, c)
            hi = fields(par, comp, m + 1, c)
            out.append(
                dict(
                    z=hi[0] - lo[0], y=hi[1] + lo[1], yz=hi[1] - lo[1], x=hi[2] + lo[2], zx=hi[2] - lo[2],
                    xy=hi[3] + lo[3], xyz=hi[3] - lo[3],
                )
            )
        return out

    def ghost(par):
        for n, X in enumerate((XA, XD)):
            arrived(X[par].at[:, 0, 0:rows, :], r_x.at[par, n])
            for c in range(NL):
                X[par][2, 0, 8 * c : 8 * c + 8, :] = -X[par][2, 0, 8 * c : 8 * c + 8, :]

    there = jnp.where(inside(jnp.where(core == 1, 8, -1)), f32(1.0), f32(0.0))

    def far_ghost(s):
        arrived(ZG.at[s], r_z.at[s])
        par = s % 2
        if s == 1:
            arrived(INVD.at[5], r_i)
            for c in range(NL):
                INVD[5, 8 * c : 8 * c + 8, :] = INVD[5, 8 * c : 8 * c + 8, :] * there
        for comp in range(3):
            scale = -there if comp == 2 else there
            for c in range(NL):
                at = slice(8 * c, 8 * c + 8)
                v = ZG[s, comp, at, :] * scale
                if s > 0:
                    v = v - coefs[s - 1][1] * (INVD[5, at, :] * KU[comp, at, :])
                n = xnext(v)
                XA[par][comp, 5, at, :] = v + n
                XD[par][comp, 5, at, :] = n - v

    coefs = chebyshev()

    def lay_out(half):
        for n in range(2):
            k = 2 * half + n
            m = jnp.where(core == 1, k + 1, 4 - k)
            for c in range(NL):
                at = slice(8 * c, 8 * c + 8)
                for comp in range(3):
                    v = SOL[comp, m, at, :]
                    OUT[comp, k, at, :] = v * flip if comp == 2 else v

    def o_make(half):
        return remote(
            OUT.at[:, pl.ds(2 * half, 2)], disp.at[yh], s_o.at[half], r_o.at[yh], dev(l, z, core, half)
        )

    def element_forces(par, m, c):
        u, v, w = modes(par, m, c)
        e = EM[m, 8 * c : 8 * c + 8, :]
        e2, e3, eq = e + e, e * (1.0 / 3.0), e * ((RATIO + 4.0) / 9.0)
        tr = (0.5 * RATIO) * (u["x"] + v["y"] + w["z"])
        fx = e2 * (tr + u["x"])
        fy = e2 * (tr + v["y"])
        fz = e2 * (tr + w["z"])
        sxy = e * (u["y"] + v["x"])
        syz = e * (v["z"] + w["y"])
        szx = e * (u["z"] + w["x"])
        h = 0.5 * (v["xy"] + w["zx"])
        vxy, wzx = e * (v["xy"] + h), e * (w["zx"] + h)
        h = 0.5 * (u["xy"] + w["yz"])
        uxy, wyz = e * (u["xy"] + h), e * (w["yz"] + h)
        h = 0.5 * (u["zx"] + v["yz"])
        uzx, vyz = e * (u["zx"] + h), e * (v["yz"] + h)
        h = u["yz"] + v["zx"] + w["xy"]
        uyz, vzx, wxy = e3 * (u["yz"] + h), e3 * (v["zx"] + h), e3 * (w["xy"] + h)
        uq, vq, wq = eq * u["xyz"], eq * v["xyz"], eq * w["xyz"]
        return (
            (szx, sxy, uyz, fx, uzx, uxy, uq),
            (syz, fy, vyz, sxy, vzx, vxy, vq),
            (fz, syz, wyz, szx, wzx, wxy, wq),
        )

    def push_up(comp, at, force):
        gz_, gy, gyz, gx, gzx, gxy, gxyz = force
        UP[4 * comp, at, :] = gz_
        UP[4 * comp + 1, at, :] = gy + gyz
        UP[4 * comp + 2, at, :] = gx + gzx
        UP[4 * comp + 3, at, :] = gxy + gxyz

    def pull(buf, comp, c, taa, tay, tda, tdy):
        buf[2 * comp, 8 * c + 8 : 8 * c + 16, :] = taa + tay
        buf[2 * comp + 1, 8 * c + 8 : 8 * c + 16, :] = tda + tdy
        a = (taa - tay) + buf[2 * comp, 8 * c + 7 : 8 * c + 15, :]
        b = (tda - tdy) + buf[2 * comp + 1, 8 * c + 7 : 8 * c + 15, :]
        return (a - b) + xprev(a + b)

    def sweep(s):
        par = s % 2
        nxt = 1 - par
        c1, c2 = coefs[s]

        for c in range(NL):
            at = slice(8 * c, 8 * c + 8)
            inv = INVD[4, at, :]
            for comp, force in enumerate(element_forces(par, 3, c)):
                gz_, gy, gyz, gx, gzx, gxy, gxyz = force
                res = R[comp, 4, at, :] - pull(GU, comp, c, gz_, gy + gyz, gx + gzx, gxy + gxyz)
                R[comp, 4, at, :] = res
                step = c1 * STEP[comp, 4, at, :] + c2 * (inv * res)
                STEP[comp, 4, at, :] = step
                ZS[s + 1, comp, at, :] = SOL[comp, 4, at, :] + step if s == SWEEPS - 1 else step
        if s < SWEEPS - 1:
            z_make(s + 1).start()
            pending.append(z_make(s + 1).wait_send)
        else:
            @pl.when(core == 0)
            def _():
                z_make(SWEEPS).start()

        ghost(par)
        for c in range(NL):
            at = slice(8 * c, 8 * c + 8)
            for comp, force in enumerate(element_forces(par, 0, c)):
                push_up(comp, at, force)

        def send_on(comp, m, at, step):
            sent = SOL[comp, m, at, :] + step
            SOL[comp, m, at, :] = sent
            if s < SWEEPS - 1:
                sent = step
            n = xnext(sent)
            XA[nxt][comp, m, at, :] = sent + n
            XD[nxt][comp, m, at, :] = n - sent

        def layer(m, _):
            for c in range(NL):
                at = slice(8 * c, 8 * c + 8)
                inv = INVD[m, at, :]
                for comp, force in enumerate(element_forces(par, m, c)):
                    gz_, gy, gyz, gx, gzx, gxy, gxyz = force
                    taa = UP[4 * comp, at, :] - gz_
                    tay = UP[4 * comp + 1, at, :] + (gy - gyz)
                    tda = UP[4 * comp + 2, at, :] + (gx - gzx)
                    tdy = UP[4 * comp + 3, at, :] + (gxy - gxyz)
                    push_up(comp, at, force)
                    res = R[comp, m, at, :] - pull(GU, comp, c, taa, tay, tda, tdy)
                    R[comp, m, at, :] = res
                    step = c1 * STEP[comp, m, at, :] + c2 * (inv * res)
                    STEP[comp, m, at, :] = step
                    send_on(comp, m, at, step)

            @pl.when(m == 1)
            def _():
                for cp in x_make(par):
                    cp.wait_send()
                for cp in x_make(nxt):
                    cp.start()

            return 0

        lax.fori_loop(1, 4, layer, 0)

        if s == SWEEPS - 1:
            lay_out(1 - core)
            o_make(1 - core).start()
        filter_part(s)
        far_ghost(s)
        for c in range(NL):
            at = slice(8 * c, 8 * c + 8)
            inv = INVD[4, at, :]
            for comp, force in enumerate(element_forces(par, 4, c)):
                gz_, gy, gyz, gx, gzx, gxy, gxyz = force
                near = pull(GU, comp, c, -gz_, gy - gyz, gx - gzx, gxy - gxyz)
                KU[comp, at, :] = pull(GV, comp, c, gz_, gy + gyz, gx + gzx, gxy + gxyz)
                R[comp, 4, at, :] = R[comp, 4, at, :] - near
                step = STEP[comp, 4, at, :] - c2 * (inv * near)
                STEP[comp, 4, at, :] = step
                send_on(comp, 4, at, step)

    for s in range(SWEEPS):
        sweep(s)

    @pl.when(both)
    def _():
        lay_out(core)
        pltpu.make_async_copy(OUT.at[:, pl.ds(2 * core, 2)], disp.at[yh], r_o.at[yh]).start()

    @pl.when(jnp.logical_not(both))
    def _():
        lay_out(core)
        o_make(core).start()

    def o_ended():
        o_make(1 - core).wait_send()

        @pl.when(jnp.logical_not(both))
        def _():
            o_make(core).wait_send()

        for k in range(2):
            arrived(disp.at[k], r_o.at[k])

    pending.append(o_ended)

    fin = SWEEPS % 2
    pending.extend(cp.wait_send for cp in x_make(fin))
    pending.append(v_sent)

    def z_sent():
        @pl.when(core == 0)
        def _():
            z_make(SWEEPS).wait_send()

    pending.append(z_sent)
    weight = weights[2 * l + yh].astype(f32)
    weight_sum = weights[0]
    for n in range(1, 2 * NL):
        weight_sum = weight_sum + weights[n]
    weight_sum = weight_sum.astype(f32)

    def energy_layer(k, share):
        m = jnp.where(core == 1, k + 1, 3 - k)
        for c in range(NL):
            u, v, w = modes(fin, m, c)
            tr = u["x"] + v["y"] + w["z"]
            sq = lambda t: t * t
            normal = sq(u["x"]) + sq(v["y"]) + sq(w["z"])
            shear = sq(u["y"] + v["x"]) + sq(v["z"] + w["y"]) + sq(u["z"] + w["x"])
            pairs = (
                sq(v["xy"]) + sq(w["zx"]) + sq(u["xy"]) + sq(w["yz"]) + sq(u["zx"]) + sq(v["yz"])
            )
            joint = sq(v["xy"] + w["zx"]) + sq(u["xy"] + w["yz"]) + sq(u["zx"] + v["yz"])
            s = u["yz"] + v["zx"] + w["xy"]
            triple = sq(u["yz"]) + sq(v["zx"]) + sq(w["xy"]) + sq(s)
            quad = sq(u["xyz"]) + sq(v["xyz"]) + sq(w["xyz"])
            total = (
                (RATIO * sq(tr) + 2.0 * normal + shear) + (pairs + 0.5 * joint)
                + (1.0 / 3.0) * triple + ((RATIO + 4.0) / 9.0) * quad
            )
            t = (weight * UNIT) * total
            half, j = k // 2, k % 2
            MS[c, half, j] = t
            if c > 0:
                MS[c - 1, half, 2, pl.ds(2 * j + 1, 1), :] = t[0:1, :]
            if c < NL - 1:
                MS[c + 1, half, 2, pl.ds(2 * j, 1), :] = t[7:8, :]
            share = share + t * G[k, 8 * c : 8 * c + 8, :]
        return share

    def last_layer(k, got):
        @pl.when(k == 3)
        def _():
            ghost(fin)

            @pl.when(core == 1)
            def _():
                far_ghost(SWEEPS)

        return energy_layer(k, got)

    share = lax.fori_loop(0, 4, last_layer, zero8)
    share = jnp.sum(share, axis=0, keepdims=True)
    for c in range(NL):
        for k in range(2):
            MS[c, k, 2, 4:5, :] = share

    me = 2 * l + yh
    m_copies = []
    def m_make(k, cc):
        ll = lax.rem(l + k, NL)
        return remote(MS.at[ll, cc], RX.at[me], s_m.at[k, cc], r_m, dev(ll, z, core, cc))

    for k in far_first(NL):
        for cc in range(2):
            if k > 0:
                m_make(k, cc).start()
            else:
                alone = jnp.logical_and(both, core == cc)

                @pl.when(alone)
                def _():
                    pltpu.make_async_copy(MS.at[l, cc], RX.at[me], r_m).start()

                @pl.when(jnp.logical_not(alone))
                def _():
                    m_make(k, cc).start()

    def m_sent():
        for k in range(NL):
            for cc in range(2):
                if k > 0:
                    m_make(k, cc).wait_send()
                else:
                    @pl.when(jnp.logical_not(jnp.logical_and(both, core == cc)))
                    def _():
                        m_make(k, cc).wait_send()

    pending.append(m_sent)

    arrived(RX, r_m)
    scale = (3.0 * (1.0 - EMIN)) / weight_sum
    def summed(k):
        parts = [RX[n, k] for n in range(2 * NL)]
        while len(parts) > 1:
            parts = [a + b for a, b in zip(parts[::2], parts[1::2])]
        return parts[0]

    rim = summed(2)
    SV[...] = rim[4:5, :]

    def s_make(kz, ky):
        return remote(SV, RX2.at[2 * z + yh], s_s.at[kz, ky], r_s, dev(l, z + kz, (yh + ky) % 2, core))

    for kz in far_first(Z):
        for ky in (1, 0):
            if (kz, ky) != (0, 0):
                s_make(kz, ky).start()
    pltpu.make_async_copy(SV, RX2.at[2 * z + yh], r_s).start()

    def s_sent():
        for kz in range(Z):
            for ky in range(2):
                if (kz, ky) != (0, 0):
                    s_make(kz, ky).wait_send()

    pending.append(s_sent)
    native = 4 * yh + 2 * (1 - core)
    for k in range(2):
        main = summed(k)
        rated = []
        for n in range(3):
            near = pl.ds(pl.multiple_of(8 * l + 8 * n, 8), 8)
            d = D[native + k, near, :]
            row = jnp.clip(8 * l + 8 * (n - 1), 0, rows - 8)
            lab = LAB[native + k, pl.ds(pl.multiple_of(row, 8), 8), :]
            solid = jnp.where(lab == 2, 1.0, d)
            rated.append(d * solid * solid * scale)
        above = jnp.where(l > 0, f32(1.0), f32(0.0)) * rated[0][7:8, :]
        below = jnp.where(l < NL - 1, f32(1.0), f32(0.0)) * rated[2][0:1, :]
        DS[k + 1, 8:16, :] = main * rated[1]
        DS[k + 1, 7:8, :] = rim[2 * k : 2 * k + 1, :] * above
        DS[k + 1, 16:17, :] = rim[2 * k + 1 : 2 * k + 2, :] * below

    def h_make(up):
        to = lax.rem(g + (1 if up else 4 * Z - 1), 4 * Z)
        return remote(DS.at[2 if up else 1], DS.at[0 if up else 3], s_h.at[int(up)], r_h.at[int(up)], (l, to))

    for up in (False, True):
        h_make(up).start()
        pending.append(h_make(up).wait_send)
    arrived(DS.at[3], r_h.at[0])
    arrived(DS.at[0], r_h.at[1])

    planes = []
    for k in range(4):
        planes.append(plane_sums(DS[k, 8:16, :], DS[k, 7:15, :], DS[k, 9:17, :]))
    low = jnp.where(g > 0, f32(1.0), f32(0.0)) * planes[0][1]
    high = jnp.where(g < 4 * Z - 1, f32(1.0), f32(0.0)) * planes[3][1]
    numer = [planes[1][0] + low + planes[2][1], planes[2][0] + planes[1][1] + high]
    @pl.when(both)
    def _():
        for k in range(2):
            VO[k] = V[1 + 2 * core + k, here8, :]

    @pl.when(jnp.logical_not(both))
    def _():
        arrived(VO, r_v)

    arrived(RX2, r_s)
    total = RX2[0]
    for n in range(1, 2 * Z):
        total = total + RX2[n]
    mean = jnp.sum(total, axis=1, keepdims=True) * scale / (8 * Z * rows * 128)
    for k in range(2):
        filtered = numer[k] * VO[k]
        d = D[native + k, here8, :]
        candidate = d * jnp.sqrt(filtered / mean)
        lower = jnp.maximum(d - MOVE_LIMIT, FLOOR_DENSITY)
        upper = jnp.minimum(d + MOVE_LIMIT, 1.0)
        new = jnp.minimum(jnp.maximum(candidate, lower), upper)
        newd[k] = jnp.where(LAB[native + k, mine, :] == 2, 1.0, new)

    for end in pending:
        end()


def solution(mesh):
    NL, Z = mesh.shape["load"], mesh.shape["gz"] // 4
    rows = 8 * NL

    def on_device(density, labels, forces, case_weights):
        vm = lambda *shape: pltpu.VMEM(shape, jnp.float32)
        dma = lambda *shape: pltpu.SemaphoreType.DMA(shape)
        scratch = [
            vm(*density.shape),
            pltpu.VMEM(labels.shape, jnp.int32),
            vm(*forces.shape),
            vm(3, 4, rows, 128),
            pltpu.VMEM((8, rows, 128), jnp.int32),
            vm(8, rows + 16, 128),
            vm(6, rows, 128),
            vm(6, rows + 8, 128),
            vm(6, rows, 128),
            vm(3, 6, rows, 128),
            vm(3, 6, rows, 128),
            vm(3, 6, rows, 128),
            vm(3, 6, rows + 8, 128),
            vm(3, 6, rows + 8, 128),
            vm(3, 6, rows + 8, 128),
            vm(3, 6, rows + 8, 128),
            vm(12, rows, 128),
            vm(6, rows + 8, 128),
            vm(6, rows + 8, 128),
            vm(3, rows, 128),
            vm(3, 4, rows, 128),
            vm(4, 3, rows, 128),
            vm(4, 3, rows, 128),
            vm(8, rows, 128),
            vm(8, rows, 128),
            vm(6, rows + 16, 128),
            vm(2, 8, 128),
            vm(4, rows, 128),
            vm(NL, 2, 3, 8, 128),
            vm(2 * NL, 3, 8, 128),
            vm(4, 24, 128),
            vm(1, 128),
            vm(2 * Z, 1, 128),
            pltpu.SMEM((2 * NL,), jnp.int32),
            vm(46 << 11, 128),
            dma(NL, 2), pltpu.SemaphoreType.DMA,
            pltpu.SemaphoreType.DMA, pltpu.SemaphoreType.DMA,
            dma(2), dma(2),
            dma(2), dma(2),
            dma(2), dma(2),
            pltpu.SemaphoreType.DMA, pltpu.SemaphoreType.DMA,
            pltpu.SemaphoreType.DMA, pltpu.SemaphoreType.DMA,
            pltpu.SemaphoreType.DMA, pltpu.SemaphoreType.DMA,
            dma(2, 2), dma(2, 2),
            dma(4), dma(4),
            dma(2), dma(2),
            dma(NL, 2), pltpu.SemaphoreType.DMA,
            dma(2), dma(2),
            dma(Z, 2), pltpu.SemaphoreType.DMA,
            dma(4),
        ]
        return pl.pallas_call(
            functools.partial(kernel, NL, Z),
            out_shape=(
                pltpu.VMEM(density.shape, jnp.float32),
                pltpu.VMEM(forces.shape, jnp.float32),
            ),
            in_specs=[pl.BlockSpec(memory_space=pltpu.HBM)] * 4,
            out_specs=(pl.BlockSpec(memory_space=pltpu.VMEM), pl.BlockSpec(memory_space=pltpu.VMEM)),
            scratch_shapes=scratch,
            compiler_params=pltpu.CompilerParams(
                collective_id=1, has_side_effects=True, vmem_limit_bytes=60 << 20
            ),
            name="step",
        )(density, labels, forces, case_weights)

    return jax.shard_map(
        on_device,
        mesh=mesh,
        in_specs=(
            P("gz", "load", None),
            P("gz", None, None),
            P("load", None, "gz", None, None),
            P(),
        ),
        out_specs=(P("gz", "load", None), P("load", None, "gz", None, None)),
        check_vma=False,
    )
```

```python
import functools

import jax
import jax.numpy as jnp
import numpy as np
from jax import lax
from jax.experimental import pallas as pl
from jax.experimental.pallas import tpu as pltpu
from jax.sharding import PartitionSpec as P

MESH = pl.DeviceIdType.MESH
SWEEPS = 3
EMIN = 0.001
LOWER_EIG = 0.1
UPPER_EIG = 2.5
MOVE_LIMIT = 0.2
FLOOR_DENSITY = 0.001
THETA = 0.5 * (UPPER_EIG + LOWER_EIG)
DELTA = 0.5 * (UPPER_EIG - LOWER_EIG)
POISSON = 0.3
SHEAR = 1.0 / (2 * (1 + POISSON))
RATIO = 2 * POISSON / (1 - 2 * POISSON)
UNIT = SHEAR / 16.0
DIAG = UNIT * ((RATIO + 4.0) + (2.0 * (RATIO + 3.0) + 2.0) / 3.0 + (RATIO + 4.0) / 9.0)
EDGE = 1.5 - float(np.sqrt(2.0))


def chebyshev():
    sigma = THETA / DELTA
    factor = 1.0 / sigma
    pairs = []
    for _ in range(SWEEPS):
        following = 1.0 / (2.0 * sigma - factor)
        pairs.append((following * factor, 2.0 * following / DELTA))
        factor = following
    return pairs


def kernel(
    NL, Z, density_in, labels_in, forces_in, weights_in, newd, disp,
    density, labels, forces, F, LAB, D, EM, TX, INVD, R, STEP, SOL, XA0, XA1, XD0, XD1, UP, GU, GV, KU, OUT, ZS, ZG,
    PA, PB, V, VO, G, MS, RX, DS, SV, RX2, weights, spare,
    s_d, r_d, s_e, r_e, s_f, r_f, s_l, r_l, s_y, r_y, s_w, r_w, s_i, r_i, s_v, r_v, s_x, r_x, s_z, r_z,
    s_o, r_o, s_m, r_m, s_h, r_h, s_s, r_s, loc,
):
    rows = 8 * NL
    f32 = jnp.float32
    XA, XD = (XA0, XA1), (XD0, XD1)
    l = lax.axis_index("load")
    g = lax.axis_index("gz")
    core = g % 2
    yh = (g // 2) % 2
    z = g // 4

    def dev(ll, zz, yy, cc):
        return (lax.rem(ll + NL, NL), (lax.rem(zz + Z, Z) * 2 + yy) * 2 + cc)

    def remote(src, dst, ssem, rsem, target):
        return pltpu.make_async_remote_copy(
            src_ref=src, dst_ref=dst, send_sem=ssem, recv_sem=rsem, device_id=target, device_id_type=MESH
        )

    def arrived(ref, sem):
        pltpu.make_async_copy(ref, ref, sem).wait()

    pending = []

    def far_first(count):
        return sorted(range(count), key=lambda k: -min(k, count - k))

    lane = lax.broadcasted_iota(jnp.int32, (8, 128), 1)

    def xnext(v):
        return jnp.where(lane == 127, 0.0, pltpu.roll(v, 127, 1))

    def xprev(v):
        return jnp.where(lane == 0, 0.0, pltpu.roll(v, 1, 1))

    staged = [
        pltpu.make_async_copy(given, here, loc.at[n])
        for n, (given, here) in enumerate(
            ((density_in, density), (labels_in, labels), (forces_in, forces), (weights_in, weights))
        )
    ]
    for cp in staged:
        cp.start()
    barrier = pltpu.get_barrier_semaphore()

    def greet(target):
        pl.semaphore_signal(barrier, inc=1, device_id=target, device_id_type=MESH)

    both = yh == core
    far = z + 2 * core - 1
    sibling = dev(l, z, yh, 1 - core)
    is_self = [jnp.logical_and(both, yh == 0), jnp.logical_and(both, yh == 1)]

    for k in range(NL):
        for cc in range(2):
            if k > 0:
                greet(dev(l + k, z, core, cc))
            else:
                @pl.when(jnp.logical_not(jnp.logical_and(both, core == cc)))
                def _():
                    greet(dev(l, z, core, cc))
    greet(sibling)
    greet(dev(l, far, yh, 1 - core))
    for k in range(1, Z):
        greet(dev(l, z + k, yh, core))
    pl.semaphore_wait(barrier, 2 * NL + 2 + (Z - 1) - jnp.where(both, 1, 0))

    for cp in staged:
        cp.wait()

    mine = pl.ds(pl.multiple_of(8 * l, 8), 8)
    here8 = pl.ds(pl.multiple_of(8 * l + 8, 8), 8)
    two = pl.ds(2 * core + 2, 2)

    def d_make(n, k):
        return remote(density, D.at[two, here8, :], s_d.at[n, k], r_d, dev(l + n, z, k, yh))

    def l_make(k):
        return remote(labels, LAB.at[two], s_l.at[k], r_l.at[core], dev(l, z, k, yh))

    def f_make(k):
        return remote(forces.at[k], F.at[:, pl.ds(2 * core, 2)], s_f.at[k], r_f.at[core], dev(l, z, k, yh))

    for n in far_first(NL)[:-1]:
        for k in range(2):
            cp = d_make(n, k)
            cp.start()
            pending.append(cp.wait_send)
    for k in range(2):
        @pl.when(is_self[k])
        def _():
            pltpu.make_async_copy(density, D.at[two, here8, :], r_d).start()
            pltpu.make_async_copy(labels, LAB.at[two], r_l.at[core]).start()
            pltpu.make_async_copy(forces.at[k], F.at[:, pl.ds(2 * core, 2)], r_f.at[core]).start()

        @pl.when(jnp.logical_not(is_self[k]))
        def _():
            d_make(0, k).start()
            l_make(k).start()
            f_make(k).start()

    def native_sent():
        for k in range(2):
            @pl.when(jnp.logical_not(is_self[k]))
            def _():
                d_make(0, k).wait_send()
                l_make(k).wait_send()
                f_make(k).wait_send()

    pending.append(native_sent)
    zero8 = jnp.zeros((8, 128), f32)
    for r in range(8):
        D[r, 0:8, :] = zero8
        D[r, rows + 8 : rows + 16, :] = zero8
    for r in range(6):
        V[r, 0:8, :] = zero8
        V[r, rows + 8 : rows + 16, :] = zero8
        TX[r, 0:8, :] = zero8
        GU[r, 0:8, :] = zero8
        GV[r, 0:8, :] = zero8
        for k in range(2):
            for c in range(3):
                XA[k][c, r, rows : rows + 8, :] = zero8
                XD[k][c, r, rows : rows + 8, :] = zero8
    for k in range(4):
        for t in range(3):
            DS[k, 8 * t : 8 * t + 8, :] = zero8
    for c in range(NL):
        for k in range(2):
            MS[c, k, 2] = zero8

    arrived(D.at[2:6, 8 : rows + 8, :], r_d)
    for k in range(2):
        arrived(LAB.at[2 + 2 * k : 4 + 2 * k], r_l.at[k])

    src2, dst2 = pl.ds(4 - 2 * core, 2), pl.ds(6 * core, 2)
    got2 = pl.ds(6 * (1 - core), 2)
    relays = [
        remote(LAB.at[src2], LAB.at[pl.ds(6 * core, 2)], s_y.at[0], r_y.at[0], sibling),
        remote(D.at[src2, 8 : rows + 8, :], D.at[dst2, 8 : rows + 8, :], s_y.at[1], r_y.at[1], sibling),
    ]
    for cp in relays:
        cp.start()
        pending.append(cp.wait_send)

    sgn = 2 * core - 1

    def inside(p):
        at = 8 * z + p
        return jnp.logical_and(at >= 0, at < 8 * Z)

    def moduli_layer(m, _):
        p = 3 + sgn * m
        r = p + 2 - 4 * core
        scale = jnp.where(inside(p), f32(UNIT), f32(0.0))
        for c in range(NL):
            d = D[r, 8 * c + 8 : 8 * c + 16, :]
            solid = jnp.where(LAB[r, 8 * c : 8 * c + 8, :] == 2, 1.0, d)
            e = (EMIN + (1.0 - EMIN) * solid * solid * solid) * scale
            EM[m, 8 * c : 8 * c + 8, :] = e
            TX[m, 8 * c + 8 : 8 * c + 16, :] = e + xprev(e)
        return 0

    lax.fori_loop(core, core + 4, moduli_layer, 0)

    def e_make():
        return remote(EM.at[4], EM.at[4], s_e, r_e, dev(l, far, yh, 1 - core))

    @pl.when(core == 1)
    def _():
        e_make().start()

    def e_sent():
        @pl.when(core == 1)
        def _():
            e_make().wait_send()

    pending.append(e_sent)

    def w_make():
        return remote(
            D.at[pl.ds(2 + 2 * core, 2), 8 : rows + 8, :],
            D.at[pl.ds(6 * (1 - core), 2), 8 : rows + 8, :],
            s_w, r_w, dev(l, far, yh, 1 - core),
        )

    arrived(LAB.at[pl.ds(6 * (1 - core), 2)], r_y.at[0])
    arrived(D.at[got2, 8 : rows + 8, :], r_y.at[1])

    @pl.when(core == 1)
    def _():
        moduli_layer(0, 0)

    def inverse_layer(m, _):
        p = jnp.where(core == 1, 3 + m, 4 - m)
        r = p + 2 - 4 * core
        keep = jnp.where(inside(p), 1, 0)
        for c in range(NL):
            near = TX[m, 8 * c + 8 : 8 * c + 16, :] + TX[m, 8 * c + 7 : 8 * c + 15, :]
            back = TX[m - 1, 8 * c + 8 : 8 * c + 16, :] + TX[m - 1, 8 * c + 7 : 8 * c + 15, :]
            lab = LAB[r, 8 * c : 8 * c + 8, :] * keep + (1 - keep)
            INVD[m, 8 * c : 8 * c + 8, :] = jnp.where(lab != 1, (UNIT / DIAG) / (near + back), 0.0)
        return 0

    lax.fori_loop(1, 4, inverse_layer, 0)

    @pl.when(core == 0)
    def _():
        arrived(EM.at[4], r_e)
        known = jnp.where(inside(-1), f32(1.0), f32(0.0))
        for c in range(NL):
            e = EM[4, 8 * c : 8 * c + 8, :] * known
            EM[4, 8 * c : 8 * c + 8, :] = e
            TX[4, 8 * c + 8 : 8 * c + 16, :] = e + xprev(e)

    inverse_layer(4, 0)

    give_inverse = remote(INVD.at[4], INVD.at[5], s_i, r_i, dev(l, far, yh, 1 - core))
    give_inverse.start()
    w_make().start()
    pending.append(w_make().wait_send)
    pending.append(give_inverse.wait_send)

    def plane_sums(center, above, below):
        ysum = above + below
        xsum = xnext(center) + xprev(center)
        cross = ysum + xsum
        corner = xnext(ysum) + xprev(ysum)
        return 1.5 * center + 0.5 * cross + EDGE * corner, 0.5 * center + EDGE * cross

    def d_plane(r, _):
        scale = jnp.where(inside(r - 2 + 4 * core), f32(1.0), f32(0.0))
        for c in range(NL):
            a, b = plane_sums(
                D[r, 8 * c + 8 : 8 * c + 16, :], D[r, 8 * c + 7 : 8 * c + 15, :], D[r, 8 * c + 9 : 8 * c + 17, :]
            )
            PA[r, 8 * c : 8 * c + 8, :] = a * scale
            PB[r, 8 * c : 8 * c + 8, :] = b * scale
        return 0

    def v_plane(r, _):
        ok = jnp.where(inside(r - 2 + 4 * core), f32(1.0), f32(0.0))
        for c in range(NL):
            at = slice(8 * c, 8 * c + 8)
            total = PA[r, at, :] + PB[r - 1, at, :] + PB[r + 1, at, :]
            V[r - 1, 8 * c + 8 : 8 * c + 16, :] = ok / (total + (1.0 - ok))
        return 0

    def v_make():
        return remote(V.at[pl.ds(3 - 2 * core, 2), here8, :], VO, s_v, r_v, sibling)

    def v_sent():
        @pl.when(both)
        def _():
            v_make().wait_send()

    def w_plane(n, _):
        for c in range(NL):
            a, b = plane_sums(
                V[n, 8 * c + 8 : 8 * c + 16, :], V[n, 8 * c + 7 : 8 * c + 15, :], V[n, 8 * c + 9 : 8 * c + 17, :]
            )
            PA[n, 8 * c : 8 * c + 8, :] = a
            PB[n, 8 * c : 8 * c + 8, :] = b
        return 0

    def g_plane(k, _):
        r = k + 2
        for c in range(NL):
            at = slice(8 * c, 8 * c + 8)
            d = D[r, 8 * c + 8 : 8 * c + 16, :]
            solid = jnp.where(LAB[r, at, :] == 2, 1.0, d)
            G[k, at, :] = (PA[k + 1, at, :] + PB[k, at, :] + PB[k + 2, at, :]) * (d * solid * solid)
        return 0

    def filter_part(s):
        if s == 0:
            arrived(D.at[pl.ds(6 * core, 2), 8 : rows + 8, :], r_w)
            lax.fori_loop(0, 8, d_plane, 0)
            lax.fori_loop(1, 7, v_plane, 0)

            @pl.when(both)
            def _():
                v_make().start()
        elif s == 2:
            lax.fori_loop(0, 6, w_plane, 0)
            lax.fori_loop(0, 4, g_plane, 0)

    for k in range(2):
        arrived(F.at[:, 2 * k : 2 * k + 2], r_f.at[k])
    flip = jnp.where(core == 1, f32(1.0), f32(-1.0))

    def x_make(par):
        return [
            remote(X[par].at[:, 1, 0:rows, :], X[par].at[:, 0, 0:rows, :], s_x.at[par, n], r_x.at[par, n], sibling)
            for n, X in enumerate((XA, XD))
        ]

    def z_make(n):
        return remote(ZS.at[n], ZG.at[n], s_z.at[n], r_z.at[n], dev(l, far, yh, 1 - core))

    def first_step(n, _):
        m = jnp.where(n == 0, 4, n)
        i = jnp.where(core == 1, m - 1, 4 - m)
        for c in range(NL):
            at = slice(8 * c, 8 * c + 8)
            inv = INVD[m, at, :]
            for comp in range(3):
                f = F[comp, i, at, :]
                if comp == 2:
                    f = f * flip
                R[comp, m, at, :] = f
                s = inv * f * (1.0 / THETA)
                STEP[comp, m, at, :] = s
                SOL[comp, m, at, :] = s
                n = xnext(s)
                XA[0][comp, m, at, :] = s + n
                XD[0][comp, m, at, :] = n - s

        @pl.when(m == 1)
        def _():
            for cp in x_make(0):
                cp.start()

        @pl.when(m == 4)
        def _():
            for comp in range(3):
                for c in range(NL):
                    ZS[0, comp, 8 * c : 8 * c + 8, :] = STEP[comp, 4, 8 * c : 8 * c + 8, :]
            z_make(0).start()

        return 0

    lax.fori_loop(0, 4, first_step, 0)
    pending.append(z_make(0).wait_send)

    def fields(par, comp, m, c):
        a0 = XA[par][comp, m, 8 * c : 8 * c + 8, :]
        a1 = XA[par][comp, m, 8 * c + 1 : 8 * c + 9, :]
        d0 = XD[par][comp, m, 8 * c : 8 * c + 8, :]
        d1 = XD[par][comp, m, 8 * c + 1 : 8 * c + 9, :]
        return a0 + a1, a1 - a0, d0 + d1, d1 - d0

    def modes(par, m, c):
        out = []
        for comp in range(3):
            lo = fields(par, comp, m, c)
            hi = fields(par, comp, m + 1, c)
            out.append(
                dict(
                    z=hi[0] - lo[0], y=hi[1] + lo[1], yz=hi[1] - lo[1], x=hi[2] + lo[2], zx=hi[2] - lo[2],
                    xy=hi[3] + lo[3], xyz=hi[3] - lo[3],
                )
            )
        return out

    def ghost(par):
        for n, X in enumerate((XA, XD)):
            arrived(X[par].at[:, 0, 0:rows, :], r_x.at[par, n])
            for c in range(NL):
                X[par][2, 0, 8 * c : 8 * c + 8, :] = -X[par][2, 0, 8 * c : 8 * c + 8, :]

    there = jnp.where(inside(jnp.where(core == 1, 8, -1)), f32(1.0), f32(0.0))

    def far_ghost(s):
        arrived(ZG.at[s], r_z.at[s])
        par = s % 2
        if s == 1:
            arrived(INVD.at[5], r_i)
            for c in range(NL):
                INVD[5, 8 * c : 8 * c + 8, :] = INVD[5, 8 * c : 8 * c + 8, :] * there
        for comp in range(3):
            scale = -there if comp == 2 else there
            for c in range(NL):
                at = slice(8 * c, 8 * c + 8)
                v = ZG[s, comp, at, :] * scale
                if s > 0:
                    v = v - coefs[s - 1][1] * (INVD[5, at, :] * KU[comp, at, :])
                n = xnext(v)
                XA[par][comp, 5, at, :] = v + n
                XD[par][comp, 5, at, :] = n - v

    coefs = chebyshev()

    def lay_out(half):
        for n in range(2):
            k = 2 * half + n
            m = jnp.where(core == 1, k + 1, 4 - k)
            for c in range(NL):
                at = slice(8 * c, 8 * c + 8)
                for comp in range(3):
                    v = SOL[comp, m, at, :]
                    OUT[comp, k, at, :] = v * flip if comp == 2 else v

    def o_make(half):
        return remote(
            OUT.at[:, pl.ds(2 * half, 2)], disp.at[yh], s_o.at[half], r_o.at[yh], dev(l, z, core, half)
        )

    def element_forces(par, m, c):
        u, v, w = modes(par, m, c)
        e = EM[m, 8 * c : 8 * c + 8, :]
        e2, e3, eq = e + e, e * (1.0 / 3.0), e * ((RATIO + 4.0) / 9.0)
        tr = (0.5 * RATIO) * (u["x"] + v["y"] + w["z"])
        fx = e2 * (tr + u["x"])
        fy = e2 * (tr + v["y"])
        fz = e2 * (tr + w["z"])
        sxy = e * (u["y"] + v["x"])
        syz = e * (v["z"] + w["y"])
        szx = e * (u["z"] + w["x"])
        h = 0.5 * (v["xy"] + w["zx"])
        vxy, wzx = e * (v["xy"] + h), e * (w["zx"] + h)
        h = 0.5 * (u["xy"] + w["yz"])
        uxy, wyz = e * (u["xy"] + h), e * (w["yz"] + h)
        h = 0.5 * (u["zx"] + v["yz"])
        uzx, vyz = e * (u["zx"] + h), e * (v["yz"] + h)
        h = u["yz"] + v["zx"] + w["xy"]
        uyz, vzx, wxy = e3 * (u["yz"] + h), e3 * (v["zx"] + h), e3 * (w["xy"] + h)
        uq, vq, wq = eq * u["xyz"], eq * v["xyz"], eq * w["xyz"]
        return (
            (szx, sxy, uyz, fx, uzx, uxy, uq),
            (syz, fy, vyz, sxy, vzx, vxy, vq),
            (fz, syz, wyz, szx, wzx, wxy, wq),
        )

    def push_up(comp, at, force):
        gz_, gy, gyz, gx, gzx, gxy, gxyz = force
        UP[4 * comp, at, :] = gz_
        UP[4 * comp + 1, at, :] = gy + gyz
        UP[4 * comp + 2, at, :] = gx + gzx
        UP[4 * comp + 3, at, :] = gxy + gxyz

    def pull(buf, comp, c, taa, tay, tda, tdy):
        buf[2 * comp, 8 * c + 8 : 8 * c + 16, :] = taa + tay
        buf[2 * comp + 1, 8 * c + 8 : 8 * c + 16, :] = tda + tdy
        a = (taa - tay) + buf[2 * comp, 8 * c + 7 : 8 * c + 15, :]
        b = (tda - tdy) + buf[2 * comp + 1, 8 * c + 7 : 8 * c + 15, :]
        return (a - b) + xprev(a + b)

    def sweep(s):
        par = s % 2
        nxt = 1 - par
        c1, c2 = coefs[s]

        for c in range(NL):
            at = slice(8 * c, 8 * c + 8)
            inv = INVD[4, at, :]
            for comp, force in enumerate(element_forces(par, 3, c)):
                gz_, gy, gyz, gx, gzx, gxy, gxyz = force
                res = R[comp, 4, at, :] - pull(GU, comp, c, gz_, gy + gyz, gx + gzx, gxy + gxyz)
                R[comp, 4, at, :] = res
                step = c1 * STEP[comp, 4, at, :] + c2 * (inv * res)
                STEP[comp, 4, at, :] = step
                ZS[s + 1, comp, at, :] = SOL[comp, 4, at, :] + step if s == SWEEPS - 1 else step
        if s < SWEEPS - 1:
            z_make(s + 1).start()
            pending.append(z_make(s + 1).wait_send)
        else:
            @pl.when(core == 0)
            def _():
                z_make(SWEEPS).start()

        ghost(par)
        for c in range(NL):
            at = slice(8 * c, 8 * c + 8)
            for comp, force in enumerate(element_forces(par, 0, c)):
                push_up(comp, at, force)

        def send_on(comp, m, at, step):
            sent = SOL[comp, m, at, :] + step
            SOL[comp, m, at, :] = sent
            if s < SWEEPS - 1:
                sent = step
            n = xnext(sent)
            XA[nxt][comp, m, at, :] = sent + n
            XD[nxt][comp, m, at, :] = n - sent

        def layer(m, _):
            for c in range(NL):
                at = slice(8 * c, 8 * c + 8)
                inv = INVD[m, at, :]
                for comp, force in enumerate(element_forces(par, m, c)):
                    gz_, gy, gyz, gx, gzx, gxy, gxyz = force
                    taa = UP[4 * comp, at, :] - gz_
                    tay = UP[4 * comp + 1, at, :] + (gy - gyz)
                    tda = UP[4 * comp + 2, at, :] + (gx - gzx)
                    tdy = UP[4 * comp + 3, at, :] + (gxy - gxyz)
                    push_up(comp, at, force)
                    res = R[comp, m, at, :] - pull(GU, comp, c, taa, tay, tda, tdy)
                    R[comp, m, at, :] = res
                    step = c1 * STEP[comp, m, at, :] + c2 * (inv * res)
                    STEP[comp, m, at, :] = step
                    send_on(comp, m, at, step)

            @pl.when(m == 1)
            def _():
                for cp in x_make(par):
                    cp.wait_send()
                for cp in x_make(nxt):
                    cp.start()

            return 0

        lax.fori_loop(1, 4, layer, 0)

        if s == SWEEPS - 1:
            lay_out(1 - core)
            o_make(1 - core).start()
        filter_part(s)
        far_ghost(s)
        for c in range(NL):
            at = slice(8 * c, 8 * c + 8)
            inv = INVD[4, at, :]
            for comp, force in enumerate(element_forces(par, 4, c)):
                gz_, gy, gyz, gx, gzx, gxy, gxyz = force
                near = pull(GU, comp, c, -gz_, gy - gyz, gx - gzx, gxy - gxyz)
                KU[comp, at, :] = pull(GV, comp, c, gz_, gy + gyz, gx + gzx, gxy + gxyz)
                R[comp, 4, at, :] = R[comp, 4, at, :] - near
                step = STEP[comp, 4, at, :] - c2 * (inv * near)
                STEP[comp, 4, at, :] = step
                send_on(comp, 4, at, step)

    for s in range(SWEEPS):
        sweep(s)

    @pl.when(both)
    def _():
        lay_out(core)
        pltpu.make_async_copy(OUT.at[:, pl.ds(2 * core, 2)], disp.at[yh], r_o.at[yh]).start()

    @pl.when(jnp.logical_not(both))
    def _():
        lay_out(core)
        o_make(core).start()

    def o_ended():
        o_make(1 - core).wait_send()

        @pl.when(jnp.logical_not(both))
        def _():
            o_make(core).wait_send()

        for k in range(2):
            arrived(disp.at[k], r_o.at[k])

    pending.append(o_ended)

    fin = SWEEPS % 2
    pending.extend(cp.wait_send for cp in x_make(fin))
    pending.append(v_sent)

    def z_sent():
        @pl.when(core == 0)
        def _():
            z_make(SWEEPS).wait_send()

    pending.append(z_sent)
    weight = weights[2 * l + yh].astype(f32)
    weight_sum = weights[0]
    for n in range(1, 2 * NL):
        weight_sum = weight_sum + weights[n]
    weight_sum = weight_sum.astype(f32)

    def energy_layer(k, share):
        m = jnp.where(core == 1, k + 1, 3 - k)
        for c in range(NL):
            u, v, w = modes(fin, m, c)
            tr = u["x"] + v["y"] + w["z"]
            sq = lambda t: t * t
            normal = sq(u["x"]) + sq(v["y"]) + sq(w["z"])
            shear = sq(u["y"] + v["x"]) + sq(v["z"] + w["y"]) + sq(u["z"] + w["x"])
            pairs = (
                sq(v["xy"]) + sq(w["zx"]) + sq(u["xy"]) + sq(w["yz"]) + sq(u["zx"]) + sq(v["yz"])
            )
            joint = sq(v["xy"] + w["zx"]) + sq(u["xy"] + w["yz"]) + sq(u["zx"] + v["yz"])
            s = u["yz"] + v["zx"] + w["xy"]
            triple = sq(u["yz"]) + sq(v["zx"]) + sq(w["xy"]) + sq(s)
            quad = sq(u["xyz"]) + sq(v["xyz"]) + sq(w["xyz"])
            total = (
                (RATIO * sq(tr) + 2.0 * normal + shear) + (pairs + 0.5 * joint)
                + (1.0 / 3.0) * triple + ((RATIO + 4.0) / 9.0) * quad
            )
            t = (weight * UNIT) * total
            half, j = k // 2, k % 2
            MS[c, half, j] = t
            if c > 0:
                MS[c - 1, half, 2, pl.ds(2 * j + 1, 1), :] = t[0:1, :]
            if c < NL - 1:
                MS[c + 1, half, 2, pl.ds(2 * j, 1), :] = t[7:8, :]
            share = share + t * G[k, 8 * c : 8 * c + 8, :]
        return share

    def last_layer(k, got):
        @pl.when(k == 3)
        def _():
            ghost(fin)

            @pl.when(core == 1)
            def _():
                far_ghost(SWEEPS)

        return energy_layer(k, got)

    share = lax.fori_loop(0, 4, last_layer, zero8)
    share = jnp.sum(share, axis=0, keepdims=True)
    for c in range(NL):
        for k in range(2):
            MS[c, k, 2, 4:5, :] = share

    me = 2 * l + yh
    m_copies = []
    def m_make(k, cc):
        ll = lax.rem(l + k, NL)
        return remote(MS.at[ll, cc], RX.at[me], s_m.at[k, cc], r_m, dev(ll, z, core, cc))

    for k in far_first(NL):
        for cc in range(2):
            if k > 0:
                m_make(k, cc).start()
            else:
                alone = jnp.logical_and(both, core == cc)

                @pl.when(alone)
                def _():
                    pltpu.make_async_copy(MS.at[l, cc], RX.at[me], r_m).start()

                @pl.when(jnp.logical_not(alone))
                def _():
                    m_make(k, cc).start()

    def m_sent():
        for k in range(NL):
            for cc in range(2):
                if k > 0:
                    m_make(k, cc).wait_send()
                else:
                    @pl.when(jnp.logical_not(jnp.logical_and(both, core == cc)))
                    def _():
                        m_make(k, cc).wait_send()

    pending.append(m_sent)

    arrived(RX, r_m)
    scale = (3.0 * (1.0 - EMIN)) / weight_sum
    def summed(k):
        parts = [RX[n, k] for n in range(2 * NL)]
        while len(parts) > 1:
            parts = [a + b for a, b in zip(parts[::2], parts[1::2])]
        return parts[0]

    rim = summed(2)
    SV[...] = rim[4:5, :]

    def s_make(kz, ky):
        return remote(SV, RX2.at[2 * z + yh], s_s.at[kz, ky], r_s, dev(l, z + kz, (yh + ky) % 2, core))

    for kz in far_first(Z):
        for ky in (1, 0):
            if (kz, ky) != (0, 0):
                s_make(kz, ky).start()
    pltpu.make_async_copy(SV, RX2.at[2 * z + yh], r_s).start()

    def s_sent():
        for kz in range(Z):
            for ky in range(2):
                if (kz, ky) != (0, 0):
                    s_make(kz, ky).wait_send()

    pending.append(s_sent)
    native = 4 * yh + 2 * (1 - core)
    for k in range(2):
        main = summed(k)
        rated = []
        for n in range(3):
            near = pl.ds(pl.multiple_of(8 * l + 8 * n, 8), 8)
            d = D[native + k, near, :]
            row = jnp.clip(8 * l + 8 * (n - 1), 0, rows - 8)
            lab = LAB[native + k, pl.ds(pl.multiple_of(row, 8), 8), :]
            solid = jnp.where(lab == 2, 1.0, d)
            rated.append(d * solid * solid * scale)
        above = jnp.where(l > 0, f32(1.0), f32(0.0)) * rated[0][7:8, :]
        below = jnp.where(l < NL - 1, f32(1.0), f32(0.0)) * rated[2][0:1, :]
        DS[k + 1, 8:16, :] = main * rated[1]
        DS[k + 1, 7:8, :] = rim[2 * k : 2 * k + 1, :] * above
        DS[k + 1, 16:17, :] = rim[2 * k + 1 : 2 * k + 2, :] * below

    def h_make(up):
        to = lax.rem(g + (1 if up else 4 * Z - 1), 4 * Z)
        return remote(DS.at[2 if up else 1], DS.at[0 if up else 3], s_h.at[int(up)], r_h.at[int(up)], (l, to))

    for up in (False, True):
        h_make(up).start()
        pending.append(h_make(up).wait_send)
    arrived(DS.at[3], r_h.at[0])
    arrived(DS.at[0], r_h.at[1])

    planes = []
    for k in range(4):
        planes.append(plane_sums(DS[k, 8:16, :], DS[k, 7:15, :], DS[k, 9:17, :]))
    low = jnp.where(g > 0, f32(1.0), f32(0.0)) * planes[0][1]
    high = jnp.where(g < 4 * Z - 1, f32(1.0), f32(0.0)) * planes[3][1]
    numer = [planes[1][0] + low + planes[2][1], planes[2][0] + planes[1][1] + high]
    @pl.when(both)
    def _():
        for k in range(2):
            VO[k] = V[1 + 2 * core + k, here8, :]

    @pl.when(jnp.logical_not(both))
    def _():
        arrived(VO, r_v)

    arrived(RX2, r_s)
    total = RX2[0]
    for n in range(1, 2 * Z):
        total = total + RX2[n]
    mean = jnp.sum(total, axis=1, keepdims=True) * scale / (8 * Z * rows * 128)
    for k in range(2):
        filtered = numer[k] * VO[k]
        d = D[native + k, here8, :]
        candidate = d * jnp.sqrt(filtered / mean)
        lower = jnp.maximum(d - MOVE_LIMIT, FLOOR_DENSITY)
        upper = jnp.minimum(d + MOVE_LIMIT, 1.0)
        new = jnp.minimum(jnp.maximum(candidate, lower), upper)
        newd[k] = jnp.where(LAB[native + k, mine, :] == 2, 1.0, new)

    for end in pending:
        end()


def solution(mesh):
    NL, Z = mesh.shape["load"], mesh.shape["gz"] // 4
    rows = 8 * NL

    def on_device(density, labels, forces, case_weights):
        vm = lambda *shape: pltpu.VMEM(shape, jnp.float32)
        dma = lambda *shape: pltpu.SemaphoreType.DMA(shape)
        scratch = [
            vm(*density.shape),
            pltpu.VMEM(labels.shape, jnp.int32),
            vm(*forces.shape),
            vm(3, 4, rows, 128),
            pltpu.VMEM((8, rows, 128), jnp.int32),
            vm(8, rows + 16, 128),
            vm(6, rows, 128),
            vm(6, rows + 8, 128),
            vm(6, rows, 128),
            vm(3, 6, rows, 128),
            vm(3, 6, rows, 128),
            vm(3, 6, rows, 128),
            vm(3, 6, rows + 8, 128),
            vm(3, 6, rows + 8, 128),
            vm(3, 6, rows + 8, 128),
            vm(3, 6, rows + 8, 128),
            vm(12, rows, 128),
            vm(6, rows + 8, 128),
            vm(6, rows + 8, 128),
            vm(3, rows, 128),
            vm(3, 4, rows, 128),
            vm(4, 3, rows, 128),
            vm(4, 3, rows, 128),
            vm(8, rows, 128),
            vm(8, rows, 128),
            vm(6, rows + 16, 128),
            vm(2, 8, 128),
            vm(4, rows, 128),
            vm(NL, 2, 3, 8, 128),
            vm(2 * NL, 3, 8, 128),
            vm(4, 24, 128),
            vm(1, 128),
            vm(2 * Z, 1, 128),
            pltpu.SMEM((2 * NL,), jnp.int32),
            vm(46 << 11, 128),
            dma(NL, 2), pltpu.SemaphoreType.DMA,
            pltpu.SemaphoreType.DMA, pltpu.SemaphoreType.DMA,
            dma(2), dma(2),
            dma(2), dma(2),
            dma(2), dma(2),
            pltpu.SemaphoreType.DMA, pltpu.SemaphoreType.DMA,
            pltpu.SemaphoreType.DMA, pltpu.SemaphoreType.DMA,
            pltpu.SemaphoreType.DMA, pltpu.SemaphoreType.DMA,
            dma(2, 2), dma(2, 2),
            dma(4), dma(4),
            dma(2), dma(2),
            dma(NL, 2), pltpu.SemaphoreType.DMA,
            dma(2), dma(2),
            dma(Z, 2), pltpu.SemaphoreType.DMA,
            dma(4),
        ]
        return pl.pallas_call(
            functools.partial(kernel, NL, Z),
            out_shape=(
                pltpu.VMEM(density.shape, jnp.float32),
                pltpu.VMEM(forces.shape, jnp.float32),
            ),
            in_specs=[pl.BlockSpec(memory_space=pltpu.HBM)] * 4,
            out_specs=(pl.BlockSpec(memory_space=pltpu.VMEM), pl.BlockSpec(memory_space=pltpu.VMEM)),
            scratch_shapes=scratch,
            compiler_params=pltpu.CompilerParams(
                collective_id=1, has_side_effects=True, vmem_limit_bytes=60 << 20
            ),
            name="step",
        )(density, labels, forces, case_weights)

    return jax.shard_map(
        on_device,
        mesh=mesh,
        in_specs=(
            P("gz", "load", None),
            P("gz", None, None),
            P("load", None, "gz", None, None),
            P(),
        ),
        out_specs=(P("gz", "load", None), P("load", None, "gz", None, None)),
        check_vma=False,
    )
```
